32 devices in a mesh: lm: 4 (over z), sl: 8 (over y, x, core).
Axes of the slice: x: 2, y: 2, z: 4, core: 2. Of those that a mesh axis runs over, the one named last changes fastest.
Arguments:
- slab: bfloat16 [8192, 1024], P('sl'), may hold values from -6 to 6
- landmarks: bfloat16 [8192, 1024], P(('lm', 'sl')), may hold values from -6 to 6
- codes: bfloat16 [8192, 96], P(('lm', 'sl')), may hold values from -4 to 4
- exponents: int32 [64], P(('lm', 'sl')), may hold values from -3 to 3
- eigvec: bfloat16 [96, 64], replicated, may hold values from -0.625 to 0.625
- ritz: float32 [64], replicated, may hold values from 0.5 to 4
Outputs:
- extended: float32 [8192, 64], P('sl')
The draws below stay inside these ranges and needn't reach their ends.
All inputs are finite; a program needn't handle non-finite values.
Results may differ from the reference program's by a relative error of at most 0.004.
Values may be sent and summed in bfloat16 or wider, within the bound.
No kernel may reach another device: no remote copies, remote signals or barrier semaphores. Data moves between devices by JAX's collectives and lax.ppermute only.
A program may use at most 128 MiB of HBM per device.

```python
import math
import jax
import jax.numpy as jnp
from jax import lax

FEAT = 1024
BASIS = 96
RITZ = 64
BLOCK = 128
LM_DEV = 256
NL = 8192
SLAB = 8192


def with_ends(result, stream_key, smallest, top_value):
    extent = result.shape
    spot = [jax.random.randint(jax.random.fold_in(stream_key, axis), (), 0, extent[axis]) for axis in range(len(extent))]
    result = result.at[tuple(spot)].set(smallest)
    longest = extent.index(max(extent))
    spot[longest] = (spot[longest] + 1) % extent[longest]
    return result.at[tuple(spot)].set(top_value)


def shard_levels(key, dims, split, smallest, high):
    loudness = 1.0
    for axis_at, blocks in split:
        heights = jax.random.uniform(jax.random.fold_in(jax.random.fold_in(key, 6), axis_at), (blocks,), jnp.float32, smallest / len(split), high / len(split))
        loudness = loudness * jnp.repeat(jnp.exp(heights), dims[axis_at] // blocks).reshape((-1,) + (1,) * (len(dims) - 1 - axis_at))
    return loudness


def centred(stream_key, extent, deviation, bound, split=(), dtype=jnp.bfloat16):
    values = jax.random.normal(stream_key, extent, jnp.float32) * deviation
    if len(split) > 0:
        values = shard_levels(stream_key, extent, split, -0.22, 0.18) * values
    return jnp.clip(values, min=-bound, max=bound).astype(dtype)


def setup_inputs(seed: int = 0) -> dict:
    seeds = jax.random.split(jax.random.key(seed), 7)
    slab = centred(seeds[0], (SLAB, FEAT), 1.0, 6.0, ((0, 8),))
    landmarks = centred(seeds[1], (NL, FEAT), 1.0, 6.0, ((0, 32),))
    codes = centred(seeds[2], (NL, BASIS), 1.0, 4.0, ((0, 32),))
    exponents = with_ends(jax.random.randint(seeds[3], (NL // BLOCK,), -3, 4), jax.random.fold_in(seeds[3], 1), -3, 3).astype(jnp.int32)
    eigvec = centred(seeds[4], (BASIS, RITZ), BASIS ** -0.5, 0.625)
    ritz = jnp.clip(jnp.exp(jax.random.uniform(seeds[5], (RITZ,), jnp.float32, math.log(0.5), math.log(4.0))), 0.5, 4.0)
    return {"slab": slab, "landmarks": landmarks, "codes": codes, "exponents": exponents, "eigvec": eigvec, "ritz": ritz}


def reference(slab, landmarks, codes, exponents, eigvec, ritz):
    scale = jnp.exp2(exponents.astype(jnp.float32))
    rows_scale = jnp.repeat(scale, BLOCK)
    basis = (codes.astype(jnp.float32) * rows_scale[:, None]).astype(jnp.bfloat16)
    vectors = jnp.dot(basis, eigvec, preferred_element_type=jnp.float32).astype(jnp.bfloat16)
    factor = 1.0 / (ritz * math.sqrt(NL))
    coeff = 1.0 / math.sqrt(FEAT)
    width = LM_DEV
    count = NL // width
    land_blocks = landmarks.reshape(count, width, FEAT)
    vec_blocks = vectors.reshape(count, width, RITZ)

    def step(total, pieces):
        land_piece, vec_piece = pieces
        scores = jnp.dot(slab, land_piece.T, preferred_element_type=jnp.float32) * coeff
        affinity = jnp.exp(scores).astype(jnp.bfloat16)
        return (total + jnp.dot(affinity, vec_piece, preferred_element_type=jnp.float32), None)
    total, unused = lax.scan(step, jnp.zeros((SLAB, RITZ), jnp.float32), (land_blocks, vec_blocks))
    return total * factor[None, :]
```

```python
import math

import jax
import jax.numpy as jnp
from jax import lax
from jax.sharding import PartitionSpec as P

BLOCK = 128


def affinity_sum(rows, land_piece, vec_piece, coeff):
    scores = jnp.dot(rows, land_piece.T, preferred_element_type=jnp.float32) * coeff
    affinity = jnp.exp(scores).astype(jnp.bfloat16)
    return jnp.dot(affinity, vec_piece, preferred_element_type=jnp.float32)


def local(slab, landmarks, codes, exponents, eigvec, ritz):
    total_land = codes.shape[0] * lax.axis_size("lm") * lax.axis_size("sl")
    coeff = 1.0 / math.sqrt(slab.shape[1])
    factor = 1.0 / (ritz * math.sqrt(total_land))
    scale = jnp.exp2(exponents.astype(jnp.float32))
    rows_scale = jnp.repeat(scale, BLOCK)
    basis = (codes.astype(jnp.float32) * rows_scale[:, None]).astype(jnp.bfloat16)
    vectors = jnp.dot(basis, eigvec, preferred_element_type=jnp.float32).astype(jnp.bfloat16)
    land_all = lax.all_gather(landmarks, "sl", axis=0, tiled=True)
    vec_all = lax.all_gather(vectors, "sl", axis=0, tiled=True)
    terms = affinity_sum(slab, land_all, vec_all, coeff)
    return lax.psum(terms, "lm") * factor[None, :]


def solution(mesh):
    return jax.shard_map(
        local,
        mesh=mesh,
        in_specs=(
            P("sl", None),
            P(("lm", "sl"), None),
            P(("lm", "sl"), None),
            P(("lm", "sl")),
            P(),
            P(),
        ),
        out_specs=P("sl", None),
        check_vma=False,
    )
```

```python
import functools
import math

import jax
import jax.numpy as jnp
from jax import lax
from jax.experimental import pallas as pl
from jax.experimental.pallas import tpu as pltpu
from jax.sharding import PartitionSpec as P

BLOCK = 128
VMEM_LIMIT = 40 * 2**20


def xor_send(value, bit, n):
    return lax.ppermute(value, "sl", [(i, i ^ bit) for i in range(n)])


def gather_slots(piece, n):
    half = piece.shape[0] // 2
    slots = {0: [piece[:half], piece[half:]]}
    bits = [b for b in (1 << k for k in range(1, 31)) if b < n]
    for bit in bits:
        slots[bit] = [None, None]
    for first in (0, 1):
        for k, bit in enumerate(bits):
            part = first if k % 2 == 0 else 1 - first
            slots[bit][part] = xor_send(slots[0][part], bit, n)
    for d in range(2, n, 2):
        if d in slots:
            continue
        own = [b for b in bits if d & b]
        low, high = own[0], own[-1]
        slots[d] = [
            xor_send(slots[d ^ high][0], high, n),
            xor_send(slots[d ^ low][1], low, n),
        ]
    for d in range(0, n, 2):
        slots[d + 1] = [xor_send(part, 1, n) for part in slots[d]]
    return slots


def gather_small(piece, n):
    return {d: (piece if d == 0 else xor_send(piece, d, n)) for d in range(n)}


def vectors_kernel(codes_ref, scale_ref, eig_ref, out_ref):
    basis = (codes_ref[...].astype(jnp.float32) * scale_ref[...]).astype(jnp.bfloat16)
    vectors = jnp.dot(basis, eig_ref[...], preferred_element_type=jnp.float32)
    half = vectors.shape[0] // 2
    out_ref[...] = jnp.concatenate([vectors[:half], vectors[half:]], axis=1).astype(jnp.bfloat16)


def pack_vectors(codes, rows_scale, eigvec):
    rows, ritz = codes.shape[0], eigvec.shape[1]
    return pl.pallas_call(
        vectors_kernel,
        out_shape=jax.ShapeDtypeStruct((rows // 2, 2 * ritz), jnp.bfloat16),
    )(codes, rows_scale[:, None], eigvec)


def stage_kernel(blocks, coeff, has_acc, parts_out, *refs):
    slab_ref = refs[0]
    lands = refs[1 : 1 + 2 * blocks]
    vecs = refs[1 + 2 * blocks : 1 + 3 * blocks]
    rest = refs[1 + 3 * blocks :]
    acc = None
    if has_acc:
        acc, rest = rest[0][...], rest[1:]
    for b in range(blocks):
        land = jnp.concatenate([lands[2 * b][...], lands[2 * b + 1][...]], axis=0)
        packed = vecs[b][...]
        ritz = packed.shape[1] // 2
        vec = jnp.concatenate([packed[:, :ritz], packed[:, ritz:]], axis=0)
        scores = lax.dot_general(
            slab_ref[...], land, (((1,), (1,)), ((), ())), preferred_element_type=jnp.float32
        )
        affinity = jnp.exp(scores * coeff).astype(jnp.bfloat16)
        term = jnp.dot(affinity, vec, preferred_element_type=jnp.float32)
        acc = term if acc is None else acc + term
    if not parts_out:
        rest[0][...] = acc
        return
    scratch = rest[-1]
    scratch[...] = acc
    me = lax.axis_index("lm")
    rows = acc.shape[0] // parts_out
    for d in range(parts_out):
        start = pl.multiple_of(lax.rem(me + d, parts_out) * rows, rows)
        lo = scratch[pl.ds(start, rows // 2), :]
        hi = scratch[pl.ds(start + rows // 2, rows // 2), :]
        rest[d][...] = jnp.concatenate([lo, hi], axis=1)


def stage(slab, lands, vecs, acc, coeff, parts_out):
    rows, feat = slab.shape
    ritz = vecs[0].shape[1] // 2
    blocks = len(vecs)
    if parts_out:
        part = jax.ShapeDtypeStruct((rows // parts_out // 2, 2 * ritz), jnp.float32)
        out_shape = [part] * parts_out
        scratch = [pltpu.VMEM((rows, ritz), jnp.float32)]
    else:
        out_shape = jax.ShapeDtypeStruct((rows, ritz), jnp.float32)
        scratch = []
    land_rows = 2 * blocks * lands[0].shape[0]
    args = [slab, *lands, *vecs] + ([] if acc is None else [acc])
    return pl.pallas_call(
        functools.partial(stage_kernel, blocks, coeff, acc is not None, parts_out),
        out_shape=out_shape,
        scratch_shapes=scratch,
        compiler_params=pltpu.CompilerParams(vmem_limit_bytes=VMEM_LIMIT),
        cost_estimate=pl.CostEstimate(
            flops=2 * rows * land_rows * (feat + 4 * ritz),
            bytes_accessed=2 * (rows + land_rows) * feat,
            transcendentals=rows * land_rows,
        ),
    )(*args)


def sum_kernel(parts, *refs):
    total = refs[0][...]
    for part in refs[1:parts]:
        total = total + part[...]
    refs[parts][...] = total


def finish_kernel(n, factor_ref, *refs):
    me = lax.axis_index("lm")
    out_ref = refs[n]
    rows = out_ref.shape[0] // n
    ritz = out_ref.shape[1]
    factor = factor_ref[...]
    for d in range(n):
        start = pl.multiple_of(lax.rem(me + n - d, n) * rows, rows)
        packed = refs[d][...].astype(jnp.float32)
        out_ref[pl.ds(start, rows // 2), :] = packed[:, :ritz] * factor
        out_ref[pl.ds(start + rows // 2, rows // 2), :] = packed[:, ritz:] * factor


def lm_send(value, d, n):
    return lax.ppermute(value, "lm", [(i, (i + d) % n) for i in range(n)])


def local(slab, landmarks, codes, exponents, eigvec, ritz):
    n_lm, n_sl = lax.axis_size("lm"), lax.axis_size("sl")
    total_land = codes.shape[0] * n_lm * n_sl
    coeff = 1.0 / math.sqrt(slab.shape[1])
    factor = 1.0 / (ritz * math.sqrt(total_land))
    rows_scale = jnp.repeat(jnp.exp2(exponents.astype(jnp.float32)), BLOCK)
    packed = pack_vectors(codes, rows_scale, eigvec)
    lands = gather_slots(landmarks, n_sl)
    vecs = gather_small(packed, n_sl)
    acc = None
    for d in range(0, n_sl, 2):
        last = d + 2 == n_sl
        acc = stage(
            slab, lands[d] + lands[d + 1], [vecs[d], vecs[d + 1]], acc, coeff, n_lm if last else 0
        )
    received = [acc[0]] + [lm_send(acc[d], d, n_lm) for d in range(1, n_lm)]
    mine = pl.pallas_call(
        functools.partial(sum_kernel, n_lm),
        out_shape=jax.ShapeDtypeStruct(received[0].shape, jnp.float32),
    )(*received)
    pieces = [mine] + [lm_send(mine, d, n_lm) for d in range(1, n_lm)]
    return pl.pallas_call(
        functools.partial(finish_kernel, n_lm),
        out_shape=jax.ShapeDtypeStruct((slab.shape[0], ritz.shape[0]), jnp.float32),
    )(factor[None, :], *pieces)


def solution(mesh):
    return jax.shard_map(
        local,
        mesh=mesh,
        in_specs=(
            P("sl", None),
            P(("lm", "sl"), None),
            P(("lm", "sl"), None),
            P(("lm", "sl")),
            P(),
            P(),
        ),
        out_specs=P("sl", None),
        check_vma=False,
    )
```

```python
import functools
import math

import jax
import jax.numpy as jnp
from jax import lax
from jax.experimental import pallas as pl
from jax.experimental.pallas import tpu as pltpu
from jax.sharding import PartitionSpec as P

BLOCK = 128
MIB = 2**20


def xor_send(value, bit, n):
    return lax.ppermute(value, "sl", [(i, i ^ bit) for i in range(n)])


def prepare_kernel(land_ref, codes_ref, exponents_ref, eig_ref, first_ref, second_ref):
    half = land_ref.shape[0] // 2
    rows, feat = land_ref.shape
    ritz = eig_ref.shape[0]
    pieces = []
    for b in range(rows // BLOCK):
        scale = lax.shift_left(jnp.int32(1), exponents_ref[b] + 15).astype(jnp.float32) * 2.0**-15
        pieces.append(codes_ref[:, b * BLOCK : (b + 1) * BLOCK].astype(jnp.float32) * scale)
    basis = jnp.concatenate(pieces, axis=1).astype(jnp.bfloat16)
    vectors = jnp.dot(eig_ref[...], basis, preferred_element_type=jnp.float32).astype(jnp.bfloat16)
    first_ref[:half, :] = land_ref[:half, :]
    second_ref[...] = land_ref[half:, :]
    chunks = feat // rows
    depth = ritz // chunks
    for c in range(chunks):
        first_ref[half:, c * rows : (c + 1) * rows] = vectors[c * depth : (c + 1) * depth, :]


def prepare(landmarks, codes_t, exponents, eig_t):
    rows, feat = landmarks.shape
    extra = eig_t.shape[0] * rows // feat
    vmem = pl.BlockSpec(memory_space=pltpu.VMEM)
    return pl.pallas_call(
        prepare_kernel,
        out_shape=[
            jax.ShapeDtypeStruct((rows // 2 + extra, feat), jnp.bfloat16),
            jax.ShapeDtypeStruct((rows // 2, feat), jnp.bfloat16),
        ],
        in_specs=[vmem, vmem, pl.BlockSpec(memory_space=pltpu.SMEM), vmem],
        compiler_params=pltpu.CompilerParams(vmem_limit_bytes=8 * MIB),
    )(landmarks, codes_t, exponents, eig_t)


def block_term(slab_ref, first_ref, second_ref, coeff):
    half, feat = second_ref.shape
    rows = 2 * half
    chunks = feat // rows
    land = jnp.concatenate([first_ref[:half, :], second_ref[...]], axis=0)
    vec = jnp.concatenate(
        [first_ref[half:, c * rows : (c + 1) * rows] for c in range(chunks)], axis=0
    )
    dims = (((1,), (1,)), ((), ()))
    scores = lax.dot_general(slab_ref[...], land, dims, preferred_element_type=jnp.float32)
    affinity = jnp.exp(scores * coeff).astype(jnp.bfloat16)
    return lax.dot_general(affinity, vec, dims, preferred_element_type=jnp.float32)


def stage_kernel(count, coeff, has_acc, last, *refs):
    slabs = refs[:count]
    first_ref, second_ref = refs[count : count + 2]
    accs = refs[count + 2 : 2 * count + 2] if has_acc else [None] * count
    outs = refs[-count:]
    for slab_ref, acc_ref, out_ref in zip(slabs, accs, outs):
        term = block_term(slab_ref, first_ref, second_ref, coeff)
        if acc_ref is not None:
            term = acc_ref[...] + term
        out_ref[...] = term.T if last else term


def stage(slabs, first, second, accs, coeff, ritz, last=False):
    rows, feat = slabs[0].shape
    land = 2 * second.shape[0]
    count = len(slabs)
    shape = (ritz, rows) if last else (rows, ritz)
    return pl.pallas_call(
        functools.partial(stage_kernel, count, coeff, accs is not None, last),
        out_shape=[jax.ShapeDtypeStruct(shape, jnp.float32)] * count,
        compiler_params=pltpu.CompilerParams(vmem_limit_bytes=32 * MIB),
        cost_estimate=pl.CostEstimate(
            flops=2 * count * rows * land * (feat + 4 * ritz),
            bytes_accessed=2 * (count * rows + land) * feat,
            transcendentals=count * rows * land,
        ),
    )(*slabs, first, second, *(accs or []))


def split_kernel(a_ref, b_ref, out_ref):
    n, _, width = out_ref.shape
    for q in range(n):
        part = slice(q * width, (q + 1) * width)
        out_ref[q] = a_ref[:, part] + b_ref[:, part]


def sum_kernel(parts_ref, ritz_ref, out_ref, *, total_land):
    n = parts_ref.shape[0]
    total = parts_ref[0]
    for q in range(1, n):
        total = total + parts_ref[q]
    factor = 1.0 / (ritz_ref[...] * math.sqrt(total_land))
    result = (total * factor).astype(out_ref.dtype)
    for q in range(n):
        out_ref[q] = result


def join_kernel(parts_ref, out_ref):
    n, _, width = parts_ref.shape
    for q in range(n):
        out_ref[:, q * width : (q + 1) * width] = parts_ref[q].astype(out_ref.dtype)


def small_call(kernel, shape, dtype, *args):
    return pl.pallas_call(
        kernel,
        out_shape=jax.ShapeDtypeStruct(shape, dtype),
        compiler_params=pltpu.CompilerParams(vmem_limit_bytes=8 * MIB),
    )(*args)


def local(slab, landmarks, codes, exponents, eigvec, ritz):
    n_lm, n_sl = lax.axis_size("lm"), lax.axis_size("sl")
    total_land = codes.shape[0] * n_lm * n_sl
    coeff = 1.0 / math.sqrt(slab.shape[1])
    cols = ritz.shape[0]
    rows = slab.shape[0]
    bits = [1 << k for k in range(1, n_sl.bit_length() - 1)]

    other = xor_send(slab, 1, n_sl)
    first, second = prepare(landmarks, codes.T, exponents, eigvec.T)
    firsts, seconds = {0: first}, {0: second}
    for k, bit in enumerate(bits):
        if k % 2 == 0:
            firsts[bit] = xor_send(first, bit, n_sl)
        else:
            seconds[bit] = xor_send(second, bit, n_sl)
    for k, bit in enumerate(bits):
        if k % 2 == 0:
            seconds[bit] = xor_send(second, bit, n_sl)
        else:
            firsts[bit] = xor_send(first, bit, n_sl)
    for d in range(2, n_sl, 2):
        if d in firsts:
            continue
        own = [b for b in bits if d & b]
        low, high = own[0], own[-1]
        firsts[d] = xor_send(firsts[d ^ high], high, n_sl)
        seconds[d] = xor_send(seconds[d ^ low], low, n_sl)

    accs = None
    for d in range(0, n_sl - 2, 2):
        accs = stage([slab, other], firsts[d], seconds[d], accs, coeff, cols)
    d = n_sl - 2
    (theirs,) = stage([other], firsts[d], seconds[d], accs[1:], coeff, cols, last=True)
    received = xor_send(theirs, 1, n_sl)
    (mine,) = stage([slab], firsts[d], seconds[d], accs[:1], coeff, cols, last=True)

    part = (n_lm, cols, rows // n_lm)
    parts = small_call(split_kernel, part, jnp.float32, mine, received)
    parts = lax.all_to_all(parts, "lm", 0, 0)
    done = small_call(
        functools.partial(sum_kernel, total_land=total_land), part, jnp.bfloat16, parts, ritz[:, None]
    )
    done = lax.all_to_all(done, "lm", 0, 0)
    return small_call(join_kernel, (cols, rows), jnp.float32, done).T


def solution(mesh):
    return jax.shard_map(
        local,
        mesh=mesh,
        in_specs=(
            P("sl", None),
            P(("lm", "sl"), None),
            P(("lm", "sl"), None),
            P(("lm", "sl")),
            P(),
            P(),
        ),
        out_specs=P("sl", None),
        check_vma=False,
    )
```

```python
import functools
import math

import jax
import jax.numpy as jnp
from jax import lax
from jax.experimental import pallas as pl
from jax.experimental.pallas import tpu as pltpu
from jax.sharding import PartitionSpec as P

BLOCK = 128
MIB = 2**20


def xor_send(value, bit, n):
    return lax.ppermute(value, "sl", [(i, i ^ bit) for i in range(n)])


def lm_send(value, bit, n):
    return lax.ppermute(value, "lm", [(i, i ^ bit) for i in range(n)])


def prepare_kernel(
    land_ref, codes_ref, exponents_ref, eig_ref, first_ref, second_ref, codes, eig, exponents, extra, sems
):
    rows, feat = land_ref.shape
    half = rows // 2
    ritz = eig_ref.shape[0]
    pairs = [
        (codes_ref, codes),
        (eig_ref, eig),
        (exponents_ref, exponents),
        (land_ref.at[:half], first_ref.at[:half]),
        (land_ref.at[half:], second_ref),
        (extra, first_ref.at[half:]),
    ]
    copies = [pltpu.make_async_copy(src, dst, sems.at[k]) for k, (src, dst) in enumerate(pairs)]
    for copy in copies[:-1]:
        copy.start()
    for copy in copies[:3]:
        copy.wait()
    pieces = []
    for b in range(rows // BLOCK):
        scale = lax.shift_left(jnp.int32(1), exponents[b] + 15).astype(jnp.float32) * 2.0**-15
        pieces.append(codes[:, b * BLOCK : (b + 1) * BLOCK].astype(jnp.float32) * scale)
    basis = jnp.concatenate(pieces, axis=1).astype(jnp.bfloat16)
    vectors = jnp.dot(eig[...], basis, preferred_element_type=jnp.float32).astype(jnp.bfloat16)
    chunks = feat // rows
    depth = ritz // chunks
    for c in range(chunks):
        extra[:, c * rows : (c + 1) * rows] = vectors[c * depth : (c + 1) * depth, :]
    copies[-1].start()
    for copy in copies[3:]:
        copy.wait()


def prepare(landmarks, codes_t, exponents, eig_t):
    rows, feat = landmarks.shape
    extra = eig_t.shape[0] * rows // feat
    hbm = pl.BlockSpec(memory_space=pltpu.HBM)
    return pl.pallas_call(
        prepare_kernel,
        out_shape=[
            jax.ShapeDtypeStruct((rows // 2 + extra, feat), jnp.bfloat16),
            jax.ShapeDtypeStruct((rows // 2, feat), jnp.bfloat16),
        ],
        in_specs=[hbm] * 4,
        out_specs=[hbm] * 2,
        scratch_shapes=[
            pltpu.VMEM(codes_t.shape, codes_t.dtype),
            pltpu.VMEM(eig_t.shape, eig_t.dtype),
            pltpu.SMEM(exponents.shape, exponents.dtype),
            pltpu.VMEM((extra, feat), jnp.bfloat16),
            pltpu.SemaphoreType.DMA((6,)),
        ],
        compiler_params=pltpu.CompilerParams(vmem_limit_bytes=60 * MIB),
    )(landmarks, codes_t, exponents, eig_t)


def block_term(slab_ref, first_ref, second_ref, coeff):
    half, feat = second_ref.shape
    rows = 2 * half
    chunks = feat // rows
    land = jnp.concatenate([first_ref[:half, :], second_ref[...]], axis=0)
    vec = jnp.concatenate(
        [first_ref[half:, c * rows : (c + 1) * rows] for c in range(chunks)], axis=0
    )
    dims = (((1,), (1,)), ((), ()))
    scores = lax.dot_general(slab_ref[...], land, dims, preferred_element_type=jnp.float32)
    affinity = jnp.exp(scores * coeff).astype(jnp.bfloat16)
    return lax.dot_general(affinity, vec, dims, preferred_element_type=jnp.float32)


def stage_kernel(count, coeff, has_acc, last, *refs):
    slabs = refs[:count]
    first_ref, second_ref = refs[count : count + 2]
    accs = refs[count + 2 : 2 * count + 2] if has_acc else [None] * count
    outs = refs[-count:]
    for slab_ref, acc_ref, out_ref in zip(slabs, accs, outs):
        term = block_term(slab_ref, first_ref, second_ref, coeff)
        if acc_ref is not None:
            term = acc_ref[...] + term
        out_ref[...] = term.T if last else term


def stage(slabs, first, second, accs, coeff, ritz, last=False):
    rows, feat = slabs[0].shape
    land = 2 * second.shape[0]
    count = len(slabs)
    shape = (ritz, rows) if last else (rows, ritz)
    return pl.pallas_call(
        functools.partial(stage_kernel, count, coeff, accs is not None, last),
        out_shape=[jax.ShapeDtypeStruct(shape, jnp.float32)] * count,
        compiler_params=pltpu.CompilerParams(vmem_limit_bytes=32 * MIB),
        cost_estimate=pl.CostEstimate(
            flops=2 * count * rows * land * (feat + 4 * ritz),
            bytes_accessed=2 * (count * rows + land) * feat,
            transcendentals=count * rows * land,
        ),
    )(*slabs, first, second, *(accs or []))


def split_kernel(a_ref, b_ref, keep_ref, send_ref):
    half = keep_ref.shape[1]
    side = lax.rem(lax.axis_index("lm"), 2)
    for out_ref, place in ((keep_ref, side), (send_ref, 1 - side)):
        part = pl.ds(pl.multiple_of(place * half, half), half)
        out_ref[...] = a_ref[:, part] + b_ref[:, part]


def add_kernel(a_ref, b_ref, out_ref):
    out_ref[...] = a_ref[...] + b_ref[...]


def scale_kernel(a_ref, b_ref, ritz_ref, out_ref, *, total_land):
    factor = 1.0 / (ritz_ref[...] * math.sqrt(total_land))
    out_ref[...] = ((a_ref[...] + b_ref[...]) * factor).astype(out_ref.dtype)


def join_kernel(mine_ref, other_ref, out_ref):
    half = mine_ref.shape[1]
    side = lax.rem(lax.axis_index("lm"), 2)
    for ref, place in ((mine_ref, side), (other_ref, 1 - side)):
        part = pl.ds(pl.multiple_of(place * half, half), half)
        out_ref[:, part] = ref[...].astype(out_ref.dtype)


def small_call(kernel, shapes, dtype, *args):
    out = jax.tree.map(
        lambda shape: jax.ShapeDtypeStruct(shape, dtype), shapes, is_leaf=lambda x: isinstance(x, tuple)
    )
    return pl.pallas_call(
        kernel,
        out_shape=out,
        compiler_params=pltpu.CompilerParams(vmem_limit_bytes=8 * MIB),
    )(*args)


def local(slab, landmarks, codes, exponents, eigvec, ritz):
    n_lm, n_sl = lax.axis_size("lm"), lax.axis_size("sl")
    total_land = codes.shape[0] * n_lm * n_sl
    coeff = 1.0 / math.sqrt(slab.shape[1])
    cols = ritz.shape[0]
    rows = slab.shape[0]
    bits = [1 << k for k in range(1, n_sl.bit_length() - 1)]

    other = xor_send(slab, 1, n_sl)
    first, second = prepare(landmarks, codes.T, exponents, eigvec.T)
    firsts, seconds = {0: first}, {0: second}
    for k, bit in enumerate(bits):
        if k % 2 == 0:
            firsts[bit] = xor_send(first, bit, n_sl)
        else:
            seconds[bit] = xor_send(second, bit, n_sl)
    for k, bit in enumerate(bits):
        if k % 2 == 0:
            seconds[bit] = xor_send(second, bit, n_sl)
        else:
            firsts[bit] = xor_send(first, bit, n_sl)
    accs = stage([slab, other], first, second, None, coeff, cols)
    early = [firsts if k % 2 == 0 else seconds for k in range(len(bits))]
    held = [part[bit] for part, bit in zip(early, bits)]
    held, accs = lax.optimization_barrier((held, accs))
    for part, bit, value in zip(early, bits, held):
        part[bit] = value
    for d in range(2, n_sl, 2):
        if d in firsts:
            continue
        own = [b for b in bits if d & b]
        low, high = own[0], own[-1]
        firsts[d] = xor_send(firsts[d ^ high], high, n_sl)
        seconds[d] = xor_send(seconds[d ^ low], low, n_sl)

    for d in range(2, n_sl - 2, 2):
        accs = stage([slab, other], firsts[d], seconds[d], accs, coeff, cols)
    d = n_sl - 2
    (theirs,) = stage([other], firsts[d], seconds[d], accs[1:], coeff, cols, last=True)
    received = xor_send(theirs, 1, n_sl)
    (mine,) = stage([slab], firsts[d], seconds[d], accs[:1], coeff, cols, last=True)

    half = (cols, rows // 2)
    keep, send = small_call(split_kernel, [half, half], jnp.float32, mine, received)
    received = lm_send(send, 1, n_lm)
    for bit in [1 << k for k in range(1, n_lm.bit_length() - 1)]:
        keep = small_call(add_kernel, half, jnp.float32, keep, received)
        received = lm_send(keep, bit, n_lm)
    scale = functools.partial(scale_kernel, total_land=total_land)
    done = small_call(scale, half, jnp.bfloat16, keep, received, ritz[:, None])
    other_done = lm_send(done, 1, n_lm)
    return small_call(join_kernel, (cols, rows), jnp.float32, done, other_done).T


def solution(mesh):
    return jax.shard_map(
        local,
        mesh=mesh,
        in_specs=(
            P("sl", None),
            P(("lm", "sl"), None),
            P(("lm", "sl"), None),
            P(("lm", "sl")),
            P(),
            P(),
        ),
        out_specs=P("sl", None),
        check_vma=False,
    )
```

```python
import functools
import math

import jax
import jax.numpy as jnp
from jax import lax
from jax.experimental import pallas as pl
from jax.experimental.pallas import tpu as pltpu
from jax.sharding import PartitionSpec as P

BLOCK = 128
MIB = 2**20


def xor_send(value, bit, n):
    return lax.ppermute(value, "sl", [(i, i ^ bit) for i in range(n)])


def lm_send(value, step, n):
    return lax.ppermute(value, "lm", [(i, (i + step) % n) for i in range(n)])


def prepare_kernel(
    land_ref, codes_ref, exponents_ref, eig_ref, first_ref, second_ref, codes, eig, exponents, sems
):
    rows, feat = land_ref.shape
    half = rows // 2
    ritz = eig_ref.shape[0]
    pairs = [
        (codes_ref, codes),
        (eig_ref, eig),
        (exponents_ref, exponents),
        (land_ref.at[:half], first_ref.at[:half]),
        (land_ref.at[half:], second_ref),
    ]
    copies = [pltpu.make_async_copy(src, dst, sems.at[k]) for k, (src, dst) in enumerate(pairs)]
    for copy in copies:
        copy.start()
    for copy in copies[:3]:
        copy.wait()
    pieces = []
    for b in range(rows // BLOCK):
        scale = lax.shift_left(jnp.int32(1), exponents[b] + 15).astype(jnp.float32) * 2.0**-15
        pieces.append(codes[:, b * BLOCK : (b + 1) * BLOCK].astype(jnp.float32) * scale)
    basis = jnp.concatenate(pieces, axis=1).astype(jnp.bfloat16)
    vectors = jnp.dot(eig[...], basis, preferred_element_type=jnp.float32).astype(jnp.bfloat16)
    chunks = feat // rows
    depth = ritz // chunks
    for c in range(chunks):
        first_ref[half:, c * rows : (c + 1) * rows] = vectors[c * depth : (c + 1) * depth, :]
    for copy in copies[3:]:
        copy.wait()


def prepare(landmarks, codes_t, exponents, eig_t):
    rows, feat = landmarks.shape
    extra = eig_t.shape[0] * rows // feat
    return pl.pallas_call(
        prepare_kernel,
        out_shape=[
            jax.ShapeDtypeStruct((rows // 2 + extra, feat), jnp.bfloat16),
            jax.ShapeDtypeStruct((rows // 2, feat), jnp.bfloat16),
        ],
        in_specs=[pl.BlockSpec(memory_space=pltpu.HBM)] * 4,
        scratch_shapes=[
            pltpu.VMEM(codes_t.shape, codes_t.dtype),
            pltpu.VMEM(eig_t.shape, eig_t.dtype),
            pltpu.SMEM(exponents.shape, exponents.dtype),
            pltpu.SemaphoreType.DMA((5,)),
        ],
        compiler_params=pltpu.CompilerParams(vmem_limit_bytes=8 * MIB),
    )(*(pltpu.with_memory_space_constraint(x, pltpu.HBM) for x in (landmarks, codes_t, exponents, eig_t)))


def block_term(slab_ref, first_ref, second_ref, coeff):
    half, feat = second_ref.shape
    rows = 2 * half
    chunks = feat // rows
    land = jnp.concatenate([first_ref[:half, :], second_ref[...]], axis=0)
    vec = jnp.concatenate(
        [first_ref[half:, c * rows : (c + 1) * rows] for c in range(chunks)], axis=0
    )
    dims = (((1,), (1,)), ((), ()))
    scores = lax.dot_general(slab_ref[...], land, dims, preferred_element_type=jnp.float32)
    affinity = jnp.exp(scores * coeff).astype(jnp.bfloat16)
    return lax.dot_general(affinity, vec, dims, preferred_element_type=jnp.float32)


def stage_kernel(count, coeff, has_acc, last, *refs):
    slabs = refs[:count]
    first_ref, second_ref = refs[count : count + 2]
    accs = refs[count + 2 : 2 * count + 2] if has_acc else [None] * count
    outs = refs[-count:]
    for slab_ref, acc_ref, out_ref in zip(slabs, accs, outs):
        term = block_term(slab_ref, first_ref, second_ref, coeff)
        if acc_ref is not None:
            term = acc_ref[...] + term
        out_ref[...] = term.T if last else term


def stage(slabs, first, second, accs, coeff, ritz, last=False):
    rows, feat = slabs[0].shape
    land = 2 * second.shape[0]
    count = len(slabs)
    shape = (ritz, rows) if last else (rows, ritz)
    return pl.pallas_call(
        functools.partial(stage_kernel, count, coeff, accs is not None, last),
        out_shape=[jax.ShapeDtypeStruct(shape, jnp.float32)] * count,
        compiler_params=pltpu.CompilerParams(vmem_limit_bytes=32 * MIB),
        cost_estimate=pl.CostEstimate(
            flops=2 * count * rows * land * (feat + 4 * ritz),
            bytes_accessed=2 * (count * rows + land) * feat,
            transcendentals=count * rows * land,
        ),
    )(*slabs, first, second, *(accs or []))


def split_kernel(a_ref, b_ref, *outs):
    n = len(outs)
    width = outs[0].shape[1]
    me = lax.axis_index("lm")
    for d, out_ref in enumerate(outs):
        part = pl.ds(pl.multiple_of(lax.rem(me + d, n) * width, width), width)
        out_ref[...] = a_ref[:, part] + b_ref[:, part]


def sum_kernel(*refs, total_land):
    parts, ritz_ref, out_ref = refs[:-2], refs[-2], refs[-1]
    total = parts[0][...]
    for part in parts[1:]:
        total = total + part[...]
    factor = 1.0 / (ritz_ref[...] * math.sqrt(total_land))
    out_ref[...] = (total * factor).astype(out_ref.dtype)


def join_kernel(*refs):
    parts, out_ref = refs[:-1], refs[-1]
    n = len(parts)
    width = parts[0].shape[1]
    me = lax.axis_index("lm")
    for d, ref in enumerate(parts):
        part = pl.ds(pl.multiple_of(lax.rem(me + n - d, n) * width, width), width)
        out_ref[:, part] = ref[...].astype(out_ref.dtype)


def small_call(kernel, shapes, dtype, *args):
    out = jax.tree.map(
        lambda shape: jax.ShapeDtypeStruct(shape, dtype), shapes, is_leaf=lambda x: isinstance(x, tuple)
    )
    return pl.pallas_call(
        kernel,
        out_shape=out,
        compiler_params=pltpu.CompilerParams(vmem_limit_bytes=8 * MIB),
    )(*args)


def local(slab, landmarks, codes, exponents, eigvec, ritz):
    n_lm, n_sl = lax.axis_size("lm"), lax.axis_size("sl")
    total_land = codes.shape[0] * n_lm * n_sl
    coeff = 1.0 / math.sqrt(slab.shape[1])
    cols = ritz.shape[0]
    rows = slab.shape[0]
    bits = [1 << k for k in range(1, n_sl.bit_length() - 1)]

    other = xor_send(slab, 1, n_sl)
    first, second = prepare(landmarks, codes.T, exponents, eigvec.T)
    firsts, seconds = {0: first}, {0: second}
    for k, bit in enumerate(bits):
        if k % 2 == 0:
            firsts[bit] = xor_send(first, bit, n_sl)
        else:
            seconds[bit] = xor_send(second, bit, n_sl)
    for k, bit in enumerate(bits):
        if k % 2 == 0:
            seconds[bit] = xor_send(second, bit, n_sl)
        else:
            firsts[bit] = xor_send(first, bit, n_sl)
    accs = stage([slab, other], first, second, None, coeff, cols)
    early = [firsts if k % 2 == 0 else seconds for k in range(len(bits))]
    held = [part[bit] for part, bit in zip(early, bits)]
    held, accs = lax.optimization_barrier((held, accs))
    for part, bit, value in zip(early, bits, held):
        part[bit] = value
    for d in range(2, n_sl, 2):
        if d in firsts:
            continue
        own = [b for b in bits if d & b]
        low, high = own[0], own[-1]
        firsts[d] = xor_send(firsts[d ^ high], high, n_sl)
        seconds[d] = xor_send(seconds[d ^ low], low, n_sl)

    for d in range(2, n_sl - 2, 2):
        accs = stage([slab, other], firsts[d], seconds[d], accs, coeff, cols)
    d = n_sl - 2
    (theirs,) = stage([other], firsts[d], seconds[d], accs[1:], coeff, cols, last=True)
    received = xor_send(theirs, 1, n_sl)
    (mine,) = stage([slab], firsts[d], seconds[d], accs[:1], coeff, cols, last=True)

    part = (cols, rows // n_lm)
    parts = small_call(split_kernel, [part] * n_lm, jnp.float32, mine, received)
    parts = [lm_send(value, d, n_lm) if d else value for d, value in enumerate(parts)]
    total = functools.partial(sum_kernel, total_land=total_land)
    done = small_call(total, part, jnp.bfloat16, *parts, ritz[:, None])
    pieces = [lm_send(done, d, n_lm) if d else done for d in range(n_lm)]
    return small_call(join_kernel, (cols, rows), jnp.float32, *pieces).T


def solution(mesh):
    return jax.shard_map(
        local,
        mesh=mesh,
        in_specs=(
            P("sl", None),
            P(("lm", "sl"), None),
            P(("lm", "sl"), None),
            P(("lm", "sl")),
            P(),
            P(),
        ),
        out_specs=P("sl", None),
        check_vma=False,
    )
```

```python
import functools
import math

import jax
import jax.numpy as jnp
from jax import lax
from jax.experimental import pallas as pl
from jax.experimental.pallas import tpu as pltpu
from jax.sharding import PartitionSpec as P

BLOCK = 128
CHUNK = 256
MIB = 2**20


def xor_send(value, bit, n):
    return lax.ppermute(value, "sl", [(i, i ^ bit) for i in range(n)])


def lm_send(value, step, n):
    return lax.ppermute(value, "lm", [(i, (i + step) % n) for i in range(n)])


def prepare_kernel(
    land_ref, codes_ref, exponents_ref, eig_ref, first_ref, second_ref, codes, eig, exponents, sems
):
    rows, feat = land_ref.shape
    half = rows // 2
    ritz = eig_ref.shape[0]
    pairs = [
        (codes_ref, codes),
        (eig_ref, eig),
        (exponents_ref, exponents),
        (land_ref.at[:half], first_ref.at[:half]),
        (land_ref.at[half:], second_ref),
    ]
    copies = [pltpu.make_async_copy(src, dst, sems.at[k]) for k, (src, dst) in enumerate(pairs)]
    for copy in copies:
        copy.start()
    for copy in copies[:3]:
        copy.wait()
    pieces = []
    for b in range(rows // BLOCK):
        scale = lax.shift_left(jnp.int32(1), exponents[b] + 15).astype(jnp.float32) * 2.0**-15
        pieces.append(codes[:, b * BLOCK : (b + 1) * BLOCK].astype(jnp.float32) * scale)
    basis = jnp.concatenate(pieces, axis=1).astype(jnp.bfloat16)
    vectors = jnp.dot(eig[...], basis, preferred_element_type=jnp.float32).astype(jnp.bfloat16)
    chunks = feat // rows
    depth = ritz // chunks
    for c in range(chunks):
        first_ref[half:, c * rows : (c + 1) * rows] = vectors[c * depth : (c + 1) * depth, :]
    for copy in copies[3:]:
        copy.wait()


def prepare(landmarks, codes_t, exponents, eig_t):
    rows, feat = landmarks.shape
    extra = eig_t.shape[0] * rows // feat
    return pl.pallas_call(
        prepare_kernel,
        out_shape=[
            jax.ShapeDtypeStruct((rows // 2 + extra, feat), jnp.bfloat16),
            jax.ShapeDtypeStruct((rows // 2, feat), jnp.bfloat16),
        ],
        in_specs=[pl.BlockSpec(memory_space=pltpu.HBM)] * 4,
        scratch_shapes=[
            pltpu.VMEM(codes_t.shape, codes_t.dtype),
            pltpu.VMEM(eig_t.shape, eig_t.dtype),
            pltpu.SMEM(exponents.shape, exponents.dtype),
            pltpu.SemaphoreType.DMA((5,)),
        ],
        compiler_params=pltpu.CompilerParams(vmem_limit_bytes=8 * MIB),
    )(*(pltpu.with_memory_space_constraint(x, pltpu.HBM) for x in (landmarks, codes_t, exponents, eig_t)))


def block_term(slab_ref, first_ref, second_ref, coeff):
    half, feat = second_ref.shape
    rows = 2 * half
    chunks = feat // rows
    land = jnp.concatenate([first_ref[:half, :], second_ref[...]], axis=0)
    vec = jnp.concatenate(
        [first_ref[half:, c * rows : (c + 1) * rows] for c in range(chunks)], axis=0
    )
    dims = (((1,), (1,)), ((), ()))

    def scores(k):
        piece = slab_ref[k * CHUNK : (k + 1) * CHUNK, :]
        return lax.dot_general(piece, land, dims, preferred_element_type=jnp.float32)

    count = slab_ref.shape[0] // CHUNK
    terms = []
    ahead = scores(0)
    for k in range(count):
        now, ahead = ahead, scores(k + 1) if k + 1 < count else None
        affinity = jnp.exp(now * coeff).astype(jnp.bfloat16)
        terms.append(lax.dot_general(affinity, vec, dims, preferred_element_type=jnp.float32))
    return terms


def stage_kernel(count, coeff, has_acc, last, *refs):
    slabs = refs[:count]
    first_ref, second_ref = refs[count : count + 2]
    accs = refs[count + 2 : 2 * count + 2] if has_acc else [None] * count
    outs = refs[-count:]
    for slab_ref, acc_ref, out_ref in zip(slabs, accs, outs):
        terms = block_term(slab_ref, first_ref, second_ref, coeff)
        for k, term in enumerate(terms):
            rows = slice(k * CHUNK, (k + 1) * CHUNK)
            if acc_ref is not None:
                term = acc_ref[rows, :] + term
            if last:
                out_ref[:, rows] = term.T
            else:
                out_ref[rows, :] = term


def stage(slabs, first, second, accs, coeff, ritz, last=False):
    rows, feat = slabs[0].shape
    land = 2 * second.shape[0]
    count = len(slabs)
    shape = (ritz, rows) if last else (rows, ritz)
    return pl.pallas_call(
        functools.partial(stage_kernel, count, coeff, accs is not None, last),
        out_shape=[jax.ShapeDtypeStruct(shape, jnp.float32)] * count,
        compiler_params=pltpu.CompilerParams(vmem_limit_bytes=32 * MIB),
        cost_estimate=pl.CostEstimate(
            flops=2 * count * rows * land * (feat + 4 * ritz),
            bytes_accessed=2 * (count * rows + land) * feat,
            transcendentals=count * rows * land,
        ),
    )(*slabs, first, second, *(accs or []))


def split_kernel(a_ref, b_ref, *outs):
    n = len(outs)
    width = outs[0].shape[1]
    me = lax.axis_index("lm")
    for d, out_ref in enumerate(outs):
        part = pl.ds(pl.multiple_of(lax.rem(me + d, n) * width, width), width)
        out_ref[...] = a_ref[:, part] + b_ref[:, part]


def sum_kernel(*refs, total_land):
    parts, ritz_ref, out_ref = refs[:-2], refs[-2], refs[-1]
    total = parts[0][...]
    for part in parts[1:]:
        total = total + part[...]
    factor = 1.0 / (ritz_ref[...] * math.sqrt(total_land))
    out_ref[...] = (total * factor).astype(out_ref.dtype)


def join_kernel(*refs):
    parts, out_ref = refs[:-1], refs[-1]
    n = len(parts)
    width = parts[0].shape[1]
    me = lax.axis_index("lm")
    for d, ref in enumerate(parts):
        part = pl.ds(pl.multiple_of(lax.rem(me + n - d, n) * width, width), width)
        out_ref[:, part] = ref[...].astype(out_ref.dtype)


def small_call(kernel, shapes, dtype, *args):
    out = jax.tree.map(
        lambda shape: jax.ShapeDtypeStruct(shape, dtype), shapes, is_leaf=lambda x: isinstance(x, tuple)
    )
    return pl.pallas_call(
        kernel,
        out_shape=out,
        compiler_params=pltpu.CompilerParams(vmem_limit_bytes=8 * MIB),
    )(*args)


def local(slab, landmarks, codes, exponents, eigvec, ritz):
    n_lm, n_sl = lax.axis_size("lm"), lax.axis_size("sl")
    total_land = codes.shape[0] * n_lm * n_sl
    coeff = 1.0 / math.sqrt(slab.shape[1])
    cols = ritz.shape[0]
    rows = slab.shape[0]
    bits = [1 << k for k in range(1, n_sl.bit_length() - 1)]

    first, second = prepare(landmarks, codes.T, exponents, eigvec.T)
    firsts, seconds = {0: first}, {0: second}
    for k, bit in enumerate(bits):
        if k % 2 == 0:
            seconds[bit] = xor_send(second, bit, n_sl)
        else:
            firsts[bit] = xor_send(first, bit, n_sl)
    for k, bit in enumerate(bits):
        if k % 2 == 0:
            firsts[bit] = xor_send(first, bit, n_sl)
        else:
            seconds[bit] = xor_send(second, bit, n_sl)
    late_slab, _ = lax.optimization_barrier((slab, first))
    other = xor_send(late_slab, 1, n_sl)
    (acc,) = stage([slab], first, second, None, coeff, cols)
    early = [seconds if k % 2 == 0 else firsts for k in range(len(bits))]
    held = [part[bit] for part, bit in zip(early, bits)]
    held, acc = lax.optimization_barrier((held, acc))
    for part, bit, value in zip(early, bits, held):
        part[bit] = value
    (other_acc,) = stage([other], first, second, None, coeff, cols)
    accs = [acc, other_acc]
    for d in range(2, n_sl, 2):
        if d in firsts:
            continue
        own = [b for b in bits if d & b]
        low, high = own[0], own[-1]
        seconds[d] = xor_send(seconds[d ^ high], high, n_sl)
        firsts[d] = xor_send(firsts[d ^ low], low, n_sl)

    for d in range(2, n_sl - 2, 2):
        accs = stage([slab, other], firsts[d], seconds[d], accs, coeff, cols)
    d = n_sl - 2
    (theirs,) = stage([other], firsts[d], seconds[d], accs[1:], coeff, cols, last=True)
    received = xor_send(theirs, 1, n_sl)
    (mine,) = stage([slab], firsts[d], seconds[d], accs[:1], coeff, cols, last=True)

    part = (cols, rows // n_lm)
    parts = small_call(split_kernel, [part] * n_lm, jnp.float32, mine, received)
    parts = [lm_send(value, d, n_lm) if d else value for d, value in enumerate(parts)]
    total = functools.partial(sum_kernel, total_land=total_land)
    done = small_call(total, part, jnp.bfloat16, *parts, ritz[:, None])
    pieces = [lm_send(done, d, n_lm) if d else done for d in range(n_lm)]
    return small_call(join_kernel, (cols, rows), jnp.float32, *pieces).T


def solution(mesh):
    return jax.shard_map(
        local,
        mesh=mesh,
        in_specs=(
            P("sl", None),
            P(("lm", "sl"), None),
            P(("lm", "sl"), None),
            P(("lm", "sl")),
            P(),
            P(),
        ),
        out_specs=P("sl", None),
        check_vma=False,
    )
```

```python
import functools
import math

import jax
import jax.numpy as jnp
from jax import lax
from jax.experimental import pallas as pl
from jax.experimental.pallas import tpu as pltpu
from jax.sharding import PartitionSpec as P

BLOCK = 128
CHUNK = 256
MIB = 2**20


def core_send(value, n):
    return lax.ppermute(value, "sl", [(i, i ^ 1) for i in range(n)])


def chip_send(value, k, n):
    bits = [1 << b for b in range(1, n.bit_length() - 1)]
    return lax.ppermute(value, "sl", [(i, i ^ bits[(k + i % 2) % len(bits)]) for i in range(n)])


def lm_send(value, step, n):
    return lax.ppermute(value, "lm", [(i, (i + step) % n) for i in range(n)])


def prepare_kernel(
    land_ref, codes_ref, exponents_ref, eig_ref, first_ref, second_ref, codes, eig, exponents, sems
):
    rows, feat = land_ref.shape
    half = rows - second_ref.shape[0]
    ritz = eig_ref.shape[0]
    pairs = [
        (codes_ref, codes),
        (eig_ref, eig),
        (exponents_ref, exponents),
        (land_ref.at[:half], first_ref.at[:half]),
        (land_ref.at[half:], second_ref),
    ]
    copies = [pltpu.make_async_copy(src, dst, sems.at[k]) for k, (src, dst) in enumerate(pairs)]
    for copy in copies:
        copy.start()
    for copy in copies[:3]:
        copy.wait()
    pieces = []
    for b in range(rows // BLOCK):
        scale = lax.shift_left(jnp.int32(1), exponents[b] + 15).astype(jnp.float32) * 2.0**-15
        pieces.append(codes[:, b * BLOCK : (b + 1) * BLOCK].astype(jnp.float32) * scale)
    basis = jnp.concatenate(pieces, axis=1).astype(jnp.bfloat16)
    vectors = jnp.dot(eig[...], basis, preferred_element_type=jnp.float32).astype(jnp.bfloat16)
    chunks = feat // rows
    depth = ritz // chunks
    for c in range(chunks):
        first_ref[half:, c * rows : (c + 1) * rows] = vectors[c * depth : (c + 1) * depth, :]
    for copy in copies[3:]:
        copy.wait()


def prepare(landmarks, codes_t, exponents, eig_t):
    rows, feat = landmarks.shape
    extra = eig_t.shape[0] * rows // feat
    head = rows // 2
    return pl.pallas_call(
        prepare_kernel,
        out_shape=[
            jax.ShapeDtypeStruct((head + extra, feat), jnp.bfloat16),
            jax.ShapeDtypeStruct((rows - head, feat), jnp.bfloat16),
        ],
        in_specs=[pl.BlockSpec(memory_space=pltpu.HBM)] * 4,
        scratch_shapes=[
            pltpu.VMEM(codes_t.shape, codes_t.dtype),
            pltpu.VMEM(eig_t.shape, eig_t.dtype),
            pltpu.SMEM(exponents.shape, exponents.dtype),
            pltpu.SemaphoreType.DMA((5,)),
        ],
        compiler_params=pltpu.CompilerParams(vmem_limit_bytes=8 * MIB),
    )(*(pltpu.with_memory_space_constraint(x, pltpu.HBM) for x in (landmarks, codes_t, exponents, eig_t)))


def block_term(slab_ref, first_ref, second_ref, coeff, ritz):
    tail, feat = second_ref.shape
    rows = (first_ref.shape[0] + tail) * feat // (feat + ritz)
    head = rows - tail
    land = jnp.concatenate([first_ref[:head, :], second_ref[...]], axis=0)
    vec = jnp.concatenate(
        [first_ref[head:, c * rows : (c + 1) * rows] for c in range(feat // rows)], axis=0
    )
    dims = (((1,), (1,)), ((), ()))

    def scores(k):
        piece = slab_ref[k * CHUNK : (k + 1) * CHUNK, :]
        return lax.dot_general(piece, land, dims, preferred_element_type=jnp.float32)

    count = slab_ref.shape[0] // CHUNK
    terms = []
    ahead = scores(0)
    for k in range(count):
        now, ahead = ahead, scores(k + 1) if k + 1 < count else None
        affinity = jnp.exp(now * coeff).astype(jnp.bfloat16)
        terms.append(lax.dot_general(affinity, vec, dims, preferred_element_type=jnp.float32))
    return terms


def stage_kernel(count, coeff, ritz, has_acc, last, *refs):
    slabs = refs[:count]
    first_ref, second_ref = refs[count : count + 2]
    accs = refs[count + 2 : 2 * count + 2] if has_acc else [None] * count
    outs = refs[-count:]
    for slab_ref, acc_ref, out_ref in zip(slabs, accs, outs):
        terms = block_term(slab_ref, first_ref, second_ref, coeff, ritz)
        for k, term in enumerate(terms):
            rows = slice(k * CHUNK, (k + 1) * CHUNK)
            if acc_ref is not None:
                term = acc_ref[rows, :] + term
            if last:
                out_ref[:, rows] = term.T
            else:
                out_ref[rows, :] = term


def stage(slabs, first, second, accs, coeff, ritz, last=False):
    rows, feat = slabs[0].shape
    land = (first.shape[0] + second.shape[0]) * feat // (feat + ritz)
    count = len(slabs)
    shape = (ritz, rows) if last else (rows, ritz)
    return pl.pallas_call(
        functools.partial(stage_kernel, count, coeff, ritz, accs is not None, last),
        out_shape=[jax.ShapeDtypeStruct(shape, jnp.float32)] * count,
        compiler_params=pltpu.CompilerParams(vmem_limit_bytes=32 * MIB),
        cost_estimate=pl.CostEstimate(
            flops=2 * count * rows * land * (feat + 4 * ritz),
            bytes_accessed=2 * (count * rows + land) * feat,
            transcendentals=count * rows * land,
        ),
    )(*slabs, first, second, *(accs or []))


def split_kernel(a_ref, b_ref, *outs):
    n = len(outs)
    width = outs[0].shape[1]
    me = lax.axis_index("lm")
    for d, out_ref in enumerate(outs):
        part = pl.ds(pl.multiple_of(lax.rem(me + d, n) * width, width), width)
        out_ref[...] = (a_ref[:, part] + b_ref[:, part]).astype(out_ref.dtype)


def sum_kernel(*refs, total_land):
    parts, ritz_ref, out_ref = refs[:-2], refs[-2], refs[-1]
    total = parts[0][...]
    for part in parts[1:]:
        total = total + part[...].astype(jnp.float32)
    factor = 1.0 / (ritz_ref[...] * math.sqrt(total_land))
    out_ref[...] = (total * factor).astype(out_ref.dtype)


def join_kernel(*refs):
    parts, out_ref = refs[:-1], refs[-1]
    n = len(parts)
    width = parts[0].shape[1]
    me = lax.axis_index("lm")
    for d, ref in enumerate(parts):
        part = pl.ds(pl.multiple_of(lax.rem(me + n - d, n) * width, width), width)
        out_ref[:, part] = ref[...].astype(out_ref.dtype)


def small_call(kernel, out, *args):
    return pl.pallas_call(
        kernel,
        out_shape=out,
        compiler_params=pltpu.CompilerParams(vmem_limit_bytes=8 * MIB),
    )(*args)


def local(slab, landmarks, codes, exponents, eigvec, ritz):
    n_lm, n_sl = lax.axis_size("lm"), lax.axis_size("sl")
    total_land = codes.shape[0] * n_lm * n_sl
    coeff = 1.0 / math.sqrt(slab.shape[1])
    cols = ritz.shape[0]
    rows = slab.shape[0]
    ways = n_sl.bit_length() - 2

    first, second = prepare(landmarks, codes.T, exponents, eigvec.T)
    blocks = {0: [first, second]}
    for k in range(ways):
        blocks[1 << k] = [None, None]
    for turn in (0, 1):
        for k in range(ways):
            piece = (k + turn) % 2
            blocks[1 << k][piece] = chip_send(blocks[0][piece], k, n_sl)
    late_slab, _ = lax.optimization_barrier((slab, first))
    other = core_send(late_slab, n_sl)
    (acc,) = stage([slab], first, second, None, coeff, cols)
    held = [blocks[1 << k][k % 2] for k in range(ways)]
    held, acc = lax.optimization_barrier((held, acc))
    for k in range(ways):
        blocks[1 << k][k % 2] = held[k]
    (other_acc,) = stage([other], first, second, None, coeff, cols)
    accs = [acc, other_acc]
    for t in range(1, 1 << ways):
        if t in blocks:
            continue
        low, high = (t & -t).bit_length() - 1, t.bit_length() - 1
        blocks[t] = [
            chip_send(blocks[t ^ (1 << high)][0], high, n_sl),
            chip_send(blocks[t ^ (1 << low)][1], low, n_sl),
        ]

    for t in range(1, (1 << ways) - 1):
        accs = stage([slab, other], *blocks[t], accs, coeff, cols)
    end = blocks[(1 << ways) - 1]
    (theirs,) = stage([other], *end, accs[1:], coeff, cols, last=True)
    received = core_send(theirs, n_sl)
    (mine,) = stage([slab], *end, accs[:1], coeff, cols, last=True)

    wide = jax.ShapeDtypeStruct((cols, rows // n_lm), jnp.float32)
    narrow = jax.ShapeDtypeStruct(wide.shape, jnp.bfloat16)
    parts = small_call(split_kernel, [wide] + [narrow] * (n_lm - 1), mine, received)
    parts = [lm_send(value, d, n_lm) if d else value for d, value in enumerate(parts)]
    total = functools.partial(sum_kernel, total_land=total_land)
    done = small_call(total, narrow, *parts, ritz[:, None])
    pieces = [lm_send(done, d, n_lm) if d else done for d in range(n_lm)]
    return small_call(join_kernel, jax.ShapeDtypeStruct((cols, rows), jnp.float32), *pieces).T


def solution(mesh):
    return jax.shard_map(
        local,
        mesh=mesh,
        in_specs=(
            P("sl", None),
            P(("lm", "sl"), None),
            P(("lm", "sl"), None),
            P(("lm", "sl")),
            P(),
            P(),
        ),
        out_specs=P("sl", None),
        check_vma=False,
    )
```

```python
import functools
import math

import jax
import jax.numpy as jnp
from jax import lax
from jax.experimental import pallas as pl
from jax.experimental.pallas import tpu as pltpu
from jax.sharding import PartitionSpec as P

BLOCK = 128
CHUNK = 256
MIB = 2**20


def core_send(value, n):
    return lax.ppermute(value, "sl", [(i, i ^ 1) for i in range(n)])


def chip_send(value, k, n):
    bits = [1 << b for b in range(1, n.bit_length() - 1)]
    return lax.ppermute(value, "sl", [(i, i ^ bits[(k + i % 2) % len(bits)]) for i in range(n)])


def lm_send(value, bit, n):
    return lax.ppermute(value, "lm", [(i, i ^ bit) for i in range(n)])


def prepare_kernel(
    land_ref, codes_ref, exponents_ref, eig_ref, first_ref, second_ref, codes, eig, exponents, sems
):
    rows, feat = land_ref.shape
    half = rows - second_ref.shape[0]
    ritz = eig_ref.shape[0]
    pairs = [
        (codes_ref, codes),
        (eig_ref, eig),
        (exponents_ref, exponents),
        (land_ref.at[:half], first_ref.at[:half]),
        (land_ref.at[half:], second_ref),
    ]
    copies = [pltpu.make_async_copy(src, dst, sems.at[k]) for k, (src, dst) in enumerate(pairs)]
    for copy in copies:
        copy.start()
    for copy in copies[:3]:
        copy.wait()
    pieces = []
    for b in range(rows // BLOCK):
        scale = lax.shift_left(jnp.int32(1), exponents[b] + 15).astype(jnp.float32) * 2.0**-15
        pieces.append(codes[:, b * BLOCK : (b + 1) * BLOCK].astype(jnp.float32) * scale)
    basis = jnp.concatenate(pieces, axis=1).astype(jnp.bfloat16)
    vectors = jnp.dot(eig[...], basis, preferred_element_type=jnp.float32).astype(jnp.bfloat16)
    chunks = feat // rows
    depth = ritz // chunks
    for c in range(chunks):
        first_ref[half:, c * rows : (c + 1) * rows] = vectors[c * depth : (c + 1) * depth, :]
    for copy in copies[3:]:
        copy.wait()


def prepare(landmarks, codes_t, exponents, eig_t):
    rows, feat = landmarks.shape
    extra = eig_t.shape[0] * rows // feat
    head = rows // 2
    return pl.pallas_call(
        prepare_kernel,
        out_shape=[
            jax.ShapeDtypeStruct((head + extra, feat), jnp.bfloat16),
            jax.ShapeDtypeStruct((rows - head, feat), jnp.bfloat16),
        ],
        in_specs=[pl.BlockSpec(memory_space=pltpu.HBM)] * 4,
        scratch_shapes=[
            pltpu.VMEM(codes_t.shape, codes_t.dtype),
            pltpu.VMEM(eig_t.shape, eig_t.dtype),
            pltpu.SMEM(exponents.shape, exponents.dtype),
            pltpu.SemaphoreType.DMA((5,)),
        ],
        compiler_params=pltpu.CompilerParams(vmem_limit_bytes=8 * MIB),
    )(*(pltpu.with_memory_space_constraint(x, pltpu.HBM) for x in (landmarks, codes_t, exponents, eig_t)))


def transpose_kernel(in_ref, out_ref):
    for k in range(in_ref.shape[0] // CHUNK):
        rows = slice(k * CHUNK, (k + 1) * CHUNK)
        out_ref[:, rows] = in_ref[rows, :].T


def stage_kernel(count, coeff, ritz, has_acc, *refs):
    slabs = refs[:count]
    first_ref, second_ref = refs[count : count + 2]
    accs = refs[count + 2 : 2 * count + 2] if has_acc else [None] * count
    outs = refs[-count:]
    tail, feat = second_ref.shape
    rows = (first_ref.shape[0] + tail) * feat // (feat + ritz)
    head = rows - tail
    land = jnp.concatenate([first_ref[:head, :], second_ref[...]], axis=0)
    vec = jnp.concatenate(
        [first_ref[head:, c * rows : (c + 1) * rows] for c in range(feat // rows)], axis=0
    )
    work = [
        (k, slice(c * CHUNK, (c + 1) * CHUNK))
        for k in range(count)
        for c in range(slabs[k].shape[1] // CHUNK)
    ]

    def scores(k, cols):
        return jnp.dot(land, slabs[k][:, cols], preferred_element_type=jnp.float32)

    ahead = scores(*work[0])
    for n, (k, cols) in enumerate(work):
        now, ahead = ahead, scores(*work[n + 1]) if n + 1 < len(work) else None
        affinity = jnp.exp(now * coeff).astype(jnp.bfloat16)
        term = jnp.dot(vec, affinity, preferred_element_type=jnp.float32)
        outs[k][:, cols] = term if accs[k] is None else accs[k][:, cols] + term


def stage(slabs, first, second, accs, coeff, ritz):
    feat, rows = slabs[0].shape
    land = (first.shape[0] + second.shape[0]) * feat // (feat + ritz)
    count = len(slabs)
    return pl.pallas_call(
        functools.partial(stage_kernel, count, coeff, ritz, accs is not None),
        out_shape=[jax.ShapeDtypeStruct((ritz, rows), jnp.float32)] * count,
        compiler_params=pltpu.CompilerParams(vmem_limit_bytes=32 * MIB),
        cost_estimate=pl.CostEstimate(
            flops=2 * count * rows * land * (feat + 4 * ritz),
            bytes_accessed=2 * (count * rows + land) * feat,
            transcendentals=count * rows * land,
        ),
    )(*slabs, first, second, *(accs or []))


def add_kernel(a_ref, b_ref, out_ref):
    total = a_ref[...].astype(jnp.float32) + b_ref[...].astype(jnp.float32)
    out_ref[...] = total.astype(out_ref.dtype)


def scale_kernel(a_ref, b_ref, ritz_ref, out_ref, *, total_land):
    factor = 1.0 / (ritz_ref[...] * math.sqrt(total_land))
    total = a_ref[...].astype(jnp.float32) + b_ref[...].astype(jnp.float32)
    out_ref[...] = total * factor


def small_call(kernel, out, *args):
    return pl.pallas_call(
        kernel,
        out_shape=jax.ShapeDtypeStruct(out.shape, out.dtype),
        compiler_params=pltpu.CompilerParams(vmem_limit_bytes=8 * MIB),
    )(*args)


def local(slab, landmarks, codes, exponents, eigvec, ritz):
    n_lm, n_sl = lax.axis_size("lm"), lax.axis_size("sl")
    total_land = codes.shape[0] * n_lm * n_sl
    coeff = 1.0 / math.sqrt(slab.shape[1])
    cols = ritz.shape[0]
    ways = n_sl.bit_length() - 2

    first, second = prepare(landmarks, codes.T, exponents, eigvec.T)
    blocks = {0: [first, second]}
    for k in range(ways):
        blocks[1 << k] = [None, None]
    for turn in (0, 1):
        for k in range(ways):
            piece = (k + turn) % 2
            blocks[1 << k][piece] = chip_send(blocks[0][piece], k, n_sl)
    late_slab, _ = lax.optimization_barrier((slab, first))
    turned = jax.ShapeDtypeStruct(slab.shape[::-1], slab.dtype)
    other = small_call(transpose_kernel, turned, core_send(late_slab, n_sl))
    slab = small_call(transpose_kernel, turned, slab)
    (acc,) = stage([slab], first, second, None, coeff, cols)
    held = [blocks[1 << k][k % 2] for k in range(ways)]
    held, acc = lax.optimization_barrier((held, acc))
    for k in range(ways):
        blocks[1 << k][k % 2] = held[k]
    (other_acc,) = stage([other], first, second, None, coeff, cols)
    accs = [acc, other_acc]
    for t in range(1, 1 << ways):
        if t in blocks:
            continue
        low, high = (t & -t).bit_length() - 1, t.bit_length() - 1
        blocks[t] = [
            chip_send(blocks[t ^ (1 << high)][0], high, n_sl),
            chip_send(blocks[t ^ (1 << low)][1], low, n_sl),
        ]

    for t in range(1, (1 << ways) - 1):
        accs = stage([slab, other], *blocks[t], accs, coeff, cols)
    end = blocks[(1 << ways) - 1]
    (theirs,) = stage([other], *end, accs[1:], coeff, cols)
    received = core_send(theirs, n_sl)
    (mine,) = stage([slab], *end, accs[:1], coeff, cols)

    total = small_call(add_kernel, jax.ShapeDtypeStruct(mine.shape, jnp.bfloat16), mine, received)
    lm_bits = [1 << k for k in range(n_lm.bit_length() - 1)]
    for bit in lm_bits[:-1]:
        total = small_call(add_kernel, total, total, lm_send(total, bit, n_lm))
    scale = functools.partial(scale_kernel, total_land=total_land)
    return small_call(scale, mine, total, lm_send(total, lm_bits[-1], n_lm), ritz[:, None]).T


def solution(mesh):
    return jax.shard_map(
        local,
        mesh=mesh,
        in_specs=(
            P("sl", None),
            P(("lm", "sl"), None),
            P(("lm", "sl"), None),
            P(("lm", "sl")),
            P(),
            P(),
        ),
        out_specs=P("sl", None),
        check_vma=False,
    )
```

```python
import functools
import math

import jax
import jax.numpy as jnp
from jax import lax
from jax.experimental import pallas as pl
from jax.experimental.pallas import tpu as pltpu
from jax.sharding import PartitionSpec as P

BLOCK = 128
CHUNK = 512
HALVES = 2
MIB = 2**20


def core_send(value, n):
    return lax.ppermute(value, "sl", [(i, i ^ 1) for i in range(n)])


def chip_send(value, k, n):
    bits = [1 << b for b in range(1, n.bit_length() - 1)]
    return lax.ppermute(value, "sl", [(i, i ^ bits[(k + i % 2) % len(bits)]) for i in range(n)])


def lm_send(value, bit, n):
    return lax.ppermute(value, "lm", [(i, i ^ bit) for i in range(n)])


def prepare_kernel(
    land_ref, codes_ref, exponents_ref, eig_ref, first_ref, second_ref, codes, eig, exponents, sems
):
    rows, feat = land_ref.shape
    half = rows - second_ref.shape[0]
    ritz = eig_ref.shape[0]
    pairs = [
        (codes_ref, codes),
        (eig_ref, eig),
        (exponents_ref, exponents),
        (land_ref.at[:half], first_ref.at[:half]),
        (land_ref.at[half:], second_ref),
    ]
    copies = [pltpu.make_async_copy(src, dst, sems.at[k]) for k, (src, dst) in enumerate(pairs)]
    for copy in copies:
        copy.start()
    for copy in copies[:3]:
        copy.wait()
    pieces = []
    for b in range(rows // BLOCK):
        scale = lax.shift_left(jnp.int32(1), exponents[b] + 15).astype(jnp.float32) * 2.0**-15
        pieces.append(codes[:, b * BLOCK : (b + 1) * BLOCK].astype(jnp.float32) * scale)
    basis = jnp.concatenate(pieces, axis=1).astype(jnp.bfloat16)
    vectors = jnp.dot(eig[...], basis, preferred_element_type=jnp.float32).astype(jnp.bfloat16)
    chunks = feat // rows
    depth = ritz // chunks
    for c in range(chunks):
        first_ref[half:, c * rows : (c + 1) * rows] = vectors[c * depth : (c + 1) * depth, :]
    for copy in copies[3:]:
        copy.wait()


def prepare(landmarks, codes_t, exponents, eig_t):
    rows, feat = landmarks.shape
    extra = eig_t.shape[0] * rows // feat
    head = rows // 2
    return pl.pallas_call(
        prepare_kernel,
        out_shape=[
            jax.ShapeDtypeStruct((head + extra, feat), jnp.bfloat16),
            jax.ShapeDtypeStruct((rows - head, feat), jnp.bfloat16),
        ],
        in_specs=[pl.BlockSpec(memory_space=pltpu.HBM)] * 4,
        scratch_shapes=[
            pltpu.VMEM(codes_t.shape, codes_t.dtype),
            pltpu.VMEM(eig_t.shape, eig_t.dtype),
            pltpu.SMEM(exponents.shape, exponents.dtype),
            pltpu.SemaphoreType.DMA((5,)),
        ],
        compiler_params=pltpu.CompilerParams(vmem_limit_bytes=8 * MIB),
    )(*(pltpu.with_memory_space_constraint(x, pltpu.HBM) for x in (landmarks, codes_t, exponents, eig_t)))


def transpose_kernel(in_ref, out_ref):
    for k in range(in_ref.shape[0] // CHUNK):
        rows = slice(k * CHUNK, (k + 1) * CHUNK)
        out_ref[:, rows] = in_ref[rows, :].T


def stage_kernel(count, coeff, ritz, has_acc, span, *refs):
    start, stop = span
    slabs = refs[:count]
    first_ref, second_ref = refs[count : count + 2]
    accs = refs[count + 2 : 2 * count + 2] if has_acc else [None] * count
    outs = refs[-count:]
    tail, feat = second_ref.shape
    rows = (first_ref.shape[0] + tail) * feat // (feat + ritz)
    head = rows - tail
    land = jnp.concatenate([first_ref[:head, :], second_ref[...]], axis=0)
    vec = jnp.concatenate(
        [first_ref[head:, c * rows : (c + 1) * rows] for c in range(feat // rows)], axis=0
    )
    work = [
        (k, slice(c, min(c + CHUNK, stop))) for k in range(count) for c in range(start, stop, CHUNK)
    ]

    def scores(k, cols):
        return jnp.dot(land, slabs[k][:, cols], preferred_element_type=jnp.float32)

    ahead = scores(*work[0])
    for n, (k, cols) in enumerate(work):
        now, ahead = ahead, scores(*work[n + 1]) if n + 1 < len(work) else None
        affinity = jnp.exp(now * coeff).astype(jnp.bfloat16)
        term = jnp.dot(vec, affinity, preferred_element_type=jnp.float32)
        place = slice(cols.start - start, cols.stop - start)
        outs[k][:, place] = term if accs[k] is None else accs[k][:, cols] + term


def stage(slabs, first, second, accs, coeff, ritz, span=None):
    feat, rows = slabs[0].shape
    span = span or (0, rows)
    rows = span[1] - span[0]
    land = (first.shape[0] + second.shape[0]) * feat // (feat + ritz)
    count = len(slabs)
    return pl.pallas_call(
        functools.partial(stage_kernel, count, coeff, ritz, accs is not None, span),
        out_shape=[jax.ShapeDtypeStruct((ritz, rows), jnp.float32)] * count,
        compiler_params=pltpu.CompilerParams(vmem_limit_bytes=32 * MIB),
        cost_estimate=pl.CostEstimate(
            flops=2 * count * rows * land * (feat + 4 * ritz),
            bytes_accessed=2 * (count * rows + land) * feat,
            transcendentals=count * rows * land,
        ),
    )(*slabs, first, second, *(accs or []))


def add_kernel(a_ref, b_ref, out_ref):
    total = a_ref[...].astype(jnp.float32) + b_ref[...].astype(jnp.float32)
    out_ref[...] = total.astype(out_ref.dtype)


def scale_kernel(*refs, total_land):
    ritz_ref, out_ref = refs[-2:]
    factor = 1.0 / (ritz_ref[...] * math.sqrt(total_land))
    start = 0
    for a_ref, b_ref in zip(refs[0:-2:2], refs[1:-2:2]):
        stop = start + a_ref.shape[1]
        total = a_ref[...].astype(jnp.float32) + b_ref[...].astype(jnp.float32)
        out_ref[:, start:stop] = total * factor
        start = stop


def small_call(kernel, out, *args):
    return pl.pallas_call(
        kernel,
        out_shape=jax.ShapeDtypeStruct(out.shape, out.dtype),
        compiler_params=pltpu.CompilerParams(vmem_limit_bytes=8 * MIB),
    )(*args)


def local(slab, landmarks, codes, exponents, eigvec, ritz):
    n_lm, n_sl = lax.axis_size("lm"), lax.axis_size("sl")
    total_land = codes.shape[0] * n_lm * n_sl
    coeff = 1.0 / math.sqrt(slab.shape[1])
    cols = ritz.shape[0]
    rows = slab.shape[0]
    ways = n_sl.bit_length() - 2

    first, second = prepare(landmarks, codes.T, exponents, eigvec.T)
    blocks = {0: [first, second]}
    for k in range(ways):
        blocks[1 << k] = [None, None]
    for turn in (0, 1):
        for k in range(ways):
            piece = (k + turn) % 2
            blocks[1 << k][piece] = chip_send(blocks[0][piece], k, n_sl)
    late_slab, _ = lax.optimization_barrier((slab, first))
    turned = jax.ShapeDtypeStruct(slab.shape[::-1], slab.dtype)
    other = small_call(transpose_kernel, turned, core_send(late_slab, n_sl))
    slab = small_call(transpose_kernel, turned, slab)
    (acc,) = stage([slab], first, second, None, coeff, cols)
    held = [blocks[1 << k][k % 2] for k in range(ways)]
    held, acc = lax.optimization_barrier((held, acc))
    for k in range(ways):
        blocks[1 << k][k % 2] = held[k]
    (other_acc,) = stage([other], first, second, None, coeff, cols)
    accs = [acc, other_acc]
    for t in range(1, 1 << ways):
        if t in blocks:
            continue
        low, high = (t & -t).bit_length() - 1, t.bit_length() - 1
        blocks[t] = [
            chip_send(blocks[t ^ (1 << high)][0], high, n_sl),
            chip_send(blocks[t ^ (1 << low)][1], low, n_sl),
        ]

    for t in range(1, (1 << ways) - 1):
        accs = stage([slab, other], *blocks[t], accs, coeff, cols)
    end = blocks[(1 << ways) - 1]
    width = rows // HALVES
    spans = [(h * width, (h + 1) * width) for h in range(HALVES)]
    theirs = [stage([other], *end, accs[1:], coeff, cols, span)[0] for span in spans]
    received = [core_send(value, n_sl) for value in theirs]
    half = jax.ShapeDtypeStruct((cols, width), jnp.bfloat16)
    totals, acc = [], accs[0]
    for span, part in zip(spans, received):
        (mine,) = stage([slab], *end, [acc], coeff, cols, span)
        total = small_call(add_kernel, half, mine, part)
        acc, total = lax.optimization_barrier((acc, total))
        totals.append(total)
    lm_bits = [1 << k for k in range(n_lm.bit_length() - 1)]
    for bit in lm_bits[:-1]:
        arrived = [lm_send(total, bit, n_lm) for total in totals]
        totals = [small_call(add_kernel, half, a, b) for a, b in zip(totals, arrived)]
    pairs = [(total, lm_send(total, lm_bits[-1], n_lm)) for total in totals]
    scale = functools.partial(scale_kernel, total_land=total_land)
    out = jax.ShapeDtypeStruct((cols, rows), jnp.float32)
    return small_call(scale, out, *(x for pair in pairs for x in pair), ritz[:, None]).T


def solution(mesh):
    return jax.shard_map(
        local,
        mesh=mesh,
        in_specs=(
            P("sl", None),
            P(("lm", "sl"), None),
            P(("lm", "sl"), None),
            P(("lm", "sl")),
            P(),
            P(),
        ),
        out_specs=P("sl", None),
        check_vma=False,
    )
```

```python
import functools
import math

import jax
import jax.numpy as jnp
from jax import lax
from jax.experimental import pallas as pl
from jax.experimental.pallas import tpu as pltpu
from jax.sharding import PartitionSpec as P

BLOCK = 128
CHUNK = 512
HALVES = 2
MIB = 2**20


def core_send(value, n):
    return lax.ppermute(value, "sl", [(i, i ^ 1) for i in range(n)])


def chip_send(value, k, n):
    bits = [1 << b for b in range(1, n.bit_length() - 1)]
    return lax.ppermute(value, "sl", [(i, i ^ bits[(k + i % 2) % len(bits)]) for i in range(n)])


def lm_send(value, k, n_lm, n_sl):
    bits = [1 << b for b in range(n_lm.bit_length() - 1)]
    perm = [
        (i * n_sl + j, (i ^ bits[(k + j % 2) % len(bits)]) * n_sl + j)
        for i in range(n_lm)
        for j in range(n_sl)
    ]
    return lax.ppermute(value, ("lm", "sl"), perm)


def prepare_kernel(
    land_ref, codes_ref, exponents_ref, eig_ref, first_ref, second_ref, codes, eig, exponents, sems
):
    rows, feat = land_ref.shape
    half = rows - second_ref.shape[0]
    ritz = eig_ref.shape[0]
    pairs = [
        (codes_ref, codes),
        (eig_ref, eig),
        (exponents_ref, exponents),
        (land_ref.at[:half], first_ref.at[:half]),
        (land_ref.at[half:], second_ref),
    ]
    copies = [pltpu.make_async_copy(src, dst, sems.at[k]) for k, (src, dst) in enumerate(pairs)]
    for copy in copies:
        copy.start()
    for copy in copies[:3]:
        copy.wait()
    pieces = []
    for b in range(rows // BLOCK):
        scale = lax.shift_left(jnp.int32(1), exponents[b] + 15).astype(jnp.float32) * 2.0**-15
        pieces.append(codes[:, b * BLOCK : (b + 1) * BLOCK].astype(jnp.float32) * scale)
    basis = jnp.concatenate(pieces, axis=1).astype(jnp.bfloat16)
    vectors = jnp.dot(eig[...], basis, preferred_element_type=jnp.float32).astype(jnp.bfloat16)
    chunks = feat // rows
    depth = ritz // chunks
    for c in range(chunks):
        first_ref[half:, c * rows : (c + 1) * rows] = vectors[c * depth : (c + 1) * depth, :]
    for copy in copies[3:]:
        copy.wait()


def prepare(landmarks, codes_t, exponents, eig_t):
    rows, feat = landmarks.shape
    extra = eig_t.shape[0] * rows // feat
    head = rows // 2
    return pl.pallas_call(
        prepare_kernel,
        out_shape=[
            jax.ShapeDtypeStruct((head + extra, feat), jnp.bfloat16),
            jax.ShapeDtypeStruct((rows - head, feat), jnp.bfloat16),
        ],
        in_specs=[pl.BlockSpec(memory_space=pltpu.HBM)] * 4,
        scratch_shapes=[
            pltpu.VMEM(codes_t.shape, codes_t.dtype),
            pltpu.VMEM(eig_t.shape, eig_t.dtype),
            pltpu.SMEM(exponents.shape, exponents.dtype),
            pltpu.SemaphoreType.DMA((5,)),
        ],
        compiler_params=pltpu.CompilerParams(vmem_limit_bytes=8 * MIB),
    )(*(pltpu.with_memory_space_constraint(x, pltpu.HBM) for x in (landmarks, codes_t, exponents, eig_t)))


def transpose_kernel(in_ref, out_ref):
    for k in range(in_ref.shape[0] // CHUNK):
        rows = slice(k * CHUNK, (k + 1) * CHUNK)
        out_ref[:, rows] = in_ref[rows, :].T


def stage_kernel(count, coeff, ritz, has_acc, span, *refs):
    start, stop = span
    slabs = refs[:count]
    first_ref, second_ref = refs[count : count + 2]
    accs = refs[count + 2 : 2 * count + 2] if has_acc else [None] * count
    outs = refs[-count:]
    tail, feat = second_ref.shape
    rows = (first_ref.shape[0] + tail) * feat // (feat + ritz)
    head = rows - tail
    land = jnp.concatenate([first_ref[:head, :], second_ref[...]], axis=0)
    vec = jnp.concatenate(
        [first_ref[head:, c * rows : (c + 1) * rows] for c in range(feat // rows)], axis=0
    )
    work = [
        (k, slice(c, min(c + CHUNK, stop))) for k in range(count) for c in range(start, stop, CHUNK)
    ]

    def scores(k, cols):
        return jnp.dot(land, slabs[k][:, cols], preferred_element_type=jnp.float32)

    ahead = scores(*work[0])
    for n, (k, cols) in enumerate(work):
        now, ahead = ahead, scores(*work[n + 1]) if n + 1 < len(work) else None
        affinity = jnp.exp(now * coeff).astype(jnp.bfloat16)
        term = jnp.dot(vec, affinity, preferred_element_type=jnp.float32)
        place = slice(cols.start - start, cols.stop - start)
        outs[k][:, place] = term if accs[k] is None else accs[k][:, cols] + term


def stage(slabs, first, second, accs, coeff, ritz, span=None):
    feat, rows = slabs[0].shape
    span = span or (0, rows)
    rows = span[1] - span[0]
    land = (first.shape[0] + second.shape[0]) * feat // (feat + ritz)
    count = len(slabs)
    return pl.pallas_call(
        functools.partial(stage_kernel, count, coeff, ritz, accs is not None, span),
        out_shape=[jax.ShapeDtypeStruct((ritz, rows), jnp.float32)] * count,
        compiler_params=pltpu.CompilerParams(vmem_limit_bytes=32 * MIB),
        cost_estimate=pl.CostEstimate(
            flops=2 * count * rows * land * (feat + 4 * ritz),
            bytes_accessed=2 * (count * rows + land) * feat,
            transcendentals=count * rows * land,
        ),
    )(*slabs, first, second, *(accs or []))


def add_kernel(a_ref, b_ref, out_ref):
    total = a_ref[...].astype(jnp.float32) + b_ref[...].astype(jnp.float32)
    out_ref[...] = total.astype(out_ref.dtype)


def scale_kernel(*refs, total_land):
    ritz_ref, out_ref = refs[-2:]
    factor = 1.0 / (ritz_ref[...] * math.sqrt(total_land))
    start = 0
    for a_ref, b_ref in zip(refs[0:-2:2], refs[1:-2:2]):
        stop = start + a_ref.shape[1]
        total = a_ref[...].astype(jnp.float32) + b_ref[...].astype(jnp.float32)
        out_ref[:, start:stop] = total * factor
        start = stop


def small_call(kernel, out, *args):
    return pl.pallas_call(
        kernel,
        out_shape=jax.ShapeDtypeStruct(out.shape, out.dtype),
        compiler_params=pltpu.CompilerParams(vmem_limit_bytes=8 * MIB),
    )(*args)


def local(slab, landmarks, codes, exponents, eigvec, ritz):
    n_lm, n_sl = lax.axis_size("lm"), lax.axis_size("sl")
    total_land = codes.shape[0] * n_lm * n_sl
    coeff = 1.0 / math.sqrt(slab.shape[1])
    cols = ritz.shape[0]
    rows = slab.shape[0]
    ways = n_sl.bit_length() - 2

    first, second = prepare(landmarks, codes.T, exponents, eigvec.T)
    blocks = {0: [first, second]}
    for k in range(ways):
        blocks[1 << k] = [None, None]
    for turn in (0, 1):
        for k in range(ways):
            piece = (k + turn) % 2
            blocks[1 << k][piece] = chip_send(blocks[0][piece], k, n_sl)
    late_slab, _ = lax.optimization_barrier((slab, first))
    turned = jax.ShapeDtypeStruct(slab.shape[::-1], slab.dtype)
    other = small_call(transpose_kernel, turned, core_send(late_slab, n_sl))
    slab = small_call(transpose_kernel, turned, slab)
    (acc,) = stage([slab], first, second, None, coeff, cols)
    held = [blocks[1 << k][k % 2] for k in range(ways)]
    held, acc = lax.optimization_barrier((held, acc))
    for k in range(ways):
        blocks[1 << k][k % 2] = held[k]
    (other_acc,) = stage([other], first, second, None, coeff, cols)
    accs = [acc, other_acc]
    for t in range(1, 1 << ways):
        if t in blocks:
            continue
        low, high = (t & -t).bit_length() - 1, t.bit_length() - 1
        blocks[t] = [
            chip_send(blocks[t ^ (1 << high)][0], high, n_sl),
            chip_send(blocks[t ^ (1 << low)][1], low, n_sl),
        ]

    for t in range(1, (1 << ways) - 1):
        accs = stage([slab, other], *blocks[t], accs, coeff, cols)
    end = blocks[(1 << ways) - 1]
    width = rows // HALVES
    spans = [(h * width, (h + 1) * width) for h in range(HALVES)]
    theirs = [stage([other], *end, accs[1:], coeff, cols, span)[0] for span in spans]
    received = [core_send(value, n_sl) for value in theirs]
    half = jax.ShapeDtypeStruct((cols, width), jnp.bfloat16)
    totals, acc = [], accs[0]
    for span, part in zip(spans, received):
        (mine,) = stage([slab], *end, [acc], coeff, cols, span)
        total = small_call(add_kernel, half, mine, part)
        acc, total = lax.optimization_barrier((acc, total))
        totals.append(total)
    turns = n_lm.bit_length() - 1
    for k in range(turns - 1):
        arrived = [lm_send(total, k, n_lm, n_sl) for total in totals]
        totals = [small_call(add_kernel, half, a, b) for a, b in zip(totals, arrived)]
    pairs = [(total, lm_send(total, turns - 1, n_lm, n_sl)) for total in totals]
    scale = functools.partial(scale_kernel, total_land=total_land)
    out = jax.ShapeDtypeStruct((cols, rows), jnp.float32)
    return small_call(scale, out, *(x for pair in pairs for x in pair), ritz[:, None]).T


def solution(mesh):
    return jax.shard_map(
        local,
        mesh=mesh,
        in_specs=(
            P("sl", None),
            P(("lm", "sl"), None),
            P(("lm", "sl"), None),
            P(("lm", "sl")),
            P(),
            P(),
        ),
        out_specs=P("sl", None),
        check_vma=False,
    )
```

```python
import functools
import math

import jax
import jax.numpy as jnp
from jax import lax
from jax.experimental import pallas as pl
from jax.experimental.pallas import tpu as pltpu
from jax.sharding import PartitionSpec as P

BLOCK = 128
SHIFT = 16
CHUNK = 512
MIB = 2**20


def core_send(value, n):
    return lax.ppermute(value, "sl", [(i, i ^ 1) for i in range(n)])


def chip_send(value, k, n):
    bits = [1 << b for b in range(1, n.bit_length() - 1)]
    return lax.ppermute(value, "sl", [(i, i ^ bits[(k + i % 2) % len(bits)]) for i in range(n)])


def lm_send(value, k, n_lm, n_sl):
    bits = [1 << b for b in range(n_lm.bit_length() - 1)]
    perm = [
        (i * n_sl + j, (i ^ bits[(k + j % 2) % len(bits)]) * n_sl + j)
        for i in range(n_lm)
        for j in range(n_sl)
    ]
    return lax.ppermute(value, ("lm", "sl"), perm)


def prepare_kernel(
    land_ref, codes_ref, exponents_ref, eig_ref, first_ref, codes, eig, exponents, sems
):
    rows, feat = land_ref.shape
    half = rows // 2 - SHIFT
    ritz = eig_ref.shape[0]
    pairs = [
        (codes_ref, codes),
        (eig_ref, eig),
        (exponents_ref, exponents),
        (land_ref.at[:half], first_ref.at[:half]),
    ]
    copies = [pltpu.make_async_copy(src, dst, sems.at[k]) for k, (src, dst) in enumerate(pairs)]
    for copy in copies:
        copy.start()
    for copy in copies[:3]:
        copy.wait()
    pieces = []
    for b in range(rows // BLOCK):
        scale = lax.shift_left(jnp.int32(1), exponents[b] + 15).astype(jnp.float32) * 2.0**-15
        pieces.append(codes[:, b * BLOCK : (b + 1) * BLOCK].astype(jnp.float32) * scale)
    basis = jnp.concatenate(pieces, axis=1).astype(jnp.bfloat16)
    vectors = jnp.dot(eig[...], basis, preferred_element_type=jnp.float32).astype(jnp.bfloat16)
    chunks = feat // rows
    depth = ritz // chunks
    for c in range(chunks):
        first_ref[half:, c * rows : (c + 1) * rows] = vectors[c * depth : (c + 1) * depth, :]
    for copy in copies[3:]:
        copy.wait()


def tail_kernel(land_ref, out_ref, sem):
    copy = pltpu.make_async_copy(land_ref.at[land_ref.shape[0] - out_ref.shape[0] :], out_ref, sem)
    copy.start()
    copy.wait()


def second_half(landmarks):
    rows, feat = landmarks.shape
    return pl.pallas_call(
        tail_kernel,
        out_shape=jax.ShapeDtypeStruct((rows // 2 + SHIFT, feat), jnp.bfloat16),
        in_specs=[pl.BlockSpec(memory_space=pltpu.HBM)],
        scratch_shapes=[pltpu.SemaphoreType.DMA],
        compiler_params=pltpu.CompilerParams(vmem_limit_bytes=8 * MIB),
    )(pltpu.with_memory_space_constraint(landmarks, pltpu.HBM))


def prepare(landmarks, codes_t, exponents, eig_t):
    rows, feat = landmarks.shape
    extra = eig_t.shape[0] * rows // feat
    return pl.pallas_call(
        prepare_kernel,
        out_shape=jax.ShapeDtypeStruct((rows // 2 - SHIFT + extra, feat), jnp.bfloat16),
        in_specs=[pl.BlockSpec(memory_space=pltpu.HBM)] * 4,
        scratch_shapes=[
            pltpu.VMEM(codes_t.shape, codes_t.dtype),
            pltpu.VMEM(eig_t.shape, eig_t.dtype),
            pltpu.SMEM(exponents.shape, exponents.dtype),
            pltpu.SemaphoreType.DMA((4,)),
        ],
        compiler_params=pltpu.CompilerParams(vmem_limit_bytes=8 * MIB),
    )(*(pltpu.with_memory_space_constraint(x, pltpu.HBM) for x in (landmarks, codes_t, exponents, eig_t)))


def transpose_kernel(in_ref, out_ref):
    for k in range(in_ref.shape[0] // CHUNK):
        rows = slice(k * CHUNK, (k + 1) * CHUNK)
        out_ref[:, rows] = in_ref[rows, :].T


def stage_kernel(count, coeff, ritz, has_acc, spans, *refs):
    slabs = refs[:count]
    first_ref, second_ref = refs[count : count + 2]
    accs = refs[count + 2 : 2 * count + 2] if has_acc else [None] * count
    outs = refs[-count:]
    tail, feat = second_ref.shape
    rows = (first_ref.shape[0] + tail) * feat // (feat + ritz)
    head = rows - tail
    land = jnp.concatenate([first_ref[:head, :], second_ref[...]], axis=0)
    vec = jnp.concatenate(
        [first_ref[head:, c * rows : (c + 1) * rows] for c in range(feat // rows)], axis=0
    )
    work = [
        (k, slice(c, min(c + CHUNK, stop)))
        for k, (start, stop) in enumerate(spans)
        for c in range(start, stop, CHUNK)
    ]

    def scores(k, cols):
        return jnp.dot(land, slabs[k][:, cols], preferred_element_type=jnp.float32)

    ahead = scores(*work[0])
    for n, (k, cols) in enumerate(work):
        now, ahead = ahead, scores(*work[n + 1]) if n + 1 < len(work) else None
        affinity = jnp.exp(now * coeff).astype(jnp.bfloat16)
        term = jnp.dot(vec, affinity, preferred_element_type=jnp.float32)
        place = slice(cols.start - spans[k][0], cols.stop - spans[k][0])
        outs[k][:, place] = term if accs[k] is None else accs[k][:, cols] + term


def stage(slabs, first, second, accs, coeff, ritz, spans=None):
    feat, rows = slabs[0].shape
    land = (first.shape[0] + second.shape[0]) * feat // (feat + ritz)
    count = len(slabs)
    spans = spans or [(0, rows)] * count
    rows = spans[0][1] - spans[0][0]
    return pl.pallas_call(
        functools.partial(stage_kernel, count, coeff, ritz, accs is not None, spans),
        out_shape=[jax.ShapeDtypeStruct((ritz, rows), jnp.float32)] * count,
        compiler_params=pltpu.CompilerParams(vmem_limit_bytes=32 * MIB),
        cost_estimate=pl.CostEstimate(
            flops=2 * count * rows * land * (feat + 4 * ritz),
            bytes_accessed=2 * (count * rows + land) * feat,
            transcendentals=count * rows * land,
        ),
    )(*slabs, first, second, *(accs or []))


def add_kernel(a_ref, b_ref, out_ref):
    total = a_ref[...].astype(jnp.float32) + b_ref[...].astype(jnp.float32)
    out_ref[...] = total.astype(out_ref.dtype)


def scale_kernel(*refs, total_land):
    ritz_ref, out_ref = refs[-2:]
    factor = 1.0 / (ritz_ref[...] * math.sqrt(total_land))
    start = 0
    for a_ref, b_ref in zip(refs[0:-2:2], refs[1:-2:2]):
        stop = start + a_ref.shape[1]
        total = a_ref[...].astype(jnp.float32) + b_ref[...].astype(jnp.float32)
        out_ref[:, start:stop] = total * factor
        start = stop


def small_call(kernel, out, *args):
    return pl.pallas_call(
        kernel,
        out_shape=jax.ShapeDtypeStruct(out.shape, out.dtype),
        compiler_params=pltpu.CompilerParams(vmem_limit_bytes=8 * MIB),
    )(*args)


def local(slab, landmarks, codes, exponents, eigvec, ritz):
    n_lm, n_sl = lax.axis_size("lm"), lax.axis_size("sl")
    total_land = codes.shape[0] * n_lm * n_sl
    coeff = 1.0 / math.sqrt(slab.shape[1])
    cols = ritz.shape[0]
    rows = slab.shape[0]
    ways = n_sl.bit_length() - 2

    second = second_half(landmarks)
    first = prepare(landmarks, codes.T, exponents, eigvec.T)
    blocks = {0: [first, second]}
    for k in range(ways):
        blocks[1 << k] = [None, None]
    for turn in (0, 1):
        for k in range(ways):
            piece = (k + turn) % 2
            blocks[1 << k][piece] = chip_send(blocks[0][piece], k, n_sl)
    late_slab, _ = lax.optimization_barrier((slab, second))
    turned = jax.ShapeDtypeStruct(slab.shape[::-1], slab.dtype)
    other = small_call(transpose_kernel, turned, core_send(late_slab, n_sl))
    slab = small_call(transpose_kernel, turned, slab)
    (acc,) = stage([slab], first, second, None, coeff, cols)
    held = [blocks[1 << k][k % 2] for k in range(ways)]
    held, acc = lax.optimization_barrier((held, acc))
    for k in range(ways):
        blocks[1 << k][k % 2] = held[k]
    (other_acc,) = stage([other], first, second, None, coeff, cols)
    accs = [acc, other_acc]
    for t in range(1, 1 << ways):
        if t in blocks:
            continue
        low, high = (t & -t).bit_length() - 1, t.bit_length() - 1
        blocks[t] = [
            chip_send(blocks[t ^ (1 << high)][0], high, n_sl),
            chip_send(blocks[t ^ (1 << low)][1], low, n_sl),
        ]

    for t in range(1, (1 << ways) - 1):
        accs = stage([slab, other], *blocks[t], accs, coeff, cols)
    end = blocks[(1 << ways) - 1]
    width = rows // 2
    spans = [(0, width), (width, rows)]
    half = jax.ShapeDtypeStruct((cols, width), jnp.bfloat16)
    (early,) = stage([other], *end, accs[1:], coeff, cols, spans[:1])
    received = [core_send(early, n_sl)]
    late, mine = stage([other, slab], *end, accs[::-1], coeff, cols, spans[::-1])
    received.append(core_send(late, n_sl))
    total = small_call(add_kernel, half, mine, received[0])
    acc, total = lax.optimization_barrier((accs[0], total))
    (mine,) = stage([slab], *end, [acc], coeff, cols, spans[1:])
    totals = [total, small_call(add_kernel, half, mine, received[1])]
    turns = n_lm.bit_length() - 1
    for k in range(turns - 1):
        arrived = [lm_send(total, k, n_lm, n_sl) for total in totals]
        totals = [small_call(add_kernel, half, a, b) for a, b in zip(totals, arrived)]
    pairs = [(total, lm_send(total, turns - 1, n_lm, n_sl)) for total in totals]
    scale = functools.partial(scale_kernel, total_land=total_land)
    out = jax.ShapeDtypeStruct((cols, rows), jnp.float32)
    return small_call(scale, out, *(x for pair in pairs for x in pair), ritz[:, None]).T


def solution(mesh):
    return jax.shard_map(
        local,
        mesh=mesh,
        in_specs=(
            P("sl", None),
            P(("lm", "sl"), None),
            P(("lm", "sl"), None),
            P(("lm", "sl")),
            P(),
            P(),
        ),
        out_specs=P("sl", None),
        check_vma=False,
    )
```

```python
import functools
import math

import jax
import jax.numpy as jnp
from jax import lax
from jax.experimental import pallas as pl
from jax.experimental.pallas import tpu as pltpu
from jax.sharding import PartitionSpec as P

BLOCK = 128
SHIFT = 16
CHUNK = 512
MIB = 2**20


def core_send(value, n):
    return lax.ppermute(value, "sl", [(i, i ^ 1) for i in range(n)])


def chip_send(value, k, n):
    bits = [1 << b for b in range(1, n.bit_length() - 1)]
    return lax.ppermute(value, "sl", [(i, i ^ bits[(k + i % 2) % len(bits)]) for i in range(n)])


def lm_send(value, k, n_lm, n_sl):
    bits = [1 << b for b in range(n_lm.bit_length() - 1)]
    perm = [
        (i * n_sl + j, (i ^ bits[(k + j % 2) % len(bits)]) * n_sl + j)
        for i in range(n_lm)
        for j in range(n_sl)
    ]
    return lax.ppermute(value, ("lm", "sl"), perm)


def prepare_kernel(
    land_ref, codes_ref, exponents_ref, eig_ref, first_ref, vec_ref, codes, eig, exponents, sems
):
    rows, feat = land_ref.shape
    half = rows // 2 - SHIFT
    ritz = eig_ref.shape[0]
    pairs = [
        (codes_ref, codes),
        (eig_ref, eig),
        (exponents_ref, exponents),
        (land_ref.at[:half], first_ref.at[:half]),
    ]
    copies = [pltpu.make_async_copy(src, dst, sems.at[k]) for k, (src, dst) in enumerate(pairs)]
    for copy in copies:
        copy.start()
    for copy in copies[:3]:
        copy.wait()
    pieces = []
    for b in range(rows // BLOCK):
        scale = lax.shift_left(jnp.int32(1), exponents[b] + 15).astype(jnp.float32) * 2.0**-15
        pieces.append(codes[:, b * BLOCK : (b + 1) * BLOCK].astype(jnp.float32) * scale)
    basis = jnp.concatenate(pieces, axis=1).astype(jnp.bfloat16)
    vectors = jnp.dot(eig[...], basis, preferred_element_type=jnp.float32).astype(jnp.bfloat16)
    chunks = feat // rows
    depth = ritz // chunks
    for c in range(chunks):
        part = vectors[c * depth : (c + 1) * depth, :]
        first_ref[half:, c * rows : (c + 1) * rows] = part
        vec_ref[:, c * rows : (c + 1) * rows] = part
    for copy in copies[3:]:
        copy.wait()


def tail_kernel(land_ref, out_ref, sem):
    copy = pltpu.make_async_copy(land_ref.at[land_ref.shape[0] - out_ref.shape[0] :], out_ref, sem)
    copy.start()
    copy.wait()


def second_half(landmarks):
    rows, feat = landmarks.shape
    return pl.pallas_call(
        tail_kernel,
        out_shape=jax.ShapeDtypeStruct((rows // 2 + SHIFT, feat), jnp.bfloat16),
        in_specs=[pl.BlockSpec(memory_space=pltpu.HBM)],
        scratch_shapes=[pltpu.SemaphoreType.DMA],
        compiler_params=pltpu.CompilerParams(vmem_limit_bytes=8 * MIB),
    )(pltpu.with_memory_space_constraint(landmarks, pltpu.HBM))


def prepare(landmarks, codes_t, exponents, eig_t):
    rows, feat = landmarks.shape
    extra = eig_t.shape[0] * rows // feat
    return pl.pallas_call(
        prepare_kernel,
        out_shape=[
            jax.ShapeDtypeStruct((rows // 2 - SHIFT + extra, feat), jnp.bfloat16),
            jax.ShapeDtypeStruct((extra, feat), jnp.bfloat16),
        ],
        in_specs=[pl.BlockSpec(memory_space=pltpu.HBM)] * 4,
        scratch_shapes=[
            pltpu.VMEM(codes_t.shape, codes_t.dtype),
            pltpu.VMEM(eig_t.shape, eig_t.dtype),
            pltpu.SMEM(exponents.shape, exponents.dtype),
            pltpu.SemaphoreType.DMA((4,)),
        ],
        compiler_params=pltpu.CompilerParams(vmem_limit_bytes=8 * MIB),
    )(*(pltpu.with_memory_space_constraint(x, pltpu.HBM) for x in (landmarks, codes_t, exponents, eig_t)))


def transpose_kernel(in_ref, out_ref):
    for k in range(in_ref.shape[0] // CHUNK):
        rows = slice(k * CHUNK, (k + 1) * CHUNK)
        out_ref[:, rows] = in_ref[rows, :].T


def stage_kernel(count, coeff, ritz, has_acc, spans, *refs):
    slabs = refs[:count]
    first_ref, second_ref = refs[count : count + 2]
    accs = refs[count + 2 : 2 * count + 2] if has_acc else [None] * count
    outs = refs[-count:]
    tail, feat = second_ref.shape
    rows = (first_ref.shape[0] + tail) * feat // (feat + ritz)
    head = rows - tail
    land = second_ref[...]
    if head:
        land = jnp.concatenate([first_ref[:head, :], land], axis=0)
    vec = jnp.concatenate(
        [first_ref[head:, c * rows : (c + 1) * rows] for c in range(feat // rows)], axis=0
    )
    work = [
        (k, slice(c, min(c + CHUNK, stop)))
        for k, (start, stop) in enumerate(spans)
        for c in range(start, stop, CHUNK)
    ]

    def scores(k, cols):
        return jnp.dot(land, slabs[k][:, cols], preferred_element_type=jnp.float32)

    ahead = scores(*work[0])
    for n, (k, cols) in enumerate(work):
        now, ahead = ahead, scores(*work[n + 1]) if n + 1 < len(work) else None
        affinity = jnp.exp(now * coeff).astype(jnp.bfloat16)
        term = jnp.dot(vec, affinity, preferred_element_type=jnp.float32)
        place = slice(cols.start - spans[k][0], cols.stop - spans[k][0])
        outs[k][:, place] = term if accs[k] is None else accs[k][:, cols] + term


def stage(slabs, first, second, accs, coeff, ritz, spans=None):
    feat, rows = slabs[0].shape
    land = (first.shape[0] + second.shape[0]) * feat // (feat + ritz)
    count = len(slabs)
    spans = spans or [(0, rows)] * count
    rows = spans[0][1] - spans[0][0]
    return pl.pallas_call(
        functools.partial(stage_kernel, count, coeff, ritz, accs is not None, spans),
        out_shape=[jax.ShapeDtypeStruct((ritz, rows), jnp.float32)] * count,
        compiler_params=pltpu.CompilerParams(vmem_limit_bytes=32 * MIB),
        cost_estimate=pl.CostEstimate(
            flops=2 * count * rows * land * (feat + 4 * ritz),
            bytes_accessed=2 * (count * rows + land) * feat,
            transcendentals=count * rows * land,
        ),
    )(*slabs, first, second, *(accs or []))


def add_kernel(a_ref, b_ref, out_ref):
    total = a_ref[...].astype(jnp.float32) + b_ref[...].astype(jnp.float32)
    out_ref[...] = total.astype(out_ref.dtype)


def scale_kernel(*refs, total_land):
    ritz_ref, out_ref = refs[-2:]
    factor = 1.0 / (ritz_ref[...] * math.sqrt(total_land))
    start = 0
    for a_ref, b_ref in zip(refs[0:-2:2], refs[1:-2:2]):
        stop = start + a_ref.shape[1]
        total = a_ref[...].astype(jnp.float32) + b_ref[...].astype(jnp.float32)
        out_ref[:, start:stop] = total * factor
        start = stop


def small_call(kernel, out, *args):
    return pl.pallas_call(
        kernel,
        out_shape=jax.ShapeDtypeStruct(out.shape, out.dtype),
        compiler_params=pltpu.CompilerParams(vmem_limit_bytes=8 * MIB),
    )(*args)


def local(slab, landmarks, codes, exponents, eigvec, ritz):
    n_lm, n_sl = lax.axis_size("lm"), lax.axis_size("sl")
    total_land = codes.shape[0] * n_lm * n_sl
    coeff = 1.0 / math.sqrt(slab.shape[1])
    cols = ritz.shape[0]
    rows = slab.shape[0]
    ways = n_sl.bit_length() - 2

    whole = chip_send(landmarks, 0, n_sl)
    other = core_send(slab, n_sl)
    second = second_half(landmarks)
    first, vectors = prepare(landmarks, codes.T, exponents, eigvec.T)
    blocks = {}
    for k in range(1, ways):
        blocks[1 << k] = [None, chip_send(second, k, n_sl)]
    for k in range(1, ways):
        blocks[1 << k][0] = chip_send(first, k, n_sl)
    blocks[1] = [chip_send(vectors, 0, n_sl), whole]
    turned = jax.ShapeDtypeStruct(slab.shape[::-1], slab.dtype)
    other = small_call(transpose_kernel, turned, other)
    slab = small_call(transpose_kernel, turned, slab)
    (acc,) = stage([slab], first, second, None, coeff, cols)
    held = [blocks[1 << k] for k in range(1, ways)]
    held, acc = lax.optimization_barrier((held, acc))
    for k in range(1, ways):
        blocks[1 << k] = held[k - 1]
    (other_acc,) = stage([other], first, second, None, coeff, cols)
    accs = [acc, other_acc]
    for t in range(3, 1 << ways):
        if t in blocks:
            continue
        low, high = (t & -t).bit_length() - 1, t.bit_length() - 1
        ways_in = (high, low) if low else (0, 0)
        blocks[t] = [chip_send(blocks[t ^ (1 << k)][p], k, n_sl) for p, k in enumerate(ways_in)]

    for t in range(1, (1 << ways) - 1):
        accs = stage([slab, other], *blocks[t], accs, coeff, cols)
    end = blocks[(1 << ways) - 1]
    width = rows // 2
    spans = [(0, width), (width, rows)]
    half = jax.ShapeDtypeStruct((cols, width), jnp.bfloat16)
    (early,) = stage([other], *end, accs[1:], coeff, cols, spans[:1])
    received = [core_send(early, n_sl)]
    late, mine = stage([other, slab], *end, accs[::-1], coeff, cols, spans[::-1])
    received.append(core_send(late, n_sl))
    total = small_call(add_kernel, half, mine, received[0])
    acc, total = lax.optimization_barrier((accs[0], total))
    (mine,) = stage([slab], *end, [acc], coeff, cols, spans[1:])
    totals = [total, small_call(add_kernel, half, mine, received[1])]
    turns = n_lm.bit_length() - 1
    for k in range(turns - 1):
        arrived = [lm_send(total, k, n_lm, n_sl) for total in totals]
        totals = [small_call(add_kernel, half, a, b) for a, b in zip(totals, arrived)]
    pairs = [(total, lm_send(total, turns - 1, n_lm, n_sl)) for total in totals]
    scale = functools.partial(scale_kernel, total_land=total_land)
    out = jax.ShapeDtypeStruct((cols, rows), jnp.float32)
    return small_call(scale, out, *(x for pair in pairs for x in pair), ritz[:, None]).T


def solution(mesh):
    return jax.shard_map(
        local,
        mesh=mesh,
        in_specs=(
            P("sl", None),
            P(("lm", "sl"), None),
            P(("lm", "sl"), None),
            P(("lm", "sl")),
            P(),
            P(),
        ),
        out_specs=P("sl", None),
        check_vma=False,
    )
```

```python
import functools
import math

import jax
import jax.numpy as jnp
from jax import lax
from jax.experimental import pallas as pl
from jax.experimental.pallas import tpu as pltpu
from jax.sharding import PartitionSpec as P

BLOCK = 128
SHIFT = 16
CHUNK = 512
MIB = 2**20


def core_send(value, n):
    return lax.ppermute(value, "sl", [(i, i ^ 1) for i in range(n)])


def chip_send(value, k, n):
    bits = [1 << b for b in range(1, n.bit_length() - 1)]
    return lax.ppermute(value, "sl", [(i, i ^ bits[(k + i % 2) % len(bits)]) for i in range(n)])


def lm_send(value, k, n_lm, n_sl):
    bits = [1 << b for b in range(n_lm.bit_length() - 1)]
    perm = [
        (i * n_sl + j, (i ^ bits[(k + j % 2) % len(bits)]) * n_sl + j)
        for i in range(n_lm)
        for j in range(n_sl)
    ]
    return lax.ppermute(value, ("lm", "sl"), perm)


def prepare_kernel(
    land_ref, codes_ref, exponents_ref, eig_ref, first_ref, codes, eig, exponents, sems
):
    rows, feat = land_ref.shape
    half = rows // 2 - SHIFT
    ritz = eig_ref.shape[0]
    pairs = [
        (codes_ref, codes),
        (eig_ref, eig),
        (exponents_ref, exponents),
        (land_ref.at[:half], first_ref.at[:half]),
    ]
    copies = [pltpu.make_async_copy(src, dst, sems.at[k]) for k, (src, dst) in enumerate(pairs)]
    for copy in copies:
        copy.start()
    for copy in copies[:3]:
        copy.wait()
    pieces = []
    for b in range(rows // BLOCK):
        scale = lax.shift_left(jnp.int32(1), exponents[b] + 15).astype(jnp.float32) * 2.0**-15
        pieces.append(codes[:, b * BLOCK : (b + 1) * BLOCK].astype(jnp.float32) * scale)
    basis = jnp.concatenate(pieces, axis=1).astype(jnp.bfloat16)
    vectors = jnp.dot(eig[...], basis, preferred_element_type=jnp.float32).astype(jnp.bfloat16)
    chunks = feat // rows
    depth = ritz // chunks
    for c in range(chunks):
        first_ref[half:, c * rows : (c + 1) * rows] = vectors[c * depth : (c + 1) * depth, :]
    for copy in copies[3:]:
        copy.wait()


def tail_kernel(land_ref, out_ref, sem):
    copy = pltpu.make_async_copy(land_ref.at[land_ref.shape[0] - out_ref.shape[0] :], out_ref, sem)
    copy.start()
    copy.wait()


def second_half(landmarks):
    rows, feat = landmarks.shape
    return pl.pallas_call(
        tail_kernel,
        out_shape=jax.ShapeDtypeStruct((rows // 2 + SHIFT, feat), jnp.bfloat16),
        in_specs=[pl.BlockSpec(memory_space=pltpu.HBM)],
        scratch_shapes=[pltpu.SemaphoreType.DMA],
        compiler_params=pltpu.CompilerParams(vmem_limit_bytes=8 * MIB),
    )(pltpu.with_memory_space_constraint(landmarks, pltpu.HBM))


def prepare(landmarks, codes_t, exponents, eig_t):
    rows, feat = landmarks.shape
    extra = eig_t.shape[0] * rows // feat
    return pl.pallas_call(
        prepare_kernel,
        out_shape=jax.ShapeDtypeStruct((rows // 2 - SHIFT + extra, feat), jnp.bfloat16),
        in_specs=[pl.BlockSpec(memory_space=pltpu.HBM)] * 4,
        scratch_shapes=[
            pltpu.VMEM(codes_t.shape, codes_t.dtype),
            pltpu.VMEM(eig_t.shape, eig_t.dtype),
            pltpu.SMEM(exponents.shape, exponents.dtype),
            pltpu.SemaphoreType.DMA((4,)),
        ],
        compiler_params=pltpu.CompilerParams(vmem_limit_bytes=8 * MIB),
    )(*(pltpu.with_memory_space_constraint(x, pltpu.HBM) for x in (landmarks, codes_t, exponents, eig_t)))


def transpose_kernel(in_ref, out_ref):
    for k in range(in_ref.shape[0] // CHUNK):
        rows = slice(k * CHUNK, (k + 1) * CHUNK)
        out_ref[:, rows] = in_ref[rows, :].T


def stage_kernel(count, coeff, ritz, has_acc, spans, *refs):
    slabs = refs[:count]
    first_ref, second_ref = refs[count : count + 2]
    accs = refs[count + 2 : 2 * count + 2] if has_acc else [None] * count
    outs = refs[-count:]
    tail, feat = second_ref.shape
    rows = (first_ref.shape[0] + tail) * feat // (feat + ritz)
    head = rows - tail
    land = jnp.concatenate([first_ref[:head, :], second_ref[...]], axis=0)
    vec = jnp.concatenate(
        [first_ref[head:, c * rows : (c + 1) * rows] for c in range(feat // rows)], axis=0
    )
    work = [
        (k, slice(c, min(c + CHUNK, stop)))
        for k, (start, stop) in enumerate(spans)
        for c in range(start, stop, CHUNK)
    ]

    def scores(k, cols):
        return jnp.dot(land, slabs[k][:, cols], preferred_element_type=jnp.float32)

    ahead = scores(*work[0])
    for n, (k, cols) in enumerate(work):
        now, ahead = ahead, scores(*work[n + 1]) if n + 1 < len(work) else None
        affinity = jnp.exp(now * coeff).astype(jnp.bfloat16)
        term = jnp.dot(vec, affinity, preferred_element_type=jnp.float32)
        place = slice(cols.start - spans[k][0], cols.stop - spans[k][0])
        outs[k][:, place] = term if accs[k] is None else accs[k][:, cols] + term


def stage(slabs, first, second, accs, coeff, ritz, spans=None):
    feat, rows = slabs[0].shape
    land = (first.shape[0] + second.shape[0]) * feat // (feat + ritz)
    count = len(slabs)
    spans = spans or [(0, rows)] * count
    rows = spans[0][1] - spans[0][0]
    return pl.pallas_call(
        functools.partial(stage_kernel, count, coeff, ritz, accs is not None, spans),
        out_shape=[jax.ShapeDtypeStruct((ritz, rows), jnp.float32)] * count,
        compiler_params=pltpu.CompilerParams(vmem_limit_bytes=32 * MIB),
        cost_estimate=pl.CostEstimate(
            flops=2 * count * rows * land * (feat + 4 * ritz),
            bytes_accessed=2 * (count * rows + land) * feat,
            transcendentals=count * rows * land,
        ),
    )(*slabs, first, second, *(accs or []))


def add_kernel(a_ref, b_ref, out_ref):
    total = a_ref[...].astype(jnp.float32) + b_ref[...].astype(jnp.float32)
    out_ref[...] = total.astype(out_ref.dtype)


def split_kernel(a_ref, b_ref, *outs):
    start = 0
    for out_ref in outs:
        stop = start + out_ref.shape[1]
        out_ref[...] = (a_ref[:, start:stop] + b_ref[:, start:stop]).astype(out_ref.dtype)
        start = stop


def scale_kernel(*refs, total_land):
    ritz_ref, out_ref = refs[-2:]
    factor = 1.0 / (ritz_ref[...] * math.sqrt(total_land))
    start = 0
    for a_ref, b_ref in zip(refs[0:-2:2], refs[1:-2:2]):
        stop = start + a_ref.shape[1]
        total = a_ref[...].astype(jnp.float32) + b_ref[...].astype(jnp.float32)
        out_ref[:, start:stop] = total * factor
        start = stop


def small_call(kernel, out, *args):
    return pl.pallas_call(
        kernel,
        out_shape=jax.tree.map(lambda x: jax.ShapeDtypeStruct(x.shape, x.dtype), out),
        compiler_params=pltpu.CompilerParams(vmem_limit_bytes=8 * MIB),
    )(*args)


def local(slab, landmarks, codes, exponents, eigvec, ritz):
    n_lm, n_sl = lax.axis_size("lm"), lax.axis_size("sl")
    total_land = codes.shape[0] * n_lm * n_sl
    coeff = 1.0 / math.sqrt(slab.shape[1])
    cols = ritz.shape[0]
    rows = slab.shape[0]
    ways = n_sl.bit_length() - 2

    second = second_half(landmarks)
    first = prepare(landmarks, codes.T, exponents, eigvec.T)
    blocks = {0: [first, second]}
    for k in range(ways):
        blocks[1 << k] = [None, None]
    for turn in (0, 1):
        for k in range(ways):
            piece = (k + turn) % 2
            blocks[1 << k][piece] = chip_send(blocks[0][piece], k, n_sl)
    late_slab, _ = lax.optimization_barrier((slab, second))
    turned = jax.ShapeDtypeStruct(slab.shape[::-1], slab.dtype)
    other = small_call(transpose_kernel, turned, core_send(late_slab, n_sl))
    slab = small_call(transpose_kernel, turned, slab)
    (acc,) = stage([slab], first, second, None, coeff, cols)
    held = [blocks[1 << k][k % 2] for k in range(ways)]
    held, acc = lax.optimization_barrier((held, acc))
    for k in range(ways):
        blocks[1 << k][k % 2] = held[k]
    (other_acc,) = stage([other], first, second, None, coeff, cols)
    accs = [acc, other_acc]
    for t in range(1, 1 << ways):
        if t in blocks:
            continue
        low, high = (t & -t).bit_length() - 1, t.bit_length() - 1
        blocks[t] = [
            chip_send(blocks[t ^ (1 << high)][0], high, n_sl),
            chip_send(blocks[t ^ (1 << low)][1], low, n_sl),
        ]

    for t in range(1, (1 << ways) - 1):
        accs = stage([slab, other], *blocks[t], accs, coeff, cols)
    end = blocks[(1 << ways) - 1]
    (theirs,) = stage([other], *end, accs[1:], coeff, cols)
    received = core_send(theirs, n_sl)
    (mine,) = stage([slab], *end, accs[:1], coeff, cols)
    half = jax.ShapeDtypeStruct((cols, rows // 2), jnp.bfloat16)
    totals = small_call(split_kernel, [half] * 2, mine, received)
    turns = n_lm.bit_length() - 1
    for k in range(turns - 1):
        arrived = [lm_send(total, k, n_lm, n_sl) for total in totals]
        totals = [small_call(add_kernel, half, a, b) for a, b in zip(totals, arrived)]
    pairs = [(total, lm_send(total, turns - 1, n_lm, n_sl)) for total in totals]
    scale = functools.partial(scale_kernel, total_land=total_land)
    out = jax.ShapeDtypeStruct((cols, rows), jnp.float32)
    return small_call(scale, out, *(x for pair in pairs for x in pair), ritz[:, None]).T


def solution(mesh):
    return jax.shard_map(
        local,
        mesh=mesh,
        in_specs=(
            P("sl", None),
            P(("lm", "sl"), None),
            P(("lm", "sl"), None),
            P(("lm", "sl")),
            P(),
            P(),
        ),
        out_specs=P("sl", None),
        check_vma=False,
    )
```

```python
import functools
import math

import jax
import jax.numpy as jnp
from jax import lax
from jax.experimental import pallas as pl
from jax.experimental.pallas import tpu as pltpu
from jax.sharding import PartitionSpec as P

BLOCK = 128
SHIFT = 16
CHUNK = 512
MIB = 2**20


def core_send(value, n):
    return lax.ppermute(value, "sl", [(i, i ^ 1) for i in range(n)])


def chip_send(value, k, n):
    bits = [1 << b for b in range(1, n.bit_length() - 1)]
    return lax.ppermute(value, "sl", [(i, i ^ bits[(k + i % 2) % len(bits)]) for i in range(n)])


def lm_send(value, k, n_lm, n_sl):
    bits = [1 << b for b in range(n_lm.bit_length() - 1)]
    perm = [
        (i * n_sl + j, (i ^ bits[(k + j % 2) % len(bits)]) * n_sl + j)
        for i in range(n_lm)
        for j in range(n_sl)
    ]
    return lax.ppermute(value, ("lm", "sl"), perm)


def prepare_kernel(
    land_ref, codes_ref, exponents_ref, eig_ref, first_ref, codes, eig, exponents, sems
):
    rows, feat = land_ref.shape
    half = rows // 2 - SHIFT
    ritz = eig_ref.shape[0]
    pairs = [
        (codes_ref, codes),
        (eig_ref, eig),
        (exponents_ref, exponents),
        (land_ref.at[:half], first_ref.at[:half]),
    ]
    copies = [pltpu.make_async_copy(src, dst, sems.at[k]) for k, (src, dst) in enumerate(pairs)]
    for copy in copies:
        copy.start()
    for copy in copies[:3]:
        copy.wait()
    pieces = []
    for b in range(rows // BLOCK):
        scale = lax.shift_left(jnp.int32(1), exponents[b] + 15).astype(jnp.float32) * 2.0**-15
        pieces.append(codes[:, b * BLOCK : (b + 1) * BLOCK].astype(jnp.float32) * scale)
    basis = jnp.concatenate(pieces, axis=1).astype(jnp.bfloat16)
    vectors = jnp.dot(eig[...], basis, preferred_element_type=jnp.float32).astype(jnp.bfloat16)
    chunks = feat // rows
    depth = ritz // chunks
    for c in range(chunks):
        first_ref[half:, c * rows : (c + 1) * rows] = vectors[c * depth : (c + 1) * depth, :]
    for copy in copies[3:]:
        copy.wait()


def tail_kernel(land_ref, out_ref, sem):
    copy = pltpu.make_async_copy(land_ref.at[land_ref.shape[0] - out_ref.shape[0] :], out_ref, sem)
    copy.start()
    copy.wait()


def second_half(landmarks):
    rows, feat = landmarks.shape
    return pl.pallas_call(
        tail_kernel,
        out_shape=jax.ShapeDtypeStruct((rows // 2 + SHIFT, feat), jnp.bfloat16),
        in_specs=[pl.BlockSpec(memory_space=pltpu.HBM)],
        scratch_shapes=[pltpu.SemaphoreType.DMA],
        compiler_params=pltpu.CompilerParams(vmem_limit_bytes=8 * MIB),
    )(pltpu.with_memory_space_constraint(landmarks, pltpu.HBM))


def prepare(landmarks, codes_t, exponents, eig_t):
    rows, feat = landmarks.shape
    extra = eig_t.shape[0] * rows // feat
    return pl.pallas_call(
        prepare_kernel,
        out_shape=jax.ShapeDtypeStruct((rows // 2 - SHIFT + extra, feat), jnp.bfloat16),
        in_specs=[pl.BlockSpec(memory_space=pltpu.HBM)] * 4,
        scratch_shapes=[
            pltpu.VMEM(codes_t.shape, codes_t.dtype),
            pltpu.VMEM(eig_t.shape, eig_t.dtype),
            pltpu.SMEM(exponents.shape, exponents.dtype),
            pltpu.SemaphoreType.DMA((4,)),
        ],
        compiler_params=pltpu.CompilerParams(vmem_limit_bytes=8 * MIB),
    )(*(pltpu.with_memory_space_constraint(x, pltpu.HBM) for x in (landmarks, codes_t, exponents, eig_t)))


def transpose_kernel(in_ref, out_ref):
    for k in range(in_ref.shape[0] // CHUNK):
        rows = slice(k * CHUNK, (k + 1) * CHUNK)
        out_ref[:, rows] = in_ref[rows, :].T


def stage_kernel(count, coeff, ritz, has_acc, cuts, *refs):
    slabs = refs[:count]
    first_ref, second_ref = refs[count : count + 2]
    accs = refs[count + 2 : 2 * count + 2] if has_acc else [None] * count
    outs = refs[-count * len(cuts) :]
    tail, feat = second_ref.shape
    rows = (first_ref.shape[0] + tail) * feat // (feat + ritz)
    head = rows - tail
    land = jnp.concatenate([first_ref[:head, :], second_ref[...]], axis=0)
    vec = jnp.concatenate(
        [first_ref[head:, c * rows : (c + 1) * rows] for c in range(feat // rows)], axis=0
    )
    work = [
        (k, c, min(c + CHUNK, slabs[k].shape[1]))
        for k in range(count)
        for c in range(0, slabs[k].shape[1], CHUNK)
    ]

    def scores(k, lo, hi):
        return jnp.dot(land, slabs[k][:, lo:hi], preferred_element_type=jnp.float32)

    ahead = scores(*work[0])
    for n, (k, lo, hi) in enumerate(work):
        now, ahead = ahead, scores(*work[n + 1]) if n + 1 < len(work) else None
        affinity = jnp.exp(now * coeff).astype(jnp.bfloat16)
        term = jnp.dot(vec, affinity, preferred_element_type=jnp.float32)
        if has_acc:
            term = accs[k][:, lo:hi] + term
        for p, (start, stop) in enumerate(cuts):
            a, b = max(lo, start), min(hi, stop)
            if a < b:
                outs[k * len(cuts) + p][:, a - start : b - start] = term[:, a - lo : b - lo]


def stage(slabs, first, second, accs, coeff, ritz, cuts=None):
    feat, rows = slabs[0].shape
    land = (first.shape[0] + second.shape[0]) * feat // (feat + ritz)
    count = len(slabs)
    cuts = cuts or [(0, rows)]
    pieces = [jax.ShapeDtypeStruct((ritz, stop - start), jnp.float32) for start, stop in cuts]
    return pl.pallas_call(
        functools.partial(stage_kernel, count, coeff, ritz, accs is not None, cuts),
        out_shape=pieces * count,
        compiler_params=pltpu.CompilerParams(vmem_limit_bytes=32 * MIB),
        cost_estimate=pl.CostEstimate(
            flops=2 * count * rows * land * (feat + 4 * ritz),
            bytes_accessed=2 * (count * rows + land) * feat,
            transcendentals=count * rows * land,
        ),
    )(*slabs, first, second, *(accs or []))


def add_kernel(a_ref, b_ref, out_ref):
    total = a_ref[...].astype(jnp.float32) + b_ref[...].astype(jnp.float32)
    out_ref[...] = total.astype(out_ref.dtype)


def add_part_kernel(a_ref, b_ref, out_ref, *, start):
    stop = start + out_ref.shape[1]
    out_ref[...] = (a_ref[:, start:stop] + b_ref[...]).astype(out_ref.dtype)


def scale_kernel(*refs, total_land):
    ritz_ref, out_ref = refs[-2:]
    factor = 1.0 / (ritz_ref[...] * math.sqrt(total_land))
    start = 0
    for a_ref, b_ref in zip(refs[0:-2:2], refs[1:-2:2]):
        stop = start + a_ref.shape[1]
        total = a_ref[...].astype(jnp.float32) + b_ref[...].astype(jnp.float32)
        out_ref[:, start:stop] = total * factor
        start = stop


def small_call(kernel, out, *args):
    return pl.pallas_call(
        kernel,
        out_shape=jax.ShapeDtypeStruct(out.shape, out.dtype),
        compiler_params=pltpu.CompilerParams(vmem_limit_bytes=8 * MIB),
    )(*args)


def local(slab, landmarks, codes, exponents, eigvec, ritz):
    n_lm, n_sl = lax.axis_size("lm"), lax.axis_size("sl")
    total_land = codes.shape[0] * n_lm * n_sl
    coeff = 1.0 / math.sqrt(slab.shape[1])
    cols = ritz.shape[0]
    rows = slab.shape[0]
    ways = n_sl.bit_length() - 2

    second = second_half(landmarks)
    first = prepare(landmarks, codes.T, exponents, eigvec.T)
    blocks = {0: [first, second]}
    for k in range(ways):
        blocks[1 << k] = [None, None]
    for turn in (0, 1):
        for k in range(ways):
            piece = (k + turn) % 2
            blocks[1 << k][piece] = chip_send(blocks[0][piece], k, n_sl)
    late_slab, _ = lax.optimization_barrier((slab, second))
    turned = jax.ShapeDtypeStruct(slab.shape[::-1], slab.dtype)
    other = small_call(transpose_kernel, turned, core_send(late_slab, n_sl))
    slab = small_call(transpose_kernel, turned, slab)
    (acc,) = stage([slab], first, second, None, coeff, cols)
    held = [blocks[1 << k][k % 2] for k in range(ways)]
    held, acc = lax.optimization_barrier((held, acc))
    for k in range(ways):
        blocks[1 << k][k % 2] = held[k]
    (other_acc,) = stage([other], first, second, None, coeff, cols)
    accs = [acc, other_acc]
    for t in range(1, 1 << ways):
        if t in blocks:
            continue
        low, high = (t & -t).bit_length() - 1, t.bit_length() - 1
        blocks[t] = [
            chip_send(blocks[t ^ (1 << high)][0], high, n_sl),
            chip_send(blocks[t ^ (1 << low)][1], low, n_sl),
        ]

    for t in range(1, (1 << ways) - 1):
        accs = stage([slab, other], *blocks[t], accs, coeff, cols)
    end = blocks[(1 << ways) - 1]
    cuts = [(0, rows * 5 // 8), (rows * 5 // 8, rows)]
    theirs = stage([other], *end, accs[1:], coeff, cols, cuts)
    received = [core_send(piece, n_sl) for piece in theirs]
    (mine,) = stage([slab], *end, accs[:1], coeff, cols)
    pieces = [jax.ShapeDtypeStruct((cols, stop - start), jnp.bfloat16) for start, stop in cuts]
    totals = [
        small_call(functools.partial(add_part_kernel, start=start), piece, mine, part)
        for (start, _), piece, part in zip(cuts, pieces, received)
    ]
    turns = n_lm.bit_length() - 1
    for k in range(turns - 1):
        arrived = [lm_send(total, k, n_lm, n_sl) for total in totals]
        totals = [small_call(add_kernel, p, a, b) for p, a, b in zip(pieces, totals, arrived)]
    pairs = [(total, lm_send(total, turns - 1, n_lm, n_sl)) for total in totals]
    scale = functools.partial(scale_kernel, total_land=total_land)
    out = jax.ShapeDtypeStruct((cols, rows), jnp.float32)
    return small_call(scale, out, *(x for pair in pairs for x in pair), ritz[:, None]).T


def solution(mesh):
    return jax.shard_map(
        local,
        mesh=mesh,
        in_specs=(
            P("sl", None),
            P(("lm", "sl"), None),
            P(("lm", "sl"), None),
            P(("lm", "sl")),
            P(),
            P(),
        ),
        out_specs=P("sl", None),
        check_vma=False,
    )
```

```python
import functools
import math

import jax
import jax.numpy as jnp
from jax import lax
from jax.experimental import pallas as pl
from jax.experimental.pallas import tpu as pltpu
from jax.sharding import PartitionSpec as P

BLOCK = 128
SHIFT = 16
CHUNK = 512
MIB = 2**20


def core_send(value, n):
    return lax.ppermute(value, "sl", [(i, i ^ 1) for i in range(n)])


def chip_send(value, k, n):
    bits = [1 << b for b in range(1, n.bit_length() - 1)]
    return lax.ppermute(value, "sl", [(i, i ^ bits[(k + i % 2) % len(bits)]) for i in range(n)])


def lm_send(value, k, n_lm, n_sl):
    bits = [1 << b for b in range(n_lm.bit_length() - 1)]
    perm = [
        (i * n_sl + j, (i ^ bits[(k + 1 - j % 2) % len(bits)]) * n_sl + j)
        for i in range(n_lm)
        for j in range(n_sl)
    ]
    return lax.ppermute(value, ("lm", "sl"), perm)


def prepare_kernel(
    land_ref, codes_ref, exponents_ref, eig_ref, first_ref, codes, eig, exponents, sems
):
    rows, feat = land_ref.shape
    half = rows // 2 - SHIFT
    ritz = eig_ref.shape[0]
    pairs = [
        (codes_ref, codes),
        (eig_ref, eig),
        (exponents_ref, exponents),
        (land_ref.at[:half], first_ref.at[:half]),
    ]
    copies = [pltpu.make_async_copy(src, dst, sems.at[k]) for k, (src, dst) in enumerate(pairs)]
    for copy in copies:
        copy.start()
    for copy in copies[:3]:
        copy.wait()
    pieces = []
    for b in range(rows // BLOCK):
        scale = lax.shift_left(jnp.int32(1), exponents[b] + 15).astype(jnp.float32) * 2.0**-15
        pieces.append(codes[:, b * BLOCK : (b + 1) * BLOCK].astype(jnp.float32) * scale)
    basis = jnp.concatenate(pieces, axis=1).astype(jnp.bfloat16)
    vectors = jnp.dot(eig[...], basis, preferred_element_type=jnp.float32).astype(jnp.bfloat16)
    chunks = feat // rows
    depth = ritz // chunks
    for c in range(chunks):
        first_ref[half:, c * rows : (c + 1) * rows] = vectors[c * depth : (c + 1) * depth, :]
    for copy in copies[3:]:
        copy.wait()


def tail_kernel(land_ref, out_ref, sem):
    copy = pltpu.make_async_copy(land_ref.at[land_ref.shape[0] - out_ref.shape[0] :], out_ref, sem)
    copy.start()
    copy.wait()


def second_half(landmarks):
    rows, feat = landmarks.shape
    return pl.pallas_call(
        tail_kernel,
        out_shape=jax.ShapeDtypeStruct((rows // 2 + SHIFT, feat), jnp.bfloat16),
        in_specs=[pl.BlockSpec(memory_space=pltpu.HBM)],
        scratch_shapes=[pltpu.SemaphoreType.DMA],
        compiler_params=pltpu.CompilerParams(vmem_limit_bytes=8 * MIB),
    )(pltpu.with_memory_space_constraint(landmarks, pltpu.HBM))


def prepare(landmarks, codes_t, exponents, eig_t):
    rows, feat = landmarks.shape
    extra = eig_t.shape[0] * rows // feat
    return pl.pallas_call(
        prepare_kernel,
        out_shape=jax.ShapeDtypeStruct((rows // 2 - SHIFT + extra, feat), jnp.bfloat16),
        in_specs=[pl.BlockSpec(memory_space=pltpu.HBM)] * 4,
        scratch_shapes=[
            pltpu.VMEM(codes_t.shape, codes_t.dtype),
            pltpu.VMEM(eig_t.shape, eig_t.dtype),
            pltpu.SMEM(exponents.shape, exponents.dtype),
            pltpu.SemaphoreType.DMA((4,)),
        ],
        compiler_params=pltpu.CompilerParams(vmem_limit_bytes=8 * MIB),
    )(*(pltpu.with_memory_space_constraint(x, pltpu.HBM) for x in (landmarks, codes_t, exponents, eig_t)))


def transpose_kernel(in_ref, out_ref):
    for k in range(in_ref.shape[0] // CHUNK):
        rows = slice(k * CHUNK, (k + 1) * CHUNK)
        out_ref[:, rows] = in_ref[rows, :].T


def stage_kernel(count, coeff, ritz, has_acc, spans, *refs):
    slabs = refs[:count]
    first_ref, second_ref = refs[count : count + 2]
    accs = refs[count + 2 : 2 * count + 2] if has_acc else [None] * count
    outs = refs[-count:]
    tail, feat = second_ref.shape
    rows = (first_ref.shape[0] + tail) * feat // (feat + ritz)
    head = rows - tail
    land = jnp.concatenate([first_ref[:head, :], second_ref[...]], axis=0)
    vec = jnp.concatenate(
        [first_ref[head:, c * rows : (c + 1) * rows] for c in range(feat // rows)], axis=0
    )
    work = [
        (k, slice(c, min(c + CHUNK, stop)))
        for k, (start, stop) in enumerate(spans)
        for c in range(start, stop, CHUNK)
    ]

    def scores(k, cols):
        return jnp.dot(land, slabs[k][:, cols], preferred_element_type=jnp.float32)

    ahead = scores(*work[0])
    for n, (k, cols) in enumerate(work):
        now, ahead = ahead, scores(*work[n + 1]) if n + 1 < len(work) else None
        affinity = jnp.exp(now * coeff).astype(jnp.bfloat16)
        term = jnp.dot(vec, affinity, preferred_element_type=jnp.float32)
        place = slice(cols.start - spans[k][0], cols.stop - spans[k][0])
        outs[k][:, place] = term if accs[k] is None else accs[k][:, cols] + term


def stage(slabs, first, second, accs, coeff, ritz, spans=None):
    feat, rows = slabs[0].shape
    land = (first.shape[0] + second.shape[0]) * feat // (feat + ritz)
    count = len(slabs)
    spans = spans or [(0, rows)] * count
    rows = spans[0][1] - spans[0][0]
    return pl.pallas_call(
        functools.partial(stage_kernel, count, coeff, ritz, accs is not None, spans),
        out_shape=[jax.ShapeDtypeStruct((ritz, rows), jnp.float32)] * count,
        compiler_params=pltpu.CompilerParams(vmem_limit_bytes=32 * MIB),
        cost_estimate=pl.CostEstimate(
            flops=2 * count * rows * land * (feat + 4 * ritz),
            bytes_accessed=2 * (count * rows + land) * feat,
            transcendentals=count * rows * land,
        ),
    )(*slabs, first, second, *(accs or []))


def add_kernel(a_ref, b_ref, out_ref):
    total = a_ref[...].astype(jnp.float32) + b_ref[...].astype(jnp.float32)
    out_ref[...] = total.astype(out_ref.dtype)


def scale_kernel(*refs, total_land):
    ritz_ref, out_ref = refs[-2:]
    factor = 1.0 / (ritz_ref[...] * math.sqrt(total_land))
    start = 0
    for a_ref, b_ref in zip(refs[0:-2:2], refs[1:-2:2]):
        stop = start + a_ref.shape[1]
        total = a_ref[...].astype(jnp.float32) + b_ref[...].astype(jnp.float32)
        out_ref[:, start:stop] = total * factor
        start = stop


def small_call(kernel, out, *args):
    return pl.pallas_call(
        kernel,
        out_shape=jax.ShapeDtypeStruct(out.shape, out.dtype),
        compiler_params=pltpu.CompilerParams(vmem_limit_bytes=8 * MIB),
    )(*args)


def local(slab, landmarks, codes, exponents, eigvec, ritz):
    n_lm, n_sl = lax.axis_size("lm"), lax.axis_size("sl")
    total_land = codes.shape[0] * n_lm * n_sl
    coeff = 1.0 / math.sqrt(slab.shape[1])
    cols = ritz.shape[0]
    rows = slab.shape[0]
    ways = n_sl.bit_length() - 2

    second = second_half(landmarks)
    first = prepare(landmarks, codes.T, exponents, eigvec.T)
    blocks = {0: [first, second]}
    for k in range(ways):
        blocks[1 << k] = [None, None]
    for turn in (0, 1):
        for k in range(ways):
            piece = (k + turn) % 2
            blocks[1 << k][piece] = chip_send(blocks[0][piece], k, n_sl)
    late_slab, _ = lax.optimization_barrier((slab, second))
    turned = jax.ShapeDtypeStruct(slab.shape[::-1], slab.dtype)
    other = small_call(transpose_kernel, turned, core_send(late_slab, n_sl))
    slab = small_call(transpose_kernel, turned, slab)
    (acc,) = stage([slab], first, second, None, coeff, cols)
    held = [blocks[1 << k][k % 2] for k in range(ways)]
    held, acc = lax.optimization_barrier((held, acc))
    for k in range(ways):
        blocks[1 << k][k % 2] = held[k]
    (other_acc,) = stage([other], first, second, None, coeff, cols)
    accs = [acc, other_acc]
    for t in range(1, 1 << ways):
        if t in blocks:
            continue
        low, high = (t & -t).bit_length() - 1, t.bit_length() - 1
        blocks[t] = [
            chip_send(blocks[t ^ (1 << high)][0], high, n_sl),
            chip_send(blocks[t ^ (1 << low)][1], low, n_sl),
        ]

    for t in range(1, (1 << ways) - 1):
        accs = stage([slab, other], *blocks[t], accs, coeff, cols)
    end = blocks[(1 << ways) - 1]
    width = rows // 2
    spans = [(0, width), (width, rows)]
    half = jax.ShapeDtypeStruct((cols, width), jnp.bfloat16)
    (early,) = stage([other], *end, accs[1:], coeff, cols, spans[:1])
    received = [core_send(early, n_sl)]
    late, mine = stage([other, slab], *end, accs[::-1], coeff, cols, spans[::-1])
    received.append(core_send(late, n_sl))
    total = small_call(add_kernel, half, mine, received[0])
    acc, total = lax.optimization_barrier((accs[0], total))
    (mine,) = stage([slab], *end, [acc], coeff, cols, spans[1:])
    totals = [total, small_call(add_kernel, half, mine, received[1])]
    turns = n_lm.bit_length() - 1
    for k in range(turns - 1):
        arrived = [lm_send(total, k, n_lm, n_sl) for total in totals]
        totals = [small_call(add_kernel, half, a, b) for a, b in zip(totals, arrived)]
    pairs = [(total, lm_send(total, turns - 1, n_lm, n_sl)) for total in totals]
    scale = functools.partial(scale_kernel, total_land=total_land)
    out = jax.ShapeDtypeStruct((cols, rows), jnp.float32)
    return small_call(scale, out, *(x for pair in pairs for x in pair), ritz[:, None]).T


def solution(mesh):
    return jax.shard_map(
        local,
        mesh=mesh,
        in_specs=(
            P("sl", None),
            P(("lm", "sl"), None),
            P(("lm", "sl"), None),
            P(("lm", "sl")),
            P(),
            P(),
        ),
        out_specs=P("sl", None),
        check_vma=False,
    )
```

```python
import functools
import math

import jax
import jax.numpy as jnp
from jax import lax
from jax.experimental import pallas as pl
from jax.experimental.pallas import tpu as pltpu
from jax.sharding import PartitionSpec as P

BLOCK = 128
SHIFT = 16
CHUNK = 512
MIB = 2**20


def core_send(value, n):
    return lax.ppermute(value, "sl", [(i, i ^ 1) for i in range(n)])


def chip_send(value, k, n):
    bits = [1 << b for b in range(1, n.bit_length() - 1)]
    return lax.ppermute(value, "sl", [(i, i ^ bits[(k + i % 2) % len(bits)]) for i in range(n)])


def lm_send(value, k, n_lm, n_sl):
    bits = [1 << b for b in range(n_lm.bit_length() - 1)]
    perm = [
        (i * n_sl + j, (i ^ bits[(k + j % 2) % len(bits)]) * n_sl + j)
        for i in range(n_lm)
        for j in range(n_sl)
    ]
    return lax.ppermute(value, ("lm", "sl"), perm)


def prepare_kernel(
    land_ref, codes_ref, exponents_ref, eig_ref, first_ref, codes, eig, exponents, sems
):
    rows, feat = land_ref.shape
    half = rows // 2 - SHIFT
    ritz = eig_ref.shape[0]
    pairs = [
        (codes_ref, codes),
        (eig_ref, eig),
        (exponents_ref, exponents),
        (land_ref.at[:half], first_ref.at[:half]),
    ]
    copies = [pltpu.make_async_copy(src, dst, sems.at[k]) for k, (src, dst) in enumerate(pairs)]
    for copy in copies:
        copy.start()
    for copy in copies[:3]:
        copy.wait()
    pieces = []
    for b in range(rows // BLOCK):
        scale = lax.shift_left(jnp.int32(1), exponents[b] + 15).astype(jnp.float32) * 2.0**-15
        pieces.append(codes[:, b * BLOCK : (b + 1) * BLOCK].astype(jnp.float32) * scale)
    basis = jnp.concatenate(pieces, axis=1).astype(jnp.bfloat16)
    vectors = jnp.dot(eig[...], basis, preferred_element_type=jnp.float32).astype(jnp.bfloat16)
    chunks = feat // rows
    depth = ritz // chunks
    for c in range(chunks):
        first_ref[half:, c * rows : (c + 1) * rows] = vectors[c * depth : (c + 1) * depth, :]
    for copy in copies[3:]:
        copy.wait()


def tail_kernel(land_ref, out_ref, sem):
    copy = pltpu.make_async_copy(land_ref.at[land_ref.shape[0] - out_ref.shape[0] :], out_ref, sem)
    copy.start()
    copy.wait()


def second_half(landmarks):
    rows, feat = landmarks.shape
    return pl.pallas_call(
        tail_kernel,
        out_shape=jax.ShapeDtypeStruct((rows // 2 + SHIFT, feat), jnp.bfloat16),
        in_specs=[pl.BlockSpec(memory_space=pltpu.HBM)],
        scratch_shapes=[pltpu.SemaphoreType.DMA],
        compiler_params=pltpu.CompilerParams(vmem_limit_bytes=8 * MIB),
    )(pltpu.with_memory_space_constraint(landmarks, pltpu.HBM))


def prepare(landmarks, codes_t, exponents, eig_t):
    rows, feat = landmarks.shape
    extra = eig_t.shape[0] * rows // feat
    return pl.pallas_call(
        prepare_kernel,
        out_shape=jax.ShapeDtypeStruct((rows // 2 - SHIFT + extra, feat), jnp.bfloat16),
        in_specs=[pl.BlockSpec(memory_space=pltpu.HBM)] * 4,
        scratch_shapes=[
            pltpu.VMEM(codes_t.shape, codes_t.dtype),
            pltpu.VMEM(eig_t.shape, eig_t.dtype),
            pltpu.SMEM(exponents.shape, exponents.dtype),
            pltpu.SemaphoreType.DMA((4,)),
        ],
        compiler_params=pltpu.CompilerParams(vmem_limit_bytes=8 * MIB),
    )(*(pltpu.with_memory_space_constraint(x, pltpu.HBM) for x in (landmarks, codes_t, exponents, eig_t)))


def transpose_kernel(in_ref, out_ref):
    for k in range(in_ref.shape[0] // CHUNK):
        rows = slice(k * CHUNK, (k + 1) * CHUNK)
        out_ref[:, rows] = in_ref[rows, :].T


def stage_kernel(count, coeff, ritz, has_acc, spans, *refs):
    slabs = refs[:count]
    first_ref, second_ref = refs[count : count + 2]
    accs = refs[count + 2 : 2 * count + 2] if has_acc else [None] * count
    outs = refs[-count:]
    tail, feat = second_ref.shape
    rows = (first_ref.shape[0] + tail) * feat // (feat + ritz)
    head = rows - tail
    vec = jnp.concatenate(
        [first_ref[head:, c * rows : (c + 1) * rows] for c in range(feat // rows)], axis=0
    )
    work = [
        (k, slice(c, min(c + CHUNK, stop)))
        for k, (start, stop) in enumerate(spans)
        for c in range(start, stop, CHUNK)
    ]

    def scores(k, cols):
        weights = slabs[k][:, cols]
        return [
            jnp.dot(land, weights, preferred_element_type=jnp.float32)
            for land in (second_ref[...], first_ref[:head, :])
        ]

    ahead = scores(*work[0])
    for n, (k, cols) in enumerate(work):
        now, ahead = ahead, scores(*work[n + 1]) if n + 1 < len(work) else None
        late, early = [jnp.exp(part * coeff).astype(jnp.bfloat16) for part in now]
        affinity = jnp.concatenate([early, late], axis=0)
        term = jnp.dot(vec, affinity, preferred_element_type=jnp.float32)
        place = slice(cols.start - spans[k][0], cols.stop - spans[k][0])
        outs[k][:, place] = term if accs[k] is None else accs[k][:, cols] + term


def stage(slabs, first, second, accs, coeff, ritz, spans=None):
    feat, rows = slabs[0].shape
    land = (first.shape[0] + second.shape[0]) * feat // (feat + ritz)
    count = len(slabs)
    spans = spans or [(0, rows)] * count
    rows = spans[0][1] - spans[0][0]
    return pl.pallas_call(
        functools.partial(stage_kernel, count, coeff, ritz, accs is not None, spans),
        out_shape=[jax.ShapeDtypeStruct((ritz, rows), jnp.float32)] * count,
        compiler_params=pltpu.CompilerParams(vmem_limit_bytes=32 * MIB),
        cost_estimate=pl.CostEstimate(
            flops=2 * count * rows * land * (feat + 4 * ritz),
            bytes_accessed=2 * (count * rows + land) * feat,
            transcendentals=count * rows * land,
        ),
    )(*slabs, first, second, *(accs or []))


def add_kernel(a_ref, b_ref, out_ref):
    total = a_ref[...].astype(jnp.float32) + b_ref[...].astype(jnp.float32)
    out_ref[...] = total.astype(out_ref.dtype)


def scale_kernel(*refs, total_land):
    ritz_ref, out_ref = refs[-2:]
    factor = 1.0 / (ritz_ref[...] * math.sqrt(total_land))
    start = 0
    for a_ref, b_ref in zip(refs[0:-2:2], refs[1:-2:2]):
        stop = start + a_ref.shape[1]
        total = a_ref[...].astype(jnp.float32) + b_ref[...].astype(jnp.float32)
        out_ref[:, start:stop] = total * factor
        start = stop


def small_call(kernel, out, *args):
    return pl.pallas_call(
        kernel,
        out_shape=jax.ShapeDtypeStruct(out.shape, out.dtype),
        compiler_params=pltpu.CompilerParams(vmem_limit_bytes=8 * MIB),
    )(*args)


def local(slab, landmarks, codes, exponents, eigvec, ritz):
    n_lm, n_sl = lax.axis_size("lm"), lax.axis_size("sl")
    total_land = codes.shape[0] * n_lm * n_sl
    coeff = 1.0 / math.sqrt(slab.shape[1])
    cols = ritz.shape[0]
    rows = slab.shape[0]
    ways = n_sl.bit_length() - 2

    second = second_half(landmarks)
    first = prepare(landmarks, codes.T, exponents, eigvec.T)
    blocks = {0: [first, second]}
    for k in range(ways):
        blocks[1 << k] = [None, None]
    for turn in (0, 1):
        for k in range(ways):
            piece = (k + turn) % 2
            blocks[1 << k][piece] = chip_send(blocks[0][piece], k, n_sl)
    late_slab, _ = lax.optimization_barrier((slab, second))
    turned = jax.ShapeDtypeStruct(slab.shape[::-1], slab.dtype)
    other = small_call(transpose_kernel, turned, core_send(late_slab, n_sl))
    slab = small_call(transpose_kernel, turned, slab)
    (acc,) = stage([slab], first, second, None, coeff, cols)
    held = [blocks[1 << k][k % 2] for k in range(ways)]
    held, acc = lax.optimization_barrier((held, acc))
    for k in range(ways):
        blocks[1 << k][k % 2] = held[k]
    (other_acc,) = stage([other], first, second, None, coeff, cols)
    accs = [acc, other_acc]
    for t in range(1, 1 << ways):
        if t in blocks:
            continue
        low, high = (t & -t).bit_length() - 1, t.bit_length() - 1
        blocks[t] = [
            chip_send(blocks[t ^ (1 << high)][0], high, n_sl),
            chip_send(blocks[t ^ (1 << low)][1], low, n_sl),
        ]

    for t in range(1, (1 << ways) - 1):
        accs = stage([slab, other], *blocks[t], accs, coeff, cols)
    end = blocks[(1 << ways) - 1]
    width = rows // 2
    spans = [(0, width), (width, rows)]
    half = jax.ShapeDtypeStruct((cols, width), jnp.bfloat16)
    (early,) = stage([other], *end, accs[1:], coeff, cols, spans[:1])
    received = [core_send(early, n_sl)]
    late, mine = stage([other, slab], *end, accs[::-1], coeff, cols, spans[::-1])
    received.append(core_send(late, n_sl))
    total = small_call(add_kernel, half, mine, received[0])
    acc, total = lax.optimization_barrier((accs[0], total))
    (mine,) = stage([slab], *end, [acc], coeff, cols, spans[1:])
    totals = [total, small_call(add_kernel, half, mine, received[1])]
    turns = n_lm.bit_length() - 1
    for k in range(turns - 1):
        arrived = [lm_send(total, k, n_lm, n_sl) for total in totals]
        totals = [small_call(add_kernel, half, a, b) for a, b in zip(totals, arrived)]
    pairs = [(total, lm_send(total, turns - 1, n_lm, n_sl)) for total in totals]
    scale = functools.partial(scale_kernel, total_land=total_land)
    out = jax.ShapeDtypeStruct((cols, rows), jnp.float32)
    return small_call(scale, out, *(x for pair in pairs for x in pair), ritz[:, None]).T


def solution(mesh):
    return jax.shard_map(
        local,
        mesh=mesh,
        in_specs=(
            P("sl", None),
            P(("lm", "sl"), None),
            P(("lm", "sl"), None),
            P(("lm", "sl")),
            P(),
            P(),
        ),
        out_specs=P("sl", None),
        check_vma=False,
    )
```

```python
import functools
import math

import jax
import jax.numpy as jnp
from jax import lax
from jax.experimental import pallas as pl
from jax.experimental.pallas import tpu as pltpu
from jax.sharding import PartitionSpec as P

BLOCK = 128
SHIFT = 16
CHUNK = 512
MIB = 2**20


def core_send(value, n):
    return lax.ppermute(value, "sl", [(i, i ^ 1) for i in range(n)])


def chip_send(value, k, n):
    bits = [1 << b for b in range(1, n.bit_length() - 1)]
    return lax.ppermute(value, "sl", [(i, i ^ bits[(k + i % 2) % len(bits)]) for i in range(n)])


def lm_send(value, k, n_lm, n_sl):
    bits = [1 << b for b in range(n_lm.bit_length() - 1)]
    perm = [
        (i * n_sl + j, (i ^ bits[(k + j % 2) % len(bits)]) * n_sl + j)
        for i in range(n_lm)
        for j in range(n_sl)
    ]
    return lax.ppermute(value, ("lm", "sl"), perm)


def prepare_kernel(
    land_ref, codes_ref, exponents_ref, eig_ref, first_ref, codes, eig, exponents, sems
):
    rows, feat = land_ref.shape
    half = rows // 2 - SHIFT
    ritz = eig_ref.shape[0]
    pairs = [
        (codes_ref, codes),
        (eig_ref, eig),
        (exponents_ref, exponents),
        (land_ref.at[:half], first_ref.at[:half]),
    ]
    copies = [pltpu.make_async_copy(src, dst, sems.at[k]) for k, (src, dst) in enumerate(pairs)]
    for copy in copies:
        copy.start()
    for copy in copies[:3]:
        copy.wait()
    pieces = []
    for b in range(rows // BLOCK):
        scale = lax.shift_left(jnp.int32(1), exponents[b] + 15).astype(jnp.float32) * 2.0**-15
        pieces.append(codes[:, b * BLOCK : (b + 1) * BLOCK].astype(jnp.float32) * scale)
    basis = jnp.concatenate(pieces, axis=1).astype(jnp.bfloat16)
    vectors = jnp.dot(eig[...], basis, preferred_element_type=jnp.float32).astype(jnp.bfloat16)
    chunks = feat // rows
    depth = ritz // chunks
    for c in range(chunks):
        first_ref[half:, c * rows : (c + 1) * rows] = vectors[c * depth : (c + 1) * depth, :]
    for copy in copies[3:]:
        copy.wait()


def tail_kernel(land_ref, out_ref, sem):
    copy = pltpu.make_async_copy(land_ref.at[land_ref.shape[0] - out_ref.shape[0] :], out_ref, sem)
    copy.start()
    copy.wait()


def second_half(landmarks):
    rows, feat = landmarks.shape
    return pl.pallas_call(
        tail_kernel,
        out_shape=jax.ShapeDtypeStruct((rows // 2 + SHIFT, feat), jnp.bfloat16),
        in_specs=[pl.BlockSpec(memory_space=pltpu.HBM)],
        scratch_shapes=[pltpu.SemaphoreType.DMA],
        compiler_params=pltpu.CompilerParams(vmem_limit_bytes=8 * MIB),
    )(pltpu.with_memory_space_constraint(landmarks, pltpu.HBM))


def prepare(landmarks, codes_t, exponents, eig_t):
    rows, feat = landmarks.shape
    extra = eig_t.shape[0] * rows // feat
    return pl.pallas_call(
        prepare_kernel,
        out_shape=jax.ShapeDtypeStruct((rows // 2 - SHIFT + extra, feat), jnp.bfloat16),
        in_specs=[pl.BlockSpec(memory_space=pltpu.HBM)] * 4,
        scratch_shapes=[
            pltpu.VMEM(codes_t.shape, codes_t.dtype),
            pltpu.VMEM(eig_t.shape, eig_t.dtype),
            pltpu.SMEM(exponents.shape, exponents.dtype),
            pltpu.SemaphoreType.DMA((4,)),
        ],
        compiler_params=pltpu.CompilerParams(vmem_limit_bytes=8 * MIB),
    )(*(pltpu.with_memory_space_constraint(x, pltpu.HBM) for x in (landmarks, codes_t, exponents, eig_t)))


def transpose_kernel(in_ref, out_ref):
    for k in range(in_ref.shape[0] // CHUNK):
        rows = slice(k * CHUNK, (k + 1) * CHUNK)
        out_ref[:, rows] = in_ref[rows, :].T


def affinity_kernel(count, coeff, *refs):
    land_ref = refs[count]
    work = [
        (k, slice(c, c + CHUNK)) for k in range(count) for c in range(0, refs[k].shape[1], CHUNK)
    ]

    def scores(k, cols):
        return jnp.dot(land_ref[...], refs[k][:, cols], preferred_element_type=jnp.float32)

    ahead = scores(*work[0])
    for n, (k, cols) in enumerate(work):
        now, ahead = ahead, scores(*work[n + 1]) if n + 1 < len(work) else None
        refs[count + 1 + k][:, cols] = jnp.exp(now * coeff).astype(jnp.bfloat16)


def affinities(slabs, land, coeff):
    count = len(slabs)
    feat, rows = slabs[0].shape
    size = land.shape[0]
    return pl.pallas_call(
        functools.partial(affinity_kernel, count, coeff),
        out_shape=[jax.ShapeDtypeStruct((size, rows), jnp.bfloat16)] * count,
        compiler_params=pltpu.CompilerParams(vmem_limit_bytes=24 * MIB),
        cost_estimate=pl.CostEstimate(
            flops=2 * count * rows * size * feat,
            bytes_accessed=2 * (count * rows + size) * feat,
            transcendentals=count * rows * size,
        ),
    )(*slabs, land)


def stage_kernel(count, coeff, ritz, has_acc, spans, rows, use, *refs):
    refs = list(refs)
    slabs = [refs.pop(0) for _ in range(count)]
    first_ref = refs.pop(0)
    second_ref = refs.pop(0) if use[1] == "land" else None
    ready = [refs.pop(0) for _ in range(count)] if use[1] == "ready" else None
    accs = [refs.pop(0) for _ in range(count)] if has_acc else [None] * count
    outs = refs
    feat = first_ref.shape[1]
    head = first_ref.shape[0] - ritz * rows // feat
    lands = [first_ref[:head, :]] if use[0] else []
    if second_ref is not None:
        lands.append(second_ref[...])
    land = jnp.concatenate(lands, axis=0) if len(lands) > 1 else lands[0]
    vec = jnp.concatenate(
        [first_ref[head:, c * rows : (c + 1) * rows] for c in range(feat // rows)], axis=0
    )
    work = [
        (k, slice(c, min(c + CHUNK, stop)))
        for k, (start, stop) in enumerate(spans)
        for c in range(start, stop, CHUNK)
    ]

    def scores(k, cols):
        return jnp.dot(land, slabs[k][:, cols], preferred_element_type=jnp.float32)

    ahead = scores(*work[0])
    for n, (k, cols) in enumerate(work):
        now, ahead = ahead, scores(*work[n + 1]) if n + 1 < len(work) else None
        affinity = jnp.exp(now * coeff).astype(jnp.bfloat16)
        width = cols.stop - cols.start
        if ready is not None:
            affinity = jnp.concatenate([affinity, ready[k][:, cols]], axis=0)
        elif not use[0]:
            affinity = jnp.concatenate([jnp.zeros((head, width), jnp.bfloat16), affinity], axis=0)
        elif not use[1]:
            blank = jnp.zeros((rows - head, width), jnp.bfloat16)
            affinity = jnp.concatenate([affinity, blank], axis=0)
        term = jnp.dot(vec, affinity, preferred_element_type=jnp.float32)
        place = slice(cols.start - spans[k][0], cols.stop - spans[k][0])
        outs[k][:, place] = term if accs[k] is None else accs[k][:, cols] + term


def stage(slabs, block, ready, accs, coeff, ritz, size, use=("land", "land"), spans=None):
    feat, rows = slabs[0].shape
    first, second = block
    count = len(slabs)
    spans = spans or [(0, rows)] * count
    rows = spans[0][1] - spans[0][0]
    head = first.shape[0] - ritz * size // feat
    land = (head if use[0] else 0) + (size - head if use[1] == "land" else 0)
    args = [*slabs, first]
    if use[1] == "land":
        args.append(second)
    if use[1] == "ready":
        args.extend(ready)
    return pl.pallas_call(
        functools.partial(stage_kernel, count, coeff, ritz, accs is not None, spans, size, use),
        out_shape=[jax.ShapeDtypeStruct((ritz, rows), jnp.float32)] * count,
        compiler_params=pltpu.CompilerParams(vmem_limit_bytes=32 * MIB),
        cost_estimate=pl.CostEstimate(
            flops=2 * count * rows * (land * feat + 4 * size * ritz),
            bytes_accessed=2 * (count * rows + land) * feat,
            transcendentals=count * rows * land,
        ),
    )(*args, *(accs or []))


def add_kernel(a_ref, b_ref, out_ref):
    total = a_ref[...].astype(jnp.float32) + b_ref[...].astype(jnp.float32)
    out_ref[...] = total.astype(out_ref.dtype)


def scale_kernel(*refs, total_land):
    ritz_ref, out_ref = refs[-2:]
    factor = 1.0 / (ritz_ref[...] * math.sqrt(total_land))
    start = 0
    for a_ref, b_ref in zip(refs[0:-2:2], refs[1:-2:2]):
        stop = start + a_ref.shape[1]
        total = a_ref[...].astype(jnp.float32) + b_ref[...].astype(jnp.float32)
        out_ref[:, start:stop] = total * factor
        start = stop


def small_call(kernel, out, *args):
    return pl.pallas_call(
        kernel,
        out_shape=jax.ShapeDtypeStruct(out.shape, out.dtype),
        compiler_params=pltpu.CompilerParams(vmem_limit_bytes=8 * MIB),
    )(*args)


def local(slab, landmarks, codes, exponents, eigvec, ritz):
    n_lm, n_sl = lax.axis_size("lm"), lax.axis_size("sl")
    total_land = codes.shape[0] * n_lm * n_sl
    coeff = 1.0 / math.sqrt(slab.shape[1])
    cols = ritz.shape[0]
    rows = slab.shape[0]
    ways = n_sl.bit_length() - 2

    second = second_half(landmarks)
    first = prepare(landmarks, codes.T, exponents, eigvec.T)
    blocks = {0: [first, second]}
    for k in range(ways):
        blocks[1 << k] = [None, None]
    for turn in (0, 1):
        for k in range(ways):
            piece = (k + turn) % 2
            blocks[1 << k][piece] = chip_send(blocks[0][piece], k, n_sl)
    late_slab, _ = lax.optimization_barrier((slab, second))
    turned = jax.ShapeDtypeStruct(slab.shape[::-1], slab.dtype)
    other = small_call(transpose_kernel, turned, core_send(late_slab, n_sl))
    slab = small_call(transpose_kernel, turned, slab)
    size = landmarks.shape[0]
    both = [slab, other]
    for k in range(1, ways, 2):
        blocks[1 << k][1], both = lax.optimization_barrier((blocks[1 << k][1], both))
    accs = stage(both, (first, second), None, None, coeff, cols, size)
    for k in range(0, ways, 2):
        blocks[1 << k][0], accs = lax.optimization_barrier((blocks[1 << k][0], accs))
    for t in range(1, 1 << ways):
        if t in blocks:
            continue
        low, high = (t & -t).bit_length() - 1, t.bit_length() - 1
        blocks[t] = [
            chip_send(blocks[t ^ (1 << high)][0], high, n_sl),
            chip_send(blocks[t ^ (1 << low)][1], low, n_sl),
        ]

    last = (1 << ways) - 1
    ready = {}
    for t in range(1, last + 1):
        if t not in [1 << k for k in range(0, ways, 2)]:
            ready[t] = affinities(both, blocks[t][1], coeff)
    for t in range(1, last):
        if t not in ready:
            accs = stage(both, blocks[t], None, accs, coeff, cols, size, ("land", ""))
    for t in range(1, last):
        use = ("land", "ready") if t in ready else ("", "land")
        accs = stage(both, blocks[t], ready.get(t), accs, coeff, cols, size, use)

    slab, other = both
    end = functools.partial(stage, coeff=coeff, ritz=cols, size=size, use=("land", "ready"))
    block, (aff, other_aff) = blocks[last], ready[last]
    width = rows // 2
    spans = [(0, width), (width, rows)]
    half = jax.ShapeDtypeStruct((cols, width), jnp.bfloat16)
    theirs = end([other] * 2, block, [other_aff] * 2, [accs[1]] * 2, spans=spans)
    received = [core_send(value, n_sl) for value in theirs]
    mine = end([slab] * 2, block, [aff] * 2, [accs[0]] * 2, spans=spans)
    totals = [small_call(add_kernel, half, a, b) for a, b in zip(mine, received)]
    turns = n_lm.bit_length() - 1
    for k in range(turns - 1):
        arrived = [lm_send(total, k, n_lm, n_sl) for total in totals]
        totals = [small_call(add_kernel, half, a, b) for a, b in zip(totals, arrived)]
    pairs = [(total, lm_send(total, turns - 1, n_lm, n_sl)) for total in totals]
    scale = functools.partial(scale_kernel, total_land=total_land)
    out = jax.ShapeDtypeStruct((cols, rows), jnp.float32)
    return small_call(scale, out, *(x for pair in pairs for x in pair), ritz[:, None]).T


def solution(mesh):
    return jax.shard_map(
        local,
        mesh=mesh,
        in_specs=(
            P("sl", None),
            P(("lm", "sl"), None),
            P(("lm", "sl"), None),
            P(("lm", "sl")),
            P(),
            P(),
        ),
        out_specs=P("sl", None),
        check_vma=False,
    )
```

```python
import functools
import math

import jax
import jax.numpy as jnp
from jax import lax
from jax.experimental import pallas as pl
from jax.experimental.pallas import tpu as pltpu
from jax.sharding import PartitionSpec as P

BLOCK = 128
SHIFT = 16
CHUNK = 512
MIB = 2**20


def core_send(value, n):
    return lax.ppermute(value, "sl", [(i, i ^ 1) for i in range(n)])


def chip_send(value, k, n):
    bits = [1 << b for b in range(1, n.bit_length() - 1)]
    return lax.ppermute(value, "sl", [(i, i ^ bits[(k + i % 2) % len(bits)]) for i in range(n)])


def lm_send(value, k, n_lm, n_sl):
    bits = [1 << b for b in range(n_lm.bit_length() - 1)]
    perm = [
        (i * n_sl + j, (i ^ bits[(k + j % 2) % len(bits)]) * n_sl + j)
        for i in range(n_lm)
        for j in range(n_sl)
    ]
    return lax.ppermute(value, ("lm", "sl"), perm)


def prepare_kernel(
    land_ref, codes_ref, exponents_ref, eig_ref, first_ref, codes, eig, exponents, sems
):
    rows, feat = land_ref.shape
    half = rows // 2 - SHIFT
    ritz = eig_ref.shape[0]
    pairs = [
        (codes_ref, codes),
        (eig_ref, eig),
        (exponents_ref, exponents),
        (land_ref.at[:half], first_ref.at[:half]),
    ]
    copies = [pltpu.make_async_copy(src, dst, sems.at[k]) for k, (src, dst) in enumerate(pairs)]
    for copy in copies:
        copy.start()
    for copy in copies[:3]:
        copy.wait()
    pieces = []
    for b in range(rows // BLOCK):
        scale = lax.shift_left(jnp.int32(1), exponents[b] + 15).astype(jnp.float32) * 2.0**-15
        pieces.append(codes[:, b * BLOCK : (b + 1) * BLOCK].astype(jnp.float32) * scale)
    basis = jnp.concatenate(pieces, axis=1).astype(jnp.bfloat16)
    vectors = jnp.dot(eig[...], basis, preferred_element_type=jnp.float32).astype(jnp.bfloat16)
    chunks = feat // rows
    depth = ritz // chunks
    for c in range(chunks):
        first_ref[half:, c * rows : (c + 1) * rows] = vectors[c * depth : (c + 1) * depth, :]
    for copy in copies[3:]:
        copy.wait()


def prepare(landmarks, codes_t, exponents, eig_t):
    rows, feat = landmarks.shape
    extra = eig_t.shape[0] * rows // feat
    return pl.pallas_call(
        prepare_kernel,
        out_shape=jax.ShapeDtypeStruct((rows // 2 - SHIFT + extra, feat), jnp.bfloat16),
        in_specs=[pl.BlockSpec(memory_space=pltpu.HBM)] * 4,
        scratch_shapes=[
            pltpu.VMEM(codes_t.shape, codes_t.dtype),
            pltpu.VMEM(eig_t.shape, eig_t.dtype),
            pltpu.SMEM(exponents.shape, exponents.dtype),
            pltpu.SemaphoreType.DMA((4,)),
        ],
        compiler_params=pltpu.CompilerParams(vmem_limit_bytes=8 * MIB),
    )(*(pltpu.with_memory_space_constraint(x, pltpu.HBM) for x in (landmarks, codes_t, exponents, eig_t)))


def transpose_kernel(in_ref, out_ref):
    for k in range(in_ref.shape[0] // CHUNK):
        rows = slice(k * CHUNK, (k + 1) * CHUNK)
        out_ref[:, rows] = in_ref[rows, :].T


def stage_kernel(count, coeff, ritz, has_acc, spans, *refs):
    slabs = refs[:count]
    first_ref, second_ref = refs[count : count + 2]
    accs = refs[count + 2 : 2 * count + 2] if has_acc else [None] * count
    outs = refs[-count:]
    tail, feat = second_ref.shape
    rows = (first_ref.shape[0] + tail) * feat // (feat + ritz)
    head = rows - tail
    land = jnp.concatenate([first_ref[:head, :], second_ref[...]], axis=0)
    vec = jnp.concatenate(
        [first_ref[head:, c * rows : (c + 1) * rows] for c in range(feat // rows)], axis=0
    )
    work = [
        (k, slice(c, min(c + CHUNK, stop)))
        for k, (start, stop) in enumerate(spans)
        for c in range(start, stop, CHUNK)
    ]

    def scores(k, cols):
        return jnp.dot(land, slabs[k][:, cols], preferred_element_type=jnp.float32)

    ahead = scores(*work[0])
    for n, (k, cols) in enumerate(work):
        now, ahead = ahead, scores(*work[n + 1]) if n + 1 < len(work) else None
        affinity = jnp.exp(now * coeff).astype(jnp.bfloat16)
        term = jnp.dot(vec, affinity, preferred_element_type=jnp.float32)
        place = slice(cols.start - spans[k][0], cols.stop - spans[k][0])
        outs[k][:, place] = term if accs[k] is None else accs[k][:, cols] + term


def stage(slabs, first, second, accs, coeff, ritz, spans=None):
    feat, rows = slabs[0].shape
    land = (first.shape[0] + second.shape[0]) * feat // (feat + ritz)
    count = len(slabs)
    spans = spans or [(0, rows)] * count
    rows = spans[0][1] - spans[0][0]
    return pl.pallas_call(
        functools.partial(stage_kernel, count, coeff, ritz, accs is not None, spans),
        out_shape=[jax.ShapeDtypeStruct((ritz, rows), jnp.float32)] * count,
        compiler_params=pltpu.CompilerParams(vmem_limit_bytes=32 * MIB),
        cost_estimate=pl.CostEstimate(
            flops=2 * count * rows * land * (feat + 4 * ritz),
            bytes_accessed=2 * (count * rows + land) * feat,
            transcendentals=count * rows * land,
        ),
    )(*slabs, first, second, *(accs or []))


def add_kernel(a_ref, b_ref, out_ref):
    total = a_ref[...].astype(jnp.float32) + b_ref[...].astype(jnp.float32)
    out_ref[...] = total.astype(out_ref.dtype)


def scale_kernel(*refs, total_land):
    ritz_ref, out_ref = refs[-2:]
    factor = 1.0 / (ritz_ref[...] * math.sqrt(total_land))
    start = 0
    for a_ref, b_ref in zip(refs[0:-2:2], refs[1:-2:2]):
        stop = start + a_ref.shape[1]
        total = a_ref[...].astype(jnp.float32) + b_ref[...].astype(jnp.float32)
        out_ref[:, start:stop] = total * factor
        start = stop


def small_call(kernel, out, *args):
    return pl.pallas_call(
        kernel,
        out_shape=jax.ShapeDtypeStruct(out.shape, out.dtype),
        compiler_params=pltpu.CompilerParams(vmem_limit_bytes=8 * MIB),
    )(*args)


def local(slab, landmarks, codes, exponents, eigvec, ritz):
    n_lm, n_sl = lax.axis_size("lm"), lax.axis_size("sl")
    total_land = codes.shape[0] * n_lm * n_sl
    coeff = 1.0 / math.sqrt(slab.shape[1])
    cols = ritz.shape[0]
    rows = slab.shape[0]
    ways = n_sl.bit_length() - 2

    second = landmarks[landmarks.shape[0] // 2 - SHIFT :]
    first = prepare(landmarks, codes.T, exponents, eigvec.T)
    blocks = {0: [first, second]}
    for k in range(ways):
        blocks[1 << k] = [None, None]
    for turn in (0, 1):
        for k in range(ways):
            piece = (k + turn) % 2
            blocks[1 << k][piece] = chip_send(blocks[0][piece], k, n_sl)
    late_slab, _ = lax.optimization_barrier((slab, second))
    turned = jax.ShapeDtypeStruct(slab.shape[::-1], slab.dtype)
    other = small_call(transpose_kernel, turned, core_send(late_slab, n_sl))
    slab = small_call(transpose_kernel, turned, slab)
    (acc,) = stage([slab], first, second, None, coeff, cols)
    held = [blocks[1 << k][k % 2] for k in range(ways)]
    held, acc = lax.optimization_barrier((held, acc))
    for k in range(ways):
        blocks[1 << k][k % 2] = held[k]
    (other_acc,) = stage([other], first, second, None, coeff, cols)
    accs = [acc, other_acc]
    for t in range(1, 1 << ways):
        if t in blocks:
            continue
        low, high = (t & -t).bit_length() - 1, t.bit_length() - 1
        blocks[t] = [
            chip_send(blocks[t ^ (1 << high)][0], high, n_sl),
            chip_send(blocks[t ^ (1 << low)][1], low, n_sl),
        ]

    for t in range(1, (1 << ways) - 1):
        accs = stage([slab, other], *blocks[t], accs, coeff, cols)
    end = blocks[(1 << ways) - 1]
    width = rows // 2
    spans = [(0, width), (width, rows)]
    half = jax.ShapeDtypeStruct((cols, width), jnp.bfloat16)
    (early,) = stage([other], *end, accs[1:], coeff, cols, spans[:1])
    received = [core_send(early, n_sl)]
    late, mine = stage([other, slab], *end, accs[::-1], coeff, cols, spans[::-1])
    received.append(core_send(late, n_sl))
    total = small_call(add_kernel, half, mine, received[0])
    acc, total = lax.optimization_barrier((accs[0], total))
    (mine,) = stage([slab], *end, [acc], coeff, cols, spans[1:])
    totals = [total, small_call(add_kernel, half, mine, received[1])]
    turns = n_lm.bit_length() - 1
    for k in range(turns - 1):
        arrived = [lm_send(total, k, n_lm, n_sl) for total in totals]
        totals = [small_call(add_kernel, half, a, b) for a, b in zip(totals, arrived)]
    pairs = [(total, lm_send(total, turns - 1, n_lm, n_sl)) for total in totals]
    scale = functools.partial(scale_kernel, total_land=total_land)
    out = jax.ShapeDtypeStruct((cols, rows), jnp.float32)
    return small_call(scale, out, *(x for pair in pairs for x in pair), ritz[:, None]).T


def solution(mesh):
    return jax.shard_map(
        local,
        mesh=mesh,
        in_specs=(
            P("sl", None),
            P(("lm", "sl"), None),
            P(("lm", "sl"), None),
            P(("lm", "sl")),
            P(),
            P(),
        ),
        out_specs=P("sl", None),
        check_vma=False,
    )
```

```python
import functools
import math

import jax
import jax.numpy as jnp
from jax import lax
from jax.experimental import pallas as pl
from jax.experimental.pallas import tpu as pltpu
from jax.sharding import PartitionSpec as P

BLOCK = 128
SHIFT = 16
CHUNK = 512
MIB = 2**20


def core_send(value, n):
    return lax.ppermute(value, "sl", [(i, i ^ 1) for i in range(n)])


def chip_send(value, k, n):
    bits = [1 << b for b in range(1, n.bit_length() - 1)]
    return lax.ppermute(value, "sl", [(i, i ^ bits[(k + i % 2) % len(bits)]) for i in range(n)])


def lm_send(value, k, n_lm, n_sl):
    bits = [1 << b for b in range(n_lm.bit_length() - 1)]
    perm = [
        (i * n_sl + j, (i ^ bits[(k + j % 2) % len(bits)]) * n_sl + j)
        for i in range(n_lm)
        for j in range(n_sl)
    ]
    return lax.ppermute(value, ("lm", "sl"), perm)


def prepare_kernel(
    land_ref, codes_ref, exponents_ref, eig_ref, first_ref, codes, eig, exponents, sems
):
    rows, feat = land_ref.shape
    half = rows // 2 - SHIFT
    ritz = eig_ref.shape[0]
    pairs = [
        (codes_ref, codes),
        (eig_ref, eig),
        (exponents_ref, exponents),
        (land_ref.at[:half], first_ref.at[:half]),
    ]
    copies = [pltpu.make_async_copy(src, dst, sems.at[k]) for k, (src, dst) in enumerate(pairs)]
    for copy in copies:
        copy.start()
    for copy in copies[:3]:
        copy.wait()
    pieces = []
    for b in range(rows // BLOCK):
        scale = lax.shift_left(jnp.int32(1), exponents[b] + 15).astype(jnp.float32) * 2.0**-15
        pieces.append(codes[:, b * BLOCK : (b + 1) * BLOCK].astype(jnp.float32) * scale)
    basis = jnp.concatenate(pieces, axis=1).astype(jnp.bfloat16)
    vectors = jnp.dot(eig[...], basis, preferred_element_type=jnp.float32).astype(jnp.bfloat16)
    chunks = feat // rows
    depth = ritz // chunks
    for c in range(chunks):
        first_ref[half:, c * rows : (c + 1) * rows] = vectors[c * depth : (c + 1) * depth, :]
    for copy in copies[3:]:
        copy.wait()


def prepare(landmarks, codes_t, exponents, eig_t):
    rows, feat = landmarks.shape
    extra = eig_t.shape[0] * rows // feat
    return pl.pallas_call(
        prepare_kernel,
        out_shape=jax.ShapeDtypeStruct((rows // 2 - SHIFT + extra, feat), jnp.bfloat16),
        in_specs=[pl.BlockSpec(memory_space=pltpu.HBM)] * 4,
        scratch_shapes=[
            pltpu.VMEM(codes_t.shape, codes_t.dtype),
            pltpu.VMEM(eig_t.shape, eig_t.dtype),
            pltpu.SMEM(exponents.shape, exponents.dtype),
            pltpu.SemaphoreType.DMA((4,)),
        ],
        compiler_params=pltpu.CompilerParams(vmem_limit_bytes=8 * MIB),
    )(*(pltpu.with_memory_space_constraint(x, pltpu.HBM) for x in (landmarks, codes_t, exponents, eig_t)))


def transpose_kernel(in_ref, out_ref):
    for k in range(in_ref.shape[0] // CHUNK):
        rows = slice(k * CHUNK, (k + 1) * CHUNK)
        out_ref[:, rows] = in_ref[rows, :].T


def stage_kernel(count, coeff, ritz, has_acc, spans, *refs):
    slabs = refs[:count]
    first_ref, second_ref = refs[count : count + 2]
    accs = refs[count + 2 : 2 * count + 2] if has_acc else [None] * count
    outs = refs[-count:]
    tail, feat = second_ref.shape
    rows = (first_ref.shape[0] + tail) * feat // (feat + ritz)
    head = rows - tail
    land = jnp.concatenate([first_ref[:head, :], second_ref[...]], axis=0)
    vec = jnp.concatenate(
        [first_ref[head:, c * rows : (c + 1) * rows] for c in range(feat // rows)], axis=0
    )
    work = [
        (k, slice(c, min(c + CHUNK, stop)))
        for k, (start, stop) in enumerate(spans)
        for c in range(start, stop, CHUNK)
    ]

    def scores(k, cols):
        return jnp.dot(land, slabs[k][:, cols], preferred_element_type=jnp.float32)

    ahead = scores(*work[0])
    for n, (k, cols) in enumerate(work):
        now, ahead = ahead, scores(*work[n + 1]) if n + 1 < len(work) else None
        affinity = jnp.exp(now * coeff).astype(jnp.bfloat16)
        term = jnp.dot(vec, affinity, preferred_element_type=jnp.float32)
        place = slice(cols.start - spans[k][0], cols.stop - spans[k][0])
        outs[k][:, place] = term if accs[k] is None else accs[k][:, cols] + term


def stage(slabs, first, second, accs, coeff, ritz, spans=None):
    feat, rows = slabs[0].shape
    land = (first.shape[0] + second.shape[0]) * feat // (feat + ritz)
    count = len(slabs)
    spans = spans or [(0, rows)] * count
    widths = [stop - start for start, stop in spans]
    return pl.pallas_call(
        functools.partial(stage_kernel, count, coeff, ritz, accs is not None, spans),
        out_shape=[jax.ShapeDtypeStruct((ritz, width), jnp.float32) for width in widths],
        compiler_params=pltpu.CompilerParams(vmem_limit_bytes=32 * MIB),
        cost_estimate=pl.CostEstimate(
            flops=2 * sum(widths) * land * (feat + 4 * ritz),
            bytes_accessed=2 * (sum(widths) + land) * feat,
            transcendentals=sum(widths) * land,
        ),
    )(*slabs, first, second, *(accs or []))


def add_kernel(a_ref, b_ref, out_ref):
    total = a_ref[...].astype(jnp.float32) + b_ref[...].astype(jnp.float32)
    out_ref[...] = total.astype(out_ref.dtype)


def scale_kernel(*refs, total_land):
    ritz_ref, out_ref = refs[-2:]
    factor = 1.0 / (ritz_ref[...] * math.sqrt(total_land))
    start = 0
    for a_ref, b_ref in zip(refs[0:-2:2], refs[1:-2:2]):
        stop = start + a_ref.shape[1]
        total = a_ref[...].astype(jnp.float32) + b_ref[...].astype(jnp.float32)
        out_ref[:, start:stop] = total * factor
        start = stop


def small_call(kernel, out, *args):
    return pl.pallas_call(
        kernel,
        out_shape=jax.ShapeDtypeStruct(out.shape, out.dtype),
        compiler_params=pltpu.CompilerParams(vmem_limit_bytes=8 * MIB),
    )(*args)


def local(slab, landmarks, codes, exponents, eigvec, ritz):
    n_lm, n_sl = lax.axis_size("lm"), lax.axis_size("sl")
    total_land = codes.shape[0] * n_lm * n_sl
    coeff = 1.0 / math.sqrt(slab.shape[1])
    cols = ritz.shape[0]
    rows = slab.shape[0]
    ways = n_sl.bit_length() - 2

    second = landmarks[landmarks.shape[0] // 2 - SHIFT :]
    first = prepare(landmarks, codes.T, exponents, eigvec.T)
    blocks = {0: [first, second]}
    for k in range(ways):
        blocks[1 << k] = [None, None]
    for turn in (0, 1):
        for k in range(ways):
            piece = (k + turn) % 2
            blocks[1 << k][piece] = chip_send(blocks[0][piece], k, n_sl)
    late_slab, _ = lax.optimization_barrier((slab, second))
    turned = jax.ShapeDtypeStruct(slab.shape[::-1], slab.dtype)
    other = small_call(transpose_kernel, turned, core_send(late_slab, n_sl))
    slab = small_call(transpose_kernel, turned, slab)
    (acc,) = stage([slab], first, second, None, coeff, cols)
    held = [blocks[1 << k][k % 2] for k in range(ways)]
    held, acc = lax.optimization_barrier((held, acc))
    for k in range(ways):
        blocks[1 << k][k % 2] = held[k]
    (other_acc,) = stage([other], first, second, None, coeff, cols)
    accs = [acc, other_acc]
    for t in range(1, 1 << ways):
        if t in blocks:
            continue
        low, high = (t & -t).bit_length() - 1, t.bit_length() - 1
        blocks[t] = [
            chip_send(blocks[t ^ (1 << high)][0], high, n_sl),
            chip_send(blocks[t ^ (1 << low)][1], low, n_sl),
        ]

    for t in range(1, (1 << ways) - 1):
        accs = stage([slab, other], *blocks[t], accs, coeff, cols)
    end = blocks[(1 << ways) - 1]
    spans = [(0, rows * 5 // 8), (rows * 5 // 8, rows)]
    pieces = [jax.ShapeDtypeStruct((cols, stop - start), jnp.bfloat16) for start, stop in spans]
    (early,) = stage([other], *end, accs[1:], coeff, cols, spans[:1])
    received = [core_send(early, n_sl)]
    late, mine = stage([other, slab], *end, accs[::-1], coeff, cols, spans[::-1])
    received.append(core_send(late, n_sl))
    total = small_call(add_kernel, pieces[0], mine, received[0])
    acc, total = lax.optimization_barrier((accs[0], total))
    (mine,) = stage([slab], *end, [acc], coeff, cols, spans[1:])
    totals = [total, small_call(add_kernel, pieces[1], mine, received[1])]
    turns = n_lm.bit_length() - 1
    for k in range(turns - 1):
        arrived = [lm_send(total, k, n_lm, n_sl) for total in totals]
        arrived[0], _ = lax.optimization_barrier((arrived[0], totals[1]))
        totals = [small_call(add_kernel, p, a, b) for p, a, b in zip(pieces, totals, arrived)]
    pairs = [(total, lm_send(total, turns - 1, n_lm, n_sl)) for total in totals]
    scale = functools.partial(scale_kernel, total_land=total_land)
    out = jax.ShapeDtypeStruct((cols, rows), jnp.float32)
    return small_call(scale, out, *(x for pair in pairs for x in pair), ritz[:, None]).T


def solution(mesh):
    return jax.shard_map(
        local,
        mesh=mesh,
        in_specs=(
            P("sl", None),
            P(("lm", "sl"), None),
            P(("lm", "sl"), None),
            P(("lm", "sl")),
            P(),
            P(),
        ),
        out_specs=P("sl", None),
        check_vma=False,
    )
```

```python
import functools
import math

import jax
import jax.numpy as jnp
from jax import lax
from jax.experimental import pallas as pl
from jax.experimental.pallas import tpu as pltpu
from jax.sharding import PartitionSpec as P

BLOCK = 128
SHIFT = 16
CHUNK = 512
MIB = 2**20


def core_send(value, n, source=None):
    perm = [(i, i ^ 1) for i in range(n) if source is None or i % 2 == source]
    return lax.ppermute(value, "sl", perm)


def chip_send(value, k, n):
    bits = [1 << b for b in range(1, n.bit_length() - 1)]
    return lax.ppermute(value, "sl", [(i, i ^ bits[(k + i % 2) % len(bits)]) for i in range(n)])


def lm_send(value, k, n_lm, n_sl):
    perm = [
        (i * n_sl + j, (i ^ (1 << k)) * n_sl + j) for i in range(n_lm) for j in range(1, n_sl, 2)
    ]
    return lax.ppermute(value, ("lm", "sl"), perm)


def prepare_kernel(
    land_ref, codes_ref, exponents_ref, eig_ref, first_ref, codes, eig, exponents, sems
):
    rows, feat = land_ref.shape
    half = rows // 2 - SHIFT
    ritz = eig_ref.shape[0]
    pairs = [
        (codes_ref, codes),
        (eig_ref, eig),
        (exponents_ref, exponents),
        (land_ref.at[:half], first_ref.at[:half]),
    ]
    copies = [pltpu.make_async_copy(src, dst, sems.at[k]) for k, (src, dst) in enumerate(pairs)]
    for copy in copies:
        copy.start()
    for copy in copies[:3]:
        copy.wait()
    pieces = []
    for b in range(rows // BLOCK):
        scale = lax.shift_left(jnp.int32(1), exponents[b] + 15).astype(jnp.float32) * 2.0**-15
        pieces.append(codes[:, b * BLOCK : (b + 1) * BLOCK].astype(jnp.float32) * scale)
    basis = jnp.concatenate(pieces, axis=1).astype(jnp.bfloat16)
    vectors = jnp.dot(eig[...], basis, preferred_element_type=jnp.float32).astype(jnp.bfloat16)
    chunks = feat // rows
    depth = ritz // chunks
    for c in range(chunks):
        first_ref[half:, c * rows : (c + 1) * rows] = vectors[c * depth : (c + 1) * depth, :]
    for copy in copies[3:]:
        copy.wait()


def prepare(landmarks, codes_t, exponents, eig_t):
    rows, feat = landmarks.shape
    extra = eig_t.shape[0] * rows // feat
    return pl.pallas_call(
        prepare_kernel,
        out_shape=jax.ShapeDtypeStruct((rows // 2 - SHIFT + extra, feat), jnp.bfloat16),
        in_specs=[pl.BlockSpec(memory_space=pltpu.HBM)] * 4,
        scratch_shapes=[
            pltpu.VMEM(codes_t.shape, codes_t.dtype),
            pltpu.VMEM(eig_t.shape, eig_t.dtype),
            pltpu.SMEM(exponents.shape, exponents.dtype),
            pltpu.SemaphoreType.DMA((4,)),
        ],
        compiler_params=pltpu.CompilerParams(vmem_limit_bytes=8 * MIB),
    )(*(pltpu.with_memory_space_constraint(x, pltpu.HBM) for x in (landmarks, codes_t, exponents, eig_t)))


def transpose_kernel(in_ref, out_ref):
    for k in range(in_ref.shape[0] // CHUNK):
        rows = slice(k * CHUNK, (k + 1) * CHUNK)
        out_ref[:, rows] = in_ref[rows, :].T


def stage_kernel(count, coeff, ritz, has_acc, spans, *refs):
    slabs = refs[:count]
    first_ref, second_ref = refs[count : count + 2]
    accs = refs[count + 2 : 2 * count + 2] if has_acc else [None] * count
    outs = refs[-count:]
    tail, feat = second_ref.shape
    rows = (first_ref.shape[0] + tail) * feat // (feat + ritz)
    head = rows - tail
    land = jnp.concatenate([first_ref[:head, :], second_ref[...]], axis=0)
    vec = jnp.concatenate(
        [first_ref[head:, c * rows : (c + 1) * rows] for c in range(feat // rows)], axis=0
    )
    work = [
        (k, slice(c, min(c + CHUNK, stop)))
        for k, (start, stop) in enumerate(spans)
        for c in range(start, stop, CHUNK)
    ]

    def scores(k, cols):
        return jnp.dot(land, slabs[k][:, cols], preferred_element_type=jnp.float32)

    ahead = scores(*work[0])
    for n, (k, cols) in enumerate(work):
        now, ahead = ahead, scores(*work[n + 1]) if n + 1 < len(work) else None
        affinity = jnp.exp(now * coeff).astype(jnp.bfloat16)
        term = jnp.dot(vec, affinity, preferred_element_type=jnp.float32)
        place = slice(cols.start - spans[k][0], cols.stop - spans[k][0])
        outs[k][:, place] = term if accs[k] is None else accs[k][:, cols] + term


def stage(slabs, first, second, accs, coeff, ritz, spans=None):
    feat, rows = slabs[0].shape
    land = (first.shape[0] + second.shape[0]) * feat // (feat + ritz)
    count = len(slabs)
    spans = spans or [(0, rows)] * count
    rows = spans[0][1] - spans[0][0]
    return pl.pallas_call(
        functools.partial(stage_kernel, count, coeff, ritz, accs is not None, spans),
        out_shape=[jax.ShapeDtypeStruct((ritz, rows), jnp.float32)] * count,
        compiler_params=pltpu.CompilerParams(vmem_limit_bytes=32 * MIB),
        cost_estimate=pl.CostEstimate(
            flops=2 * count * rows * land * (feat + 4 * ritz),
            bytes_accessed=2 * (count * rows + land) * feat,
            transcendentals=count * rows * land,
        ),
    )(*slabs, first, second, *(accs or []))


def add_kernel(a_ref, b_ref, out_ref):
    total = a_ref[...].astype(jnp.float32) + b_ref[...].astype(jnp.float32)
    out_ref[...] = total.astype(out_ref.dtype)


def scale_kernel(odd_refs, even_refs, ritz_ref, out_ref, *, total_land):
    factor = 1.0 / (ritz_ref[...] * math.sqrt(total_land))

    def write(refs):
        a_ref, b_ref = refs
        total = a_ref[...].astype(jnp.float32) + b_ref[...].astype(jnp.float32)
        out_ref[...] = total * factor

    odd = lax.rem(lax.axis_index("sl"), 2)
    pl.when(odd == 1)(lambda: write(odd_refs))
    pl.when(odd == 0)(lambda: write(even_refs))


def small_call(kernel, out, *args):
    return pl.pallas_call(
        kernel,
        out_shape=jax.ShapeDtypeStruct(out.shape, out.dtype),
        compiler_params=pltpu.CompilerParams(vmem_limit_bytes=8 * MIB),
    )(*args)


def local(slab, landmarks, codes, exponents, eigvec, ritz):
    n_lm, n_sl = lax.axis_size("lm"), lax.axis_size("sl")
    total_land = codes.shape[0] * n_lm * n_sl
    coeff = 1.0 / math.sqrt(slab.shape[1])
    cols = ritz.shape[0]
    rows = slab.shape[0]
    ways = n_sl.bit_length() - 2

    second = landmarks[landmarks.shape[0] // 2 - SHIFT :]
    first = prepare(landmarks, codes.T, exponents, eigvec.T)
    blocks = {0: [first, second]}
    for k in range(ways):
        blocks[1 << k] = [None, None]
    for turn in (0, 1):
        for k in range(ways):
            piece = (k + turn) % 2
            blocks[1 << k][piece] = chip_send(blocks[0][piece], k, n_sl)
    late_slab, _ = lax.optimization_barrier((slab, second))
    turned = jax.ShapeDtypeStruct(slab.shape[::-1], slab.dtype)
    other = small_call(transpose_kernel, turned, core_send(late_slab, n_sl))
    slab = small_call(transpose_kernel, turned, slab)
    (acc,) = stage([slab], first, second, None, coeff, cols)
    held = [blocks[1 << k][k % 2] for k in range(ways)]
    held, acc = lax.optimization_barrier((held, acc))
    for k in range(ways):
        blocks[1 << k][k % 2] = held[k]
    (other_acc,) = stage([other], first, second, None, coeff, cols)
    accs = [acc, other_acc]
    for t in range(1, 1 << ways):
        if t in blocks:
            continue
        low, high = (t & -t).bit_length() - 1, t.bit_length() - 1
        blocks[t] = [
            chip_send(blocks[t ^ (1 << high)][0], high, n_sl),
            chip_send(blocks[t ^ (1 << low)][1], low, n_sl),
        ]

    for t in range(1, (1 << ways) - 1):
        accs = stage([slab, other], *blocks[t], accs, coeff, cols)
    end = blocks[(1 << ways) - 1]
    (mine,) = stage([slab], *end, accs[:1], coeff, cols)
    from_even = core_send(mine, n_sl, 0)
    (theirs,) = stage([other], *end, accs[1:], coeff, cols)
    own_from_even = core_send(theirs, n_sl, 0)
    piece = jax.ShapeDtypeStruct((cols, rows), jnp.bfloat16)
    totals = [
        small_call(add_kernel, piece, theirs, from_even),
        small_call(add_kernel, piece, mine, own_from_even),
    ]
    turns = n_lm.bit_length() - 1
    for k in range(turns - 1):
        arrived = [lm_send(total, (k + p) % turns, n_lm, n_sl) for p, total in enumerate(totals)]
        totals = [small_call(add_kernel, piece, a, b) for a, b in zip(totals, arrived)]
    even_total = core_send(totals[0], n_sl, 1)
    arrived = [lm_send(total, (turns - 1 + p) % turns, n_lm, n_sl) for p, total in enumerate(totals)]
    even_arrived = core_send(arrived[0], n_sl, 1)
    scale = functools.partial(scale_kernel, total_land=total_land)
    out = jax.ShapeDtypeStruct((cols, rows), jnp.float32)
    odd_parts, even_parts = (totals[1], arrived[1]), (even_total, even_arrived)
    return small_call(scale, out, odd_parts, even_parts, ritz[:, None]).T


def solution(mesh):
    return jax.shard_map(
        local,
        mesh=mesh,
        in_specs=(
            P("sl", None),
            P(("lm", "sl"), None),
            P(("lm", "sl"), None),
            P(("lm", "sl")),
            P(),
            P(),
        ),
        out_specs=P("sl", None),
        check_vma=False,
    )
```

```python
import functools
import math

import jax
import jax.numpy as jnp
from jax import lax
from jax.experimental import pallas as pl
from jax.experimental.pallas import tpu as pltpu
from jax.sharding import PartitionSpec as P

BLOCK = 128
SHIFT = 16
CHUNK = 512
MIB = 2**20


def core_send(value, n):
    return lax.ppermute(value, "sl", [(i, i ^ 1) for i in range(n)])


def chip_send(value, k, n):
    bits = [1 << b for b in range(1, n.bit_length() - 1)]
    return lax.ppermute(value, "sl", [(i, i ^ bits[(k + i % 2) % len(bits)]) for i in range(n)])


def lm_send(value, k, n_lm, n_sl):
    perm = [
        (i * n_sl + j, (i ^ (j % 2 << k)) * n_sl + j) for i in range(n_lm) for j in range(n_sl)
    ]
    return lax.ppermute(value, ("lm", "sl"), perm)


def prepare_kernel(
    land_ref, codes_ref, exponents_ref, eig_ref, first_ref, codes, eig, exponents, sems
):
    rows, feat = land_ref.shape
    half = rows // 2 - SHIFT
    ritz = eig_ref.shape[0]
    pairs = [
        (codes_ref, codes),
        (eig_ref, eig),
        (exponents_ref, exponents),
        (land_ref.at[:half], first_ref.at[:half]),
    ]
    copies = [pltpu.make_async_copy(src, dst, sems.at[k]) for k, (src, dst) in enumerate(pairs)]
    for copy in copies:
        copy.start()
    for copy in copies[:3]:
        copy.wait()
    pieces = []
    for b in range(rows // BLOCK):
        scale = lax.shift_left(jnp.int32(1), exponents[b] + 15).astype(jnp.float32) * 2.0**-15
        pieces.append(codes[:, b * BLOCK : (b + 1) * BLOCK].astype(jnp.float32) * scale)
    basis = jnp.concatenate(pieces, axis=1).astype(jnp.bfloat16)
    vectors = jnp.dot(eig[...], basis, preferred_element_type=jnp.float32).astype(jnp.bfloat16)
    chunks = feat // rows
    depth = ritz // chunks
    for c in range(chunks):
        first_ref[half:, c * rows : (c + 1) * rows] = vectors[c * depth : (c + 1) * depth, :]
    for copy in copies[3:]:
        copy.wait()


def prepare(landmarks, codes_t, exponents, eig_t):
    rows, feat = landmarks.shape
    extra = eig_t.shape[0] * rows // feat
    return pl.pallas_call(
        prepare_kernel,
        out_shape=jax.ShapeDtypeStruct((rows // 2 - SHIFT + extra, feat), jnp.bfloat16),
        in_specs=[pl.BlockSpec(memory_space=pltpu.HBM)] * 4,
        scratch_shapes=[
            pltpu.VMEM(codes_t.shape, codes_t.dtype),
            pltpu.VMEM(eig_t.shape, eig_t.dtype),
            pltpu.SMEM(exponents.shape, exponents.dtype),
            pltpu.SemaphoreType.DMA((4,)),
        ],
        compiler_params=pltpu.CompilerParams(vmem_limit_bytes=8 * MIB),
    )(*(pltpu.with_memory_space_constraint(x, pltpu.HBM) for x in (landmarks, codes_t, exponents, eig_t)))


def transpose_kernel(in_ref, out_ref):
    for k in range(in_ref.shape[0] // CHUNK):
        rows = slice(k * CHUNK, (k + 1) * CHUNK)
        out_ref[:, rows] = in_ref[rows, :].T


def stage_kernel(count, coeff, ritz, has_acc, spans, *refs):
    slabs = refs[:count]
    first_ref, second_ref = refs[count : count + 2]
    accs = refs[count + 2 : 2 * count + 2] if has_acc else [None] * count
    outs = refs[-count:]
    tail, feat = second_ref.shape
    rows = (first_ref.shape[0] + tail) * feat // (feat + ritz)
    head = rows - tail
    land = jnp.concatenate([first_ref[:head, :], second_ref[...]], axis=0)
    vec = jnp.concatenate(
        [first_ref[head:, c * rows : (c + 1) * rows] for c in range(feat // rows)], axis=0
    )
    work = [
        (k, slice(c, min(c + CHUNK, stop)))
        for k, (start, stop) in enumerate(spans)
        for c in range(start, stop, CHUNK)
    ]

    def scores(k, cols):
        return jnp.dot(land, slabs[k][:, cols], preferred_element_type=jnp.float32)

    ahead = scores(*work[0])
    for n, (k, cols) in enumerate(work):
        now, ahead = ahead, scores(*work[n + 1]) if n + 1 < len(work) else None
        affinity = jnp.exp(now * coeff).astype(jnp.bfloat16)
        term = jnp.dot(vec, affinity, preferred_element_type=jnp.float32)
        place = slice(cols.start - spans[k][0], cols.stop - spans[k][0])
        outs[k][:, place] = term if accs[k] is None else accs[k][:, cols] + term


def stage(slabs, first, second, accs, coeff, ritz, spans=None):
    feat, rows = slabs[0].shape
    land = (first.shape[0] + second.shape[0]) * feat // (feat + ritz)
    count = len(slabs)
    spans = spans or [(0, rows)] * count
    rows = spans[0][1] - spans[0][0]
    return pl.pallas_call(
        functools.partial(stage_kernel, count, coeff, ritz, accs is not None, spans),
        out_shape=[jax.ShapeDtypeStruct((ritz, rows), jnp.float32)] * count,
        compiler_params=pltpu.CompilerParams(vmem_limit_bytes=32 * MIB),
        cost_estimate=pl.CostEstimate(
            flops=2 * count * rows * land * (feat + 4 * ritz),
            bytes_accessed=2 * (count * rows + land) * feat,
            transcendentals=count * rows * land,
        ),
    )(*slabs, first, second, *(accs or []))


def add_kernel(a_ref, b_ref, out_ref):
    total = a_ref[...].astype(jnp.float32) + b_ref[...].astype(jnp.float32)
    out_ref[...] = total.astype(out_ref.dtype)


def scale_kernel(odd_refs, even_refs, ritz_ref, out_ref, *, total_land):
    factor = 1.0 / (ritz_ref[...] * math.sqrt(total_land))

    def write(refs):
        a_ref, b_ref = refs
        total = a_ref[...].astype(jnp.float32) + b_ref[...].astype(jnp.float32)
        out_ref[...] = total * factor

    odd = lax.rem(lax.axis_index("sl"), 2)
    pl.when(odd == 1)(lambda: write(odd_refs))
    pl.when(odd == 0)(lambda: write(even_refs))


def small_call(kernel, out, *args):
    return pl.pallas_call(
        kernel,
        out_shape=jax.ShapeDtypeStruct(out.shape, out.dtype),
        compiler_params=pltpu.CompilerParams(vmem_limit_bytes=8 * MIB),
    )(*args)


def local(slab, landmarks, codes, exponents, eigvec, ritz):
    n_lm, n_sl = lax.axis_size("lm"), lax.axis_size("sl")
    total_land = codes.shape[0] * n_lm * n_sl
    coeff = 1.0 / math.sqrt(slab.shape[1])
    cols = ritz.shape[0]
    rows = slab.shape[0]
    ways = n_sl.bit_length() - 2

    second = landmarks[landmarks.shape[0] // 2 - SHIFT :]
    first = prepare(landmarks, codes.T, exponents, eigvec.T)
    blocks = {0: [first, second]}
    for k in range(ways):
        blocks[1 << k] = [None, None]
    for turn in (0, 1):
        for k in range(ways):
            piece = (k + turn) % 2
            blocks[1 << k][piece] = chip_send(blocks[0][piece], k, n_sl)
    late_slab, _ = lax.optimization_barrier((slab, second))
    turned = jax.ShapeDtypeStruct(slab.shape[::-1], slab.dtype)
    other = small_call(transpose_kernel, turned, core_send(late_slab, n_sl))
    slab = small_call(transpose_kernel, turned, slab)
    (acc,) = stage([slab], first, second, None, coeff, cols)
    held = [blocks[1 << k][k % 2] for k in range(ways)]
    held, acc = lax.optimization_barrier((held, acc))
    for k in range(ways):
        blocks[1 << k][k % 2] = held[k]
    (other_acc,) = stage([other], first, second, None, coeff, cols)
    accs = [acc, other_acc]
    for t in range(1, 1 << ways):
        if t in blocks:
            continue
        low, high = (t & -t).bit_length() - 1, t.bit_length() - 1
        blocks[t] = [
            chip_send(blocks[t ^ (1 << high)][0], high, n_sl),
            chip_send(blocks[t ^ (1 << low)][1], low, n_sl),
        ]

    for t in range(1, (1 << ways) - 1):
        accs = stage([slab, other], *blocks[t], accs, coeff, cols)
    end = blocks[(1 << ways) - 1]
    (mine,) = stage([slab], *end, accs[:1], coeff, cols)
    from_even = core_send(mine, n_sl)
    (theirs,) = stage([other], *end, accs[1:], coeff, cols)
    own_from_even = core_send(theirs, n_sl)
    piece = jax.ShapeDtypeStruct((cols, rows), jnp.bfloat16)
    totals = [
        small_call(add_kernel, piece, theirs, from_even),
        small_call(add_kernel, piece, mine, own_from_even),
    ]
    turns = n_lm.bit_length() - 1
    for k in range(turns - 1):
        arrived = [lm_send(total, (k + p) % turns, n_lm, n_sl) for p, total in enumerate(totals)]
        totals = [small_call(add_kernel, piece, a, b) for a, b in zip(totals, arrived)]
    even_total = core_send(totals[0], n_sl)
    arrived = [lm_send(total, (turns - 1 + p) % turns, n_lm, n_sl) for p, total in enumerate(totals)]
    even_arrived = core_send(arrived[0], n_sl)
    scale = functools.partial(scale_kernel, total_land=total_land)
    out = jax.ShapeDtypeStruct((cols, rows), jnp.float32)
    odd_parts, even_parts = (totals[1], arrived[1]), (even_total, even_arrived)
    return small_call(scale, out, odd_parts, even_parts, ritz[:, None]).T


def solution(mesh):
    return jax.shard_map(
        local,
        mesh=mesh,
        in_specs=(
            P("sl", None),
            P(("lm", "sl"), None),
            P(("lm", "sl"), None),
            P(("lm", "sl")),
            P(),
            P(),
        ),
        out_specs=P("sl", None),
        check_vma=False,
    )
```

```python
import functools
import math

import jax
import jax.numpy as jnp
from jax import lax
from jax.experimental import pallas as pl
from jax.experimental.pallas import tpu as pltpu
from jax.sharding import PartitionSpec as P

BLOCK = 128
SHIFT = 16
CHUNK = 512
MIB = 2**20


def core_send(value, n):
    return lax.ppermute(value, "sl", [(i, i ^ 1) for i in range(n)])


def chip_send(value, k, n):
    bits = [1 << b for b in range(1, n.bit_length() - 1)]
    return lax.ppermute(value, "sl", [(i, i ^ bits[(k + i % 2) % len(bits)]) for i in range(n)])


def lm_send(value, k, n_lm, n_sl):
    bits = [1 << b for b in range(n_lm.bit_length() - 1)]
    perm = [
        (i * n_sl + j, (i ^ bits[(k + j % 2) % len(bits)]) * n_sl + j)
        for i in range(n_lm)
        for j in range(n_sl)
    ]
    return lax.ppermute(value, ("lm", "sl"), perm)


def prepare_kernel(
    land_ref, codes_ref, exponents_ref, eig_ref, first_ref, codes, eig, exponents, sems
):
    rows, feat = land_ref.shape
    half = rows // 2 - SHIFT
    ritz = eig_ref.shape[0]
    pairs = [
        (codes_ref, codes),
        (eig_ref, eig),
        (exponents_ref, exponents),
        (land_ref.at[:half], first_ref.at[:half]),
    ]
    copies = [pltpu.make_async_copy(src, dst, sems.at[k]) for k, (src, dst) in enumerate(pairs)]
    for copy in copies:
        copy.start()
    for copy in copies[:3]:
        copy.wait()
    pieces = []
    for b in range(rows // BLOCK):
        scale = lax.shift_left(jnp.int32(1), exponents[b] + 15).astype(jnp.float32) * 2.0**-15
        pieces.append(codes[:, b * BLOCK : (b + 1) * BLOCK].astype(jnp.float32) * scale)
    basis = jnp.concatenate(pieces, axis=1).astype(jnp.bfloat16)
    vectors = jnp.dot(eig[...], basis, preferred_element_type=jnp.float32).astype(jnp.bfloat16)
    chunks = feat // rows
    depth = ritz // chunks
    for c in range(chunks):
        first_ref[half:, c * rows : (c + 1) * rows] = vectors[c * depth : (c + 1) * depth, :]
    for copy in copies[3:]:
        copy.wait()


def prepare(landmarks, codes_t, exponents, eig_t):
    rows, feat = landmarks.shape
    extra = eig_t.shape[0] * rows // feat
    return pl.pallas_call(
        prepare_kernel,
        out_shape=jax.ShapeDtypeStruct((rows // 2 - SHIFT + extra, feat), jnp.bfloat16),
        in_specs=[pl.BlockSpec(memory_space=pltpu.HBM)] * 4,
        scratch_shapes=[
            pltpu.VMEM(codes_t.shape, codes_t.dtype),
            pltpu.VMEM(eig_t.shape, eig_t.dtype),
            pltpu.SMEM(exponents.shape, exponents.dtype),
            pltpu.SemaphoreType.DMA((4,)),
        ],
        compiler_params=pltpu.CompilerParams(vmem_limit_bytes=8 * MIB),
    )(*(pltpu.with_memory_space_constraint(x, pltpu.HBM) for x in (landmarks, codes_t, exponents, eig_t)))


def transpose_kernel(in_ref, out_ref):
    for k in range(in_ref.shape[0] // CHUNK):
        rows = slice(k * CHUNK, (k + 1) * CHUNK)
        out_ref[:, rows] = in_ref[rows, :].T


def stage_kernel(count, coeff, ritz, has_acc, spans, rows, use, *refs):
    refs = list(refs)
    slabs = [refs.pop(0) for _ in range(count)]
    first_ref = refs.pop(0)
    second_ref = refs.pop(0) if use[1] else None
    accs = [refs.pop(0) for _ in range(count)] if has_acc else [None] * count
    outs = refs
    feat = first_ref.shape[1]
    head = first_ref.shape[0] - ritz * rows // feat
    lands = [first_ref[:head, :]] if use[0] else []
    if second_ref is not None:
        lands.append(second_ref[...])
    land = jnp.concatenate(lands, axis=0) if len(lands) > 1 else lands[0]
    vec = jnp.concatenate(
        [first_ref[head:, c * rows : (c + 1) * rows] for c in range(feat // rows)], axis=0
    )
    work = [
        (k, slice(c, min(c + CHUNK, stop)))
        for k, (start, stop) in enumerate(spans)
        for c in range(start, stop, CHUNK)
    ]

    def scores(k, cols):
        return jnp.dot(land, slabs[k][:, cols], preferred_element_type=jnp.float32)

    ahead = scores(*work[0])
    for n, (k, cols) in enumerate(work):
        now, ahead = ahead, scores(*work[n + 1]) if n + 1 < len(work) else None
        affinity = jnp.exp(now * coeff).astype(jnp.bfloat16)
        width = cols.stop - cols.start
        if not use[0]:
            affinity = jnp.concatenate([jnp.zeros((head, width), jnp.bfloat16), affinity], axis=0)
        elif not use[1]:
            blank = jnp.zeros((rows - head, width), jnp.bfloat16)
            affinity = jnp.concatenate([affinity, blank], axis=0)
        term = jnp.dot(vec, affinity, preferred_element_type=jnp.float32)
        place = slice(cols.start - spans[k][0], cols.stop - spans[k][0])
        outs[k][:, place] = term if accs[k] is None else accs[k][:, cols] + term


def stage(slabs, block, accs, coeff, ritz, size, use=(True, True), spans=None):
    feat, rows = slabs[0].shape
    first, second = block
    count = len(slabs)
    spans = spans or [(0, rows)] * count
    rows = spans[0][1] - spans[0][0]
    args = [*slabs, first]
    if use[1]:
        args.append(second)
    return pl.pallas_call(
        functools.partial(stage_kernel, count, coeff, ritz, accs is not None, spans, size, use),
        out_shape=[jax.ShapeDtypeStruct((ritz, rows), jnp.float32)] * count,
        compiler_params=pltpu.CompilerParams(vmem_limit_bytes=32 * MIB),
        cost_estimate=pl.CostEstimate(
            flops=2 * count * rows * size * (feat + 4 * ritz),
            bytes_accessed=2 * (count * rows + size) * feat,
            transcendentals=count * rows * size,
        ),
    )(*args, *(accs or []))


def add_kernel(a_ref, b_ref, out_ref):
    total = a_ref[...].astype(jnp.float32) + b_ref[...].astype(jnp.float32)
    out_ref[...] = total.astype(out_ref.dtype)


def scale_kernel(*refs, total_land):
    ritz_ref, out_ref = refs[-2:]
    factor = 1.0 / (ritz_ref[...] * math.sqrt(total_land))
    start = 0
    for a_ref, b_ref in zip(refs[0:-2:2], refs[1:-2:2]):
        stop = start + a_ref.shape[1]
        total = a_ref[...].astype(jnp.float32) + b_ref[...].astype(jnp.float32)
        out_ref[:, start:stop] = total * factor
        start = stop


def small_call(kernel, out, *args):
    return pl.pallas_call(
        kernel,
        out_shape=jax.ShapeDtypeStruct(out.shape, out.dtype),
        compiler_params=pltpu.CompilerParams(vmem_limit_bytes=8 * MIB),
    )(*args)


def local(slab, landmarks, codes, exponents, eigvec, ritz):
    n_lm, n_sl = lax.axis_size("lm"), lax.axis_size("sl")
    total_land = codes.shape[0] * n_lm * n_sl
    coeff = 1.0 / math.sqrt(slab.shape[1])
    cols = ritz.shape[0]
    rows = slab.shape[0]
    ways = n_sl.bit_length() - 2
    size = landmarks.shape[0]

    second = landmarks[landmarks.shape[0] // 2 - SHIFT :]
    first = prepare(landmarks, codes.T, exponents, eigvec.T)
    blocks = {0: [first, second]}
    for k in range(ways):
        blocks[1 << k] = [None, None]
    for turn in (0, 1):
        for k in range(ways):
            piece = (k + turn) % 2
            blocks[1 << k][piece] = chip_send(blocks[0][piece], k, n_sl)
    late_slab, _ = lax.optimization_barrier((slab, second))
    turned = jax.ShapeDtypeStruct(slab.shape[::-1], slab.dtype)
    other = small_call(transpose_kernel, turned, core_send(late_slab, n_sl))
    slab = small_call(transpose_kernel, turned, slab)
    (acc,) = stage([slab], blocks[0], None, coeff, cols, size)
    held = [blocks[1 << k][k % 2] for k in range(ways)]
    held, acc = lax.optimization_barrier((held, acc))
    for k in range(ways):
        blocks[1 << k][k % 2] = held[k]
    (other_acc,) = stage([other], blocks[0], None, coeff, cols, size)
    accs = [acc, other_acc]
    for t in range(1, 1 << ways):
        if t in blocks:
            continue
        low, high = (t & -t).bit_length() - 1, t.bit_length() - 1
        blocks[t] = [
            chip_send(blocks[t ^ (1 << high)][0], high, n_sl),
            chip_send(blocks[t ^ (1 << low)][1], low, n_sl),
        ]

    for t in range(1, (1 << ways) - 1):
        accs = stage([slab, other], blocks[t], accs, coeff, cols, size)
    block = blocks[(1 << ways) - 1]
    accs = stage([slab, other], block, accs, coeff, cols, size, (True, False))
    end = functools.partial(stage, coeff=coeff, ritz=cols, size=size, use=(False, True))
    width = rows // 2
    spans = [(0, width), (width, rows)]
    half = jax.ShapeDtypeStruct((cols, width), jnp.bfloat16)
    (early,) = end([other], block, accs[1:], spans=spans[:1])
    received = [core_send(early, n_sl)]
    late, mine = end([other, slab], block, accs[::-1], spans=spans[::-1])
    received.append(core_send(late, n_sl))
    total = small_call(add_kernel, half, mine, received[0])
    acc, total = lax.optimization_barrier((accs[0], total))
    (mine,) = end([slab], block, [acc], spans=spans[1:])
    totals = [total, small_call(add_kernel, half, mine, received[1])]
    turns = n_lm.bit_length() - 1
    for k in range(turns - 1):
        arrived = [lm_send(total, k, n_lm, n_sl) for total in totals]
        totals = [small_call(add_kernel, half, a, b) for a, b in zip(totals, arrived)]
    pairs = [(total, lm_send(total, turns - 1, n_lm, n_sl)) for total in totals]
    scale = functools.partial(scale_kernel, total_land=total_land)
    out = jax.ShapeDtypeStruct((cols, rows), jnp.float32)
    return small_call(scale, out, *(x for pair in pairs for x in pair), ritz[:, None]).T


def solution(mesh):
    return jax.shard_map(
        local,
        mesh=mesh,
        in_specs=(
            P("sl", None),
            P(("lm", "sl"), None),
            P(("lm", "sl"), None),
            P(("lm", "sl")),
            P(),
            P(),
        ),
        out_specs=P("sl", None),
        check_vma=False,
    )
```

```python
import functools
import math

import jax
import jax.numpy as jnp
from jax import lax
from jax.experimental import pallas as pl
from jax.experimental.pallas import tpu as pltpu
from jax.sharding import PartitionSpec as P

BLOCK = 128
SHIFT = 16
CHUNK = 512
MIB = 2**20


def core_send(value, n):
    return lax.ppermute(value, "sl", [(i, i ^ 1) for i in range(n)])


def chip_send(value, k, n):
    bits = [1 << b for b in range(1, n.bit_length() - 1)]
    return lax.ppermute(value, "sl", [(i, i ^ bits[(k + i % 2) % len(bits)]) for i in range(n)])


def lm_send(value, k, n_lm, n_sl):
    bits = [1 << b for b in range(n_lm.bit_length() - 1)]
    perm = [
        (i * n_sl + j, (i ^ bits[(k + j % 2) % len(bits)]) * n_sl + j)
        for i in range(n_lm)
        for j in range(n_sl)
    ]
    return lax.ppermute(value, ("lm", "sl"), perm)


def prepare_kernel(
    land_ref, codes_ref, exponents_ref, eig_ref, first_ref, vec_ref, codes, eig, exponents, sems
):
    rows, feat = land_ref.shape
    half = rows // 2 - SHIFT
    ritz = eig_ref.shape[0]
    pairs = [
        (codes_ref, codes),
        (eig_ref, eig),
        (exponents_ref, exponents),
        (land_ref.at[:half], first_ref.at[:half]),
    ]
    copies = [pltpu.make_async_copy(src, dst, sems.at[k]) for k, (src, dst) in enumerate(pairs)]
    for copy in copies:
        copy.start()
    for copy in copies[:3]:
        copy.wait()
    pieces = []
    for b in range(rows // BLOCK):
        scale = lax.shift_left(jnp.int32(1), exponents[b] + 15).astype(jnp.float32) * 2.0**-15
        pieces.append(codes[:, b * BLOCK : (b + 1) * BLOCK].astype(jnp.float32) * scale)
    basis = jnp.concatenate(pieces, axis=1).astype(jnp.bfloat16)
    vectors = jnp.dot(eig[...], basis, preferred_element_type=jnp.float32).astype(jnp.bfloat16)
    chunks = feat // rows
    depth = ritz // chunks
    for c in range(chunks):
        part = vectors[c * depth : (c + 1) * depth, :]
        first_ref[half:, c * rows : (c + 1) * rows] = part
        vec_ref[:, c * rows : (c + 1) * rows] = part
    for copy in copies[3:]:
        copy.wait()


def prepare(landmarks, codes_t, exponents, eig_t):
    rows, feat = landmarks.shape
    extra = eig_t.shape[0] * rows // feat
    return pl.pallas_call(
        prepare_kernel,
        out_shape=[
            jax.ShapeDtypeStruct((rows // 2 - SHIFT + extra, feat), jnp.bfloat16),
            jax.ShapeDtypeStruct((extra, feat), jnp.bfloat16),
        ],
        in_specs=[pl.BlockSpec(memory_space=pltpu.HBM)] * 4,
        scratch_shapes=[
            pltpu.VMEM(codes_t.shape, codes_t.dtype),
            pltpu.VMEM(eig_t.shape, eig_t.dtype),
            pltpu.SMEM(exponents.shape, exponents.dtype),
            pltpu.SemaphoreType.DMA((4,)),
        ],
        compiler_params=pltpu.CompilerParams(vmem_limit_bytes=8 * MIB),
    )(*(pltpu.with_memory_space_constraint(x, pltpu.HBM) for x in (landmarks, codes_t, exponents, eig_t)))


def cut_first_kernel(land_ref, vec_ref, out_ref):
    head = out_ref.shape[0] - vec_ref.shape[0]
    out_ref[:head, :] = land_ref[:head, :]
    out_ref[head:, :] = vec_ref[...]


def cut_second_kernel(land_ref, out_ref):
    out_ref[...] = land_ref[land_ref.shape[0] - out_ref.shape[0] :, :]


def transpose_kernel(in_ref, out_ref):
    for k in range(in_ref.shape[0] // CHUNK):
        rows = slice(k * CHUNK, (k + 1) * CHUNK)
        out_ref[:, rows] = in_ref[rows, :].T


def stage_kernel(count, coeff, ritz, has_acc, spans, *refs):
    slabs = refs[:count]
    first_ref, second_ref = refs[count : count + 2]
    accs = refs[count + 2 : 2 * count + 2] if has_acc else [None] * count
    outs = refs[-count:]
    tail, feat = second_ref.shape
    rows = (first_ref.shape[0] + tail) * feat // (feat + ritz)
    head = rows - tail
    land = second_ref[...]
    if head:
        land = jnp.concatenate([first_ref[:head, :], land], axis=0)
    vec = jnp.concatenate(
        [first_ref[head:, c * rows : (c + 1) * rows] for c in range(feat // rows)], axis=0
    )
    work = [
        (k, slice(c, min(c + CHUNK, stop)))
        for k, (start, stop) in enumerate(spans)
        for c in range(start, stop, CHUNK)
    ]

    def scores(k, cols):
        return jnp.dot(land, slabs[k][:, cols], preferred_element_type=jnp.float32)

    ahead = scores(*work[0])
    for n, (k, cols) in enumerate(work):
        now, ahead = ahead, scores(*work[n + 1]) if n + 1 < len(work) else None
        affinity = jnp.exp(now * coeff).astype(jnp.bfloat16)
        term = jnp.dot(vec, affinity, preferred_element_type=jnp.float32)
        place = slice(cols.start - spans[k][0], cols.stop - spans[k][0])
        outs[k][:, place] = term if accs[k] is None else accs[k][:, cols] + term


def stage(slabs, first, second, accs, coeff, ritz, spans=None):
    feat, rows = slabs[0].shape
    land = (first.shape[0] + second.shape[0]) * feat // (feat + ritz)
    count = len(slabs)
    spans = spans or [(0, rows)] * count
    rows = spans[0][1] - spans[0][0]
    return pl.pallas_call(
        functools.partial(stage_kernel, count, coeff, ritz, accs is not None, spans),
        out_shape=[jax.ShapeDtypeStruct((ritz, rows), jnp.float32)] * count,
        compiler_params=pltpu.CompilerParams(vmem_limit_bytes=32 * MIB),
        cost_estimate=pl.CostEstimate(
            flops=2 * count * rows * land * (feat + 4 * ritz),
            bytes_accessed=2 * (count * rows + land) * feat,
            transcendentals=count * rows * land,
        ),
    )(*slabs, first, second, *(accs or []))


def add_kernel(a_ref, b_ref, out_ref):
    total = a_ref[...].astype(jnp.float32) + b_ref[...].astype(jnp.float32)
    out_ref[...] = total.astype(out_ref.dtype)


def scale_kernel(*refs, total_land):
    ritz_ref, out_ref = refs[-2:]
    factor = 1.0 / (ritz_ref[...] * math.sqrt(total_land))
    start = 0
    for a_ref, b_ref in zip(refs[0:-2:2], refs[1:-2:2]):
        stop = start + a_ref.shape[1]
        total = a_ref[...].astype(jnp.float32) + b_ref[...].astype(jnp.float32)
        out_ref[:, start:stop] = total * factor
        start = stop


def small_call(kernel, out, *args):
    return pl.pallas_call(
        kernel,
        out_shape=jax.ShapeDtypeStruct(out.shape, out.dtype),
        compiler_params=pltpu.CompilerParams(vmem_limit_bytes=8 * MIB),
    )(*args)


def local(slab, landmarks, codes, exponents, eigvec, ritz):
    n_lm, n_sl = lax.axis_size("lm"), lax.axis_size("sl")
    total_land = codes.shape[0] * n_lm * n_sl
    coeff = 1.0 / math.sqrt(slab.shape[1])
    cols = ritz.shape[0]
    rows = slab.shape[0]
    ways = n_sl.bit_length() - 2

    first, vectors = prepare(landmarks, codes.T, exponents, eigvec.T)
    second = landmarks[landmarks.shape[0] // 2 - SHIFT :]
    whole = {k: chip_send(landmarks, k, n_sl) for k in range(1, ways, 2)}
    other = core_send(slab, n_sl)
    blocks, parts = {}, {}
    for k in range(0, ways, 2):
        blocks[1 << k] = [chip_send(first, k, n_sl), None]
    for k in range(0, ways, 2):
        blocks[1 << k][1] = chip_send(second, k, n_sl)
    turned = jax.ShapeDtypeStruct(slab.shape[::-1], slab.dtype)
    other = small_call(transpose_kernel, turned, other)
    slab = small_call(transpose_kernel, turned, slab)
    (acc,) = stage([slab], first, second, None, coeff, cols)
    heads = [blocks[1 << k][0] for k in range(0, ways, 2)]
    heads, whole, acc = lax.optimization_barrier((heads, whole, acc))
    for k in range(0, ways, 2):
        blocks[1 << k][0] = heads[k // 2]
    for k in range(1, ways, 2):
        vec = chip_send(vectors, k, n_sl)
        parts[1 << k] = [vec, whole[k]]
        blocks[1 << k] = [
            small_call(cut_first_kernel, first, whole[k], vec),
            small_call(cut_second_kernel, second, whole[k]),
        ]
    (other_acc,) = stage([other], first, second, None, coeff, cols)
    accs = [acc, other_acc]
    for t in range(1, 1 << ways):
        if t in blocks:
            continue
        low, high = (t & -t).bit_length() - 1, t.bit_length() - 1
        blocks[t] = [
            chip_send(blocks[t ^ (1 << high)][0], high, n_sl),
            chip_send(blocks[t ^ (1 << low)][1], low, n_sl),
        ]

    for t in range(1, (1 << ways) - 1):
        accs = stage([slab, other], *parts.get(t, blocks[t]), accs, coeff, cols)
    end = blocks[(1 << ways) - 1]
    width = rows // 2
    spans = [(0, width), (width, rows)]
    half = jax.ShapeDtypeStruct((cols, width), jnp.bfloat16)
    (early,) = stage([other], *end, accs[1:], coeff, cols, spans[:1])
    received = [core_send(early, n_sl)]
    late, mine = stage([other, slab], *end, accs[::-1], coeff, cols, spans[::-1])
    received.append(core_send(late, n_sl))
    total = small_call(add_kernel, half, mine, received[0])
    acc, total = lax.optimization_barrier((accs[0], total))
    (mine,) = stage([slab], *end, [acc], coeff, cols, spans[1:])
    totals = [total, small_call(add_kernel, half, mine, received[1])]
    turns = n_lm.bit_length() - 1
    for k in range(turns - 1):
        arrived = [lm_send(total, k, n_lm, n_sl) for total in totals]
        totals = [small_call(add_kernel, half, a, b) for a, b in zip(totals, arrived)]
    pairs = [(total, lm_send(total, turns - 1, n_lm, n_sl)) for total in totals]
    scale = functools.partial(scale_kernel, total_land=total_land)
    out = jax.ShapeDtypeStruct((cols, rows), jnp.float32)
    return small_call(scale, out, *(x for pair in pairs for x in pair), ritz[:, None]).T


def solution(mesh):
    return jax.shard_map(
        local,
        mesh=mesh,
        in_specs=(
            P("sl", None),
            P(("lm", "sl"), None),
            P(("lm", "sl"), None),
            P(("lm", "sl")),
            P(),
            P(),
        ),
        out_specs=P("sl", None),
        check_vma=False,
    )
```

```python
import functools
import math

import jax
import jax.numpy as jnp
from jax import lax
from jax.experimental import pallas as pl
from jax.experimental.pallas import tpu as pltpu
from jax.sharding import PartitionSpec as P

BLOCK = 128
SHIFT = 16
CHUNK = 512
MIB = 2**20


def core_send(value, n):
    return lax.ppermute(value, "sl", [(i, i ^ 1) for i in range(n)])


def chip_send(value, k, n):
    bits = [1 << b for b in range(1, n.bit_length() - 1)]
    return lax.ppermute(value, "sl", [(i, i ^ bits[(k + i % 2) % len(bits)]) for i in range(n)])


def lm_send(value, k, n_lm, n_sl):
    bits = [1 << b for b in range(n_lm.bit_length() - 1)]
    perm = [
        (i * n_sl + j, (i ^ bits[(k + j % 2) % len(bits)]) * n_sl + j)
        for i in range(n_lm)
        for j in range(n_sl)
    ]
    return lax.ppermute(value, ("lm", "sl"), perm)


def prepare_kernel(
    land_ref, codes_ref, exponents_ref, eig_ref, first_ref, codes, eig, exponents, sems
):
    rows, feat = land_ref.shape
    half = rows // 2 - SHIFT
    ritz = eig_ref.shape[0]
    pairs = [
        (codes_ref, codes),
        (eig_ref, eig),
        (exponents_ref, exponents),
        (land_ref.at[:half], first_ref.at[:half]),
    ]
    copies = [pltpu.make_async_copy(src, dst, sems.at[k]) for k, (src, dst) in enumerate(pairs)]
    for copy in copies:
        copy.start()
    for copy in copies[:3]:
        copy.wait()
    pieces = []
    for b in range(rows // BLOCK):
        scale = lax.shift_left(jnp.int32(1), exponents[b] + 15).astype(jnp.float32) * 2.0**-15
        pieces.append(codes[:, b * BLOCK : (b + 1) * BLOCK].astype(jnp.float32) * scale)
    basis = jnp.concatenate(pieces, axis=1).astype(jnp.bfloat16)
    vectors = jnp.dot(eig[...], basis, preferred_element_type=jnp.float32).astype(jnp.bfloat16)
    chunks = feat // rows
    depth = ritz // chunks
    for c in range(chunks):
        first_ref[half:, c * rows : (c + 1) * rows] = vectors[c * depth : (c + 1) * depth, :]
    for copy in copies[3:]:
        copy.wait()


def prepare(landmarks, codes_t, exponents, eig_t):
    rows, feat = landmarks.shape
    extra = eig_t.shape[0] * rows // feat
    return pl.pallas_call(
        prepare_kernel,
        out_shape=jax.ShapeDtypeStruct((rows // 2 - SHIFT + extra, feat), jnp.bfloat16),
        in_specs=[pl.BlockSpec(memory_space=pltpu.HBM)] * 4,
        scratch_shapes=[
            pltpu.VMEM(codes_t.shape, codes_t.dtype),
            pltpu.VMEM(eig_t.shape, eig_t.dtype),
            pltpu.SMEM(exponents.shape, exponents.dtype),
            pltpu.SemaphoreType.DMA((4,)),
        ],
        compiler_params=pltpu.CompilerParams(vmem_limit_bytes=8 * MIB),
    )(*(pltpu.with_memory_space_constraint(x, pltpu.HBM) for x in (landmarks, codes_t, exponents, eig_t)))


def transpose_kernel(in_ref, out_ref):
    for k in range(in_ref.shape[0] // CHUNK):
        rows = slice(k * CHUNK, (k + 1) * CHUNK)
        out_ref[:, rows] = in_ref[rows, :].T


def stage_kernel(count, coeff, ritz, has_acc, spans, *refs):
    slabs = refs[:count]
    first_ref, second_ref = refs[count : count + 2]
    accs = refs[count + 2 : 2 * count + 2] if has_acc else [None] * count
    outs = refs[-count:]
    tail, feat = second_ref.shape
    rows = (first_ref.shape[0] + tail) * feat // (feat + ritz)
    head = rows - tail
    land = jnp.concatenate([first_ref[:head, :], second_ref[...]], axis=0)
    vec = jnp.concatenate(
        [first_ref[head:, c * rows : (c + 1) * rows] for c in range(feat // rows)], axis=0
    )
    work = [
        (k, slice(c, min(c + CHUNK, stop)))
        for k, (start, stop) in enumerate(spans)
        for c in range(start, stop, CHUNK)
    ]

    def scores(k, cols):
        return jnp.dot(land, slabs[k][:, cols], preferred_element_type=jnp.float32)

    ahead = scores(*work[0])
    for n, (k, cols) in enumerate(work):
        now, ahead = ahead, scores(*work[n + 1]) if n + 1 < len(work) else None
        affinity = jnp.exp(now * coeff).astype(jnp.bfloat16)
        term = jnp.dot(vec, affinity, preferred_element_type=jnp.float32)
        place = slice(cols.start - spans[k][0], cols.stop - spans[k][0])
        outs[k][:, place] = term if accs[k] is None else accs[k][:, cols] + term


def stage(slabs, first, second, accs, coeff, ritz, spans=None):
    feat, rows = slabs[0].shape
    land = (first.shape[0] + second.shape[0]) * feat // (feat + ritz)
    count = len(slabs)
    spans = spans or [(0, rows)] * count
    rows = spans[0][1] - spans[0][0]
    return pl.pallas_call(
        functools.partial(stage_kernel, count, coeff, ritz, accs is not None, spans),
        out_shape=[jax.ShapeDtypeStruct((ritz, rows), jnp.float32)] * count,
        compiler_params=pltpu.CompilerParams(vmem_limit_bytes=32 * MIB),
        cost_estimate=pl.CostEstimate(
            flops=2 * count * rows * land * (feat + 4 * ritz),
            bytes_accessed=2 * (count * rows + land) * feat,
            transcendentals=count * rows * land,
        ),
    )(*slabs, first, second, *(accs or []))


def add_kernel(a_ref, b_ref, out_ref):
    total = a_ref[...].astype(jnp.float32) + b_ref[...].astype(jnp.float32)
    out_ref[...] = total.astype(out_ref.dtype)


def scale_kernel(*refs, total_land):
    ritz_ref, out_ref = refs[-2:]
    factor = 1.0 / (ritz_ref[...] * math.sqrt(total_land))
    start = 0
    for a_ref, b_ref in zip(refs[0:-2:2], refs[1:-2:2]):
        stop = start + a_ref.shape[1]
        total = a_ref[...].astype(jnp.float32) + b_ref[...].astype(jnp.float32)
        out_ref[:, start:stop] = total * factor
        start = stop


def small_call(kernel, out, *args):
    return pl.pallas_call(
        kernel,
        out_shape=jax.ShapeDtypeStruct(out.shape, out.dtype),
        compiler_params=pltpu.CompilerParams(vmem_limit_bytes=8 * MIB),
    )(*args)


def local(slab, landmarks, codes, exponents, eigvec, ritz):
    n_lm, n_sl = lax.axis_size("lm"), lax.axis_size("sl")
    total_land = codes.shape[0] * n_lm * n_sl
    coeff = 1.0 / math.sqrt(slab.shape[1])
    cols = ritz.shape[0]
    rows = slab.shape[0]
    ways = n_sl.bit_length() - 2

    second = landmarks[landmarks.shape[0] // 2 - SHIFT :]
    first = prepare(landmarks, codes.T, exponents, eigvec.T)
    blocks = {0: [first, second]}
    for k in range(ways):
        blocks[1 << k] = [None, None]
    for turn in (0, 1):
        for k in range(ways):
            piece = (k + turn) % 2
            blocks[1 << k][piece] = chip_send(blocks[0][piece], k, n_sl)
    late_slab, _ = lax.optimization_barrier((slab, second))
    turned = jax.ShapeDtypeStruct(slab.shape[::-1], slab.dtype)
    other = small_call(transpose_kernel, turned, core_send(late_slab, n_sl))
    slab = small_call(transpose_kernel, turned, slab)
    (acc,) = stage([slab], first, second, None, coeff, cols)
    held = [blocks[1 << k][k % 2] for k in range(ways)]
    held, acc = lax.optimization_barrier((held, acc))
    for k in range(ways):
        blocks[1 << k][k % 2] = held[k]
    (other_acc,) = stage([other], first, second, None, coeff, cols)
    accs = [acc, other_acc]
    for t in range(1, 1 << ways):
        if t in blocks:
            continue
        low, high = (t & -t).bit_length() - 1, t.bit_length() - 1
        blocks[t] = [
            chip_send(blocks[t ^ (1 << high)][0], high, n_sl),
            chip_send(blocks[t ^ (1 << low)][1], low, n_sl),
        ]

    for t in range(1, (1 << ways) - 1):
        accs = stage([slab, other], *blocks[t], accs, coeff, cols)
    end = blocks[(1 << ways) - 1]
    width = rows // 2
    spans = [(0, width), (width, rows)]
    half = jax.ShapeDtypeStruct((cols, width), jnp.bfloat16)
    (early,) = stage([other], *end, accs[1:], coeff, cols, spans[:1])
    received = [core_send(early, n_sl)]
    late, mine = stage([other, slab], *end, accs[::-1], coeff, cols, spans[::-1])
    received.append(core_send(late, n_sl))
    total = small_call(add_kernel, half, mine, received[0])
    acc, total = lax.optimization_barrier((accs[0], total))
    (mine,) = stage([slab], *end, [acc], coeff, cols, spans[1:])
    totals = [total, small_call(add_kernel, half, mine, received[1])]
    turns = n_lm.bit_length() - 1
    for k in range(turns - 1):
        arrived = [lm_send(total, k + h, n_lm, n_sl) for h, total in enumerate(totals)]
        totals = [small_call(add_kernel, half, a, b) for a, b in zip(totals, arrived)]
    last = [lm_send(total, turns - 1 + h, n_lm, n_sl) for h, total in enumerate(totals)]
    pairs = list(zip(totals, last))
    scale = functools.partial(scale_kernel, total_land=total_land)
    out = jax.ShapeDtypeStruct((cols, rows), jnp.float32)
    return small_call(scale, out, *(x for pair in pairs for x in pair), ritz[:, None]).T


def solution(mesh):
    return jax.shard_map(
        local,
        mesh=mesh,
        in_specs=(
            P("sl", None),
            P(("lm", "sl"), None),
            P(("lm", "sl"), None),
            P(("lm", "sl")),
            P(),
            P(),
        ),
        out_specs=P("sl", None),
        check_vma=False,
    )
```

```python
import functools
import math

import jax
import jax.numpy as jnp
from jax import lax
from jax.experimental import pallas as pl
from jax.experimental.pallas import tpu as pltpu
from jax.sharding import PartitionSpec as P

BLOCK = 128
SHIFT = 16
CHUNK = 512
MIB = 2**20


def core_send(value, n):
    return lax.ppermute(value, "sl", [(i, i ^ 1) for i in range(n)])


def chip_send(value, k, n):
    bits = [1 << b for b in range(1, n.bit_length() - 1)]
    return lax.ppermute(value, "sl", [(i, i ^ bits[(k + i % 2) % len(bits)]) for i in range(n)])


def lm_send(value, k, n_lm, n_sl):
    bits = [1 << b for b in range(n_lm.bit_length() - 1)]
    perm = [
        (i * n_sl + j, (i ^ bits[(k + j % 2) % len(bits)]) * n_sl + j)
        for i in range(n_lm)
        for j in range(n_sl)
    ]
    return lax.ppermute(value, ("lm", "sl"), perm)


def prepare_kernel(
    land_ref, codes_ref, exponents_ref, eig_ref, first_ref, codes, eig, exponents, sems
):
    rows, feat = land_ref.shape
    half = rows // 2 - SHIFT
    ritz = eig_ref.shape[0]
    pairs = [
        (codes_ref, codes),
        (eig_ref, eig),
        (exponents_ref, exponents),
        (land_ref.at[:half], first_ref.at[:half]),
    ]
    copies = [pltpu.make_async_copy(src, dst, sems.at[k]) for k, (src, dst) in enumerate(pairs)]
    for copy in copies:
        copy.start()
    for copy in copies[:3]:
        copy.wait()
    pieces = []
    for b in range(rows // BLOCK):
        scale = lax.shift_left(jnp.int32(1), exponents[b] + 15).astype(jnp.float32) * 2.0**-15
        pieces.append(codes[:, b * BLOCK : (b + 1) * BLOCK].astype(jnp.float32) * scale)
    basis = jnp.concatenate(pieces, axis=1).astype(jnp.bfloat16)
    vectors = jnp.dot(eig[...], basis, preferred_element_type=jnp.float32).astype(jnp.bfloat16)
    chunks = feat // rows
    depth = ritz // chunks
    for c in range(chunks):
        first_ref[half:, c * rows : (c + 1) * rows] = vectors[c * depth : (c + 1) * depth, :]
    for copy in copies[3:]:
        copy.wait()


def tail_kernel(land_ref, out_ref, sem):
    copy = pltpu.make_async_copy(land_ref.at[land_ref.shape[0] - out_ref.shape[0] :], out_ref, sem)
    copy.start()
    copy.wait()


def second_half(landmarks):
    rows, feat = landmarks.shape
    return pl.pallas_call(
        tail_kernel,
        out_shape=jax.ShapeDtypeStruct((rows // 2 + SHIFT, feat), jnp.bfloat16),
        in_specs=[pl.BlockSpec(memory_space=pltpu.HBM)],
        scratch_shapes=[pltpu.SemaphoreType.DMA],
        compiler_params=pltpu.CompilerParams(vmem_limit_bytes=8 * MIB),
    )(pltpu.with_memory_space_constraint(landmarks, pltpu.HBM))


def prepare(landmarks, codes_t, exponents, eig_t):
    rows, feat = landmarks.shape
    extra = eig_t.shape[0] * rows // feat
    return pl.pallas_call(
        prepare_kernel,
        out_shape=jax.ShapeDtypeStruct((rows // 2 - SHIFT + extra, feat), jnp.bfloat16),
        in_specs=[pl.BlockSpec(memory_space=pltpu.HBM)] * 4,
        scratch_shapes=[
            pltpu.VMEM(codes_t.shape, codes_t.dtype),
            pltpu.VMEM(eig_t.shape, eig_t.dtype),
            pltpu.SMEM(exponents.shape, exponents.dtype),
            pltpu.SemaphoreType.DMA((4,)),
        ],
        compiler_params=pltpu.CompilerParams(vmem_limit_bytes=8 * MIB),
    )(*(pltpu.with_memory_space_constraint(x, pltpu.HBM) for x in (landmarks, codes_t, exponents, eig_t)))


def transpose_kernel(in_ref, out_ref):
    for k in range(in_ref.shape[0] // CHUNK):
        rows = slice(k * CHUNK, (k + 1) * CHUNK)
        out_ref[:, rows] = in_ref[rows, :].T


def stage_kernel(count, coeff, ritz, has_acc, spans, *refs):
    slabs = refs[:count]
    first_ref, second_ref = refs[count : count + 2]
    accs = refs[count + 2 : 2 * count + 2] if has_acc else [None] * count
    outs = refs[-count:]
    tail, feat = second_ref.shape
    rows = (first_ref.shape[0] + tail) * feat // (feat + ritz)
    head = rows - tail
    land = jnp.concatenate([first_ref[:head, :], second_ref[...]], axis=0)
    vec = jnp.concatenate(
        [first_ref[head:, c * rows : (c + 1) * rows] for c in range(feat // rows)], axis=0
    )
    work = [
        (k, slice(c, min(c + CHUNK, stop)))
        for k, (start, stop) in enumerate(spans)
        for c in range(start, stop, CHUNK)
    ]

    def scores(k, cols):
        return jnp.dot(land, slabs[k][:, cols], preferred_element_type=jnp.float32)

    ahead = scores(*work[0])
    for n, (k, cols) in enumerate(work):
        now, ahead = ahead, scores(*work[n + 1]) if n + 1 < len(work) else None
        affinity = jnp.exp(now * coeff).astype(jnp.bfloat16)
        term = jnp.dot(vec, affinity, preferred_element_type=jnp.float32)
        place = slice(cols.start - spans[k][0], cols.stop - spans[k][0])
        outs[k][:, place] = term if accs[k] is None else accs[k][:, cols] + term


def stage(slabs, first, second, accs, coeff, ritz, spans=None):
    feat, rows = slabs[0].shape
    land = (first.shape[0] + second.shape[0]) * feat // (feat + ritz)
    count = len(slabs)
    spans = spans or [(0, rows)] * count
    rows = spans[0][1] - spans[0][0]
    return pl.pallas_call(
        functools.partial(stage_kernel, count, coeff, ritz, accs is not None, spans),
        out_shape=[jax.ShapeDtypeStruct((ritz, rows), jnp.float32)] * count,
        compiler_params=pltpu.CompilerParams(vmem_limit_bytes=32 * MIB),
        cost_estimate=pl.CostEstimate(
            flops=2 * count * rows * land * (feat + 4 * ritz),
            bytes_accessed=2 * (count * rows + land) * feat,
            transcendentals=count * rows * land,
        ),
    )(*slabs, first, second, *(accs or []))


def add_kernel(a_ref, b_ref, out_ref):
    total = a_ref[...].astype(jnp.float32) + b_ref[...].astype(jnp.float32)
    out_ref[...] = total.astype(out_ref.dtype)


def scale_kernel(*refs, total_land):
    ritz_ref, out_ref = refs[-2:]
    factor = 1.0 / (ritz_ref[...] * math.sqrt(total_land))
    start = 0
    for a_ref, b_ref in zip(refs[0:-2:2], refs[1:-2:2]):
        stop = start + a_ref.shape[1]
        total = a_ref[...].astype(jnp.float32) + b_ref[...].astype(jnp.float32)
        out_ref[:, start:stop] = total * factor
        start = stop


def small_call(kernel, out, *args):
    return pl.pallas_call(
        kernel,
        out_shape=jax.ShapeDtypeStruct(out.shape, out.dtype),
        compiler_params=pltpu.CompilerParams(vmem_limit_bytes=8 * MIB),
    )(*args)


def local(slab, landmarks, codes, exponents, eigvec, ritz):
    n_lm, n_sl = lax.axis_size("lm"), lax.axis_size("sl")
    total_land = codes.shape[0] * n_lm * n_sl
    coeff = 1.0 / math.sqrt(slab.shape[1])
    cols = ritz.shape[0]
    rows = slab.shape[0]
    ways = n_sl.bit_length() - 2

    second = second_half(landmarks)
    first = prepare(landmarks, codes.T, exponents, eigvec.T)
    blocks = {0: [first, second]}
    for k in range(ways):
        blocks[1 << k] = [None, None]
    for turn in (0, 1):
        for k in range(ways):
            piece = (k + turn) % 2
            blocks[1 << k][piece] = chip_send(blocks[0][piece], k, n_sl)
    late_slab, _ = lax.optimization_barrier((slab, second))
    turned = jax.ShapeDtypeStruct(slab.shape[::-1], slab.dtype)
    other = small_call(transpose_kernel, turned, core_send(late_slab, n_sl))
    slab = small_call(transpose_kernel, turned, slab)
    (acc,) = stage([slab], first, second, None, coeff, cols)
    held = [blocks[1 << k][k % 2] for k in range(ways)]
    held, acc = lax.optimization_barrier((held, acc))
    for k in range(ways):
        blocks[1 << k][k % 2] = held[k]
    (other_acc,) = stage([other], first, second, None, coeff, cols)
    accs = [acc, other_acc]
    for t in range(1, 1 << ways):
        if t in blocks:
            continue
        low, high = (t & -t).bit_length() - 1, t.bit_length() - 1
        blocks[t] = [
            chip_send(blocks[t ^ (1 << high)][0], high, n_sl),
            chip_send(blocks[t ^ (1 << low)][1], low, n_sl),
        ]

    for t in range(1, (1 << ways) - 1):
        accs = stage([slab, other], *blocks[t], accs, coeff, cols)
    end = blocks[(1 << ways) - 1]
    width = rows // 2
    spans = [(0, width), (width, rows)]
    half = jax.ShapeDtypeStruct((cols, width), jnp.bfloat16)
    (early,) = stage([other], *end, accs[1:], coeff, cols, spans[:1])
    received = [core_send(early, n_sl)]
    late, *mine = stage(
        [other, slab, slab], *end, [accs[1], accs[0], accs[0]], coeff, cols, [spans[1], *spans]
    )
    received.append(core_send(late, n_sl))
    totals = [small_call(add_kernel, half, a, b) for a, b in zip(mine, received)]
    turns = n_lm.bit_length() - 1
    for k in range(turns - 1):
        arrived = [lm_send(total, k, n_lm, n_sl) for total in totals]
        totals = [small_call(add_kernel, half, a, b) for a, b in zip(totals, arrived)]
    pairs = [(total, lm_send(total, turns - 1, n_lm, n_sl)) for total in totals]
    scale = functools.partial(scale_kernel, total_land=total_land)
    out = jax.ShapeDtypeStruct((cols, rows), jnp.float32)
    return small_call(scale, out, *(x for pair in pairs for x in pair), ritz[:, None]).T


def solution(mesh):
    return jax.shard_map(
        local,
        mesh=mesh,
        in_specs=(
            P("sl", None),
            P(("lm", "sl"), None),
            P(("lm", "sl"), None),
            P(("lm", "sl")),
            P(),
            P(),
        ),
        out_specs=P("sl", None),
        check_vma=False,
    )
```

```python
import functools
import math

import jax
import jax.numpy as jnp
from jax import lax
from jax.experimental import pallas as pl
from jax.experimental.pallas import tpu as pltpu
from jax.sharding import PartitionSpec as P

BLOCK = 128
SHIFT = 32
CHUNK = 512
MIB = 2**20


def core_send(value, n):
    return lax.ppermute(value, "sl", [(i, i ^ 1) for i in range(n)])


def chip_send(value, k, n):
    bits = [1 << b for b in range(1, n.bit_length() - 1)]
    return lax.ppermute(value, "sl", [(i, i ^ bits[(k + i % 2) % len(bits)]) for i in range(n)])


def lm_send(value, k, n_lm, n_sl):
    bits = [1 << b for b in range(n_lm.bit_length() - 1)]
    perm = [
        (i * n_sl + j, (i ^ bits[(k + j % 2) % len(bits)]) * n_sl + j)
        for i in range(n_lm)
        for j in range(n_sl)
    ]
    return lax.ppermute(value, ("lm", "sl"), perm)


def prepare_kernel(
    land_ref, codes_ref, exponents_ref, eig_ref, first_ref, codes, eig, exponents, sems
):
    rows, feat = land_ref.shape
    half = rows // 2 - SHIFT
    ritz = eig_ref.shape[0]
    pairs = [
        (codes_ref, codes),
        (eig_ref, eig),
        (exponents_ref, exponents),
        (land_ref.at[:half], first_ref.at[:half]),
    ]
    copies = [pltpu.make_async_copy(src, dst, sems.at[k]) for k, (src, dst) in enumerate(pairs)]
    for copy in copies:
        copy.start()
    for copy in copies[:3]:
        copy.wait()
    pieces = []
    for b in range(rows // BLOCK):
        scale = lax.shift_left(jnp.int32(1), exponents[b] + 15).astype(jnp.float32) * 2.0**-15
        pieces.append(codes[:, b * BLOCK : (b + 1) * BLOCK].astype(jnp.float32) * scale)
    basis = jnp.concatenate(pieces, axis=1).astype(jnp.bfloat16)
    vectors = jnp.dot(eig[...], basis, preferred_element_type=jnp.float32).astype(jnp.bfloat16)
    chunks = feat // rows
    depth = ritz // chunks
    for c in range(chunks):
        first_ref[half:, c * rows : (c + 1) * rows] = vectors[c * depth : (c + 1) * depth, :]
    for copy in copies[3:]:
        copy.wait()


def tail_kernel(land_ref, out_ref, sem):
    copy = pltpu.make_async_copy(land_ref.at[land_ref.shape[0] - out_ref.shape[0] :], out_ref, sem)
    copy.start()
    copy.wait()


def second_half(landmarks):
    rows, feat = landmarks.shape
    return pl.pallas_call(
        tail_kernel,
        out_shape=jax.ShapeDtypeStruct((rows // 2 + SHIFT, feat), jnp.bfloat16),
        in_specs=[pl.BlockSpec(memory_space=pltpu.HBM)],
        scratch_shapes=[pltpu.SemaphoreType.DMA],
        compiler_params=pltpu.CompilerParams(vmem_limit_bytes=8 * MIB),
    )(pltpu.with_memory_space_constraint(landmarks, pltpu.HBM))


def prepare(landmarks, codes_t, exponents, eig_t):
    rows, feat = landmarks.shape
    extra = eig_t.shape[0] * rows // feat
    return pl.pallas_call(
        prepare_kernel,
        out_shape=jax.ShapeDtypeStruct((rows // 2 - SHIFT + extra, feat), jnp.bfloat16),
        in_specs=[pl.BlockSpec(memory_space=pltpu.HBM)] * 4,
        scratch_shapes=[
            pltpu.VMEM(codes_t.shape, codes_t.dtype),
            pltpu.VMEM(eig_t.shape, eig_t.dtype),
            pltpu.SMEM(exponents.shape, exponents.dtype),
            pltpu.SemaphoreType.DMA((4,)),
        ],
        compiler_params=pltpu.CompilerParams(vmem_limit_bytes=8 * MIB),
    )(*(pltpu.with_memory_space_constraint(x, pltpu.HBM) for x in (landmarks, codes_t, exponents, eig_t)))


def transpose_kernel(in_ref, out_ref):
    for k in range(in_ref.shape[0] // CHUNK):
        rows = slice(k * CHUNK, (k + 1) * CHUNK)
        out_ref[:, rows] = in_ref[rows, :].T


def stage_kernel(count, coeff, ritz, has_acc, spans, *refs):
    slabs = refs[:count]
    first_ref, second_ref = refs[count : count + 2]
    accs = refs[count + 2 : 2 * count + 2] if has_acc else [None] * count
    outs = refs[-count:]
    tail, feat = second_ref.shape
    rows = (first_ref.shape[0] + tail) * feat // (feat + ritz)
    head = rows - tail
    land = jnp.concatenate([first_ref[:head, :], second_ref[...]], axis=0)
    vec = jnp.concatenate(
        [first_ref[head:, c * rows : (c + 1) * rows] for c in range(feat // rows)], axis=0
    )
    work = [
        (k, slice(c, min(c + CHUNK, stop)))
        for k, (start, stop) in enumerate(spans)
        for c in range(start, stop, CHUNK)
    ]

    def scores(k, cols):
        return jnp.dot(land, slabs[k][:, cols], preferred_element_type=jnp.float32)

    ahead = scores(*work[0])
    for n, (k, cols) in enumerate(work):
        now, ahead = ahead, scores(*work[n + 1]) if n + 1 < len(work) else None
        affinity = jnp.exp(now * coeff).astype(jnp.bfloat16)
        term = jnp.dot(vec, affinity, preferred_element_type=jnp.float32)
        place = slice(cols.start - spans[k][0], cols.stop - spans[k][0])
        outs[k][:, place] = term if accs[k] is None else accs[k][:, cols] + term


def stage(slabs, first, second, accs, coeff, ritz, spans=None):
    feat, rows = slabs[0].shape
    land = (first.shape[0] + second.shape[0]) * feat // (feat + ritz)
    count = len(slabs)
    spans = spans or [(0, rows)] * count
    rows = spans[0][1] - spans[0][0]
    return pl.pallas_call(
        functools.partial(stage_kernel, count, coeff, ritz, accs is not None, spans),
        out_shape=[jax.ShapeDtypeStruct((ritz, rows), jnp.float32)] * count,
        compiler_params=pltpu.CompilerParams(vmem_limit_bytes=32 * MIB),
        cost_estimate=pl.CostEstimate(
            flops=2 * count * rows * land * (feat + 4 * ritz),
            bytes_accessed=2 * (count * rows + land) * feat,
            transcendentals=count * rows * land,
        ),
    )(*slabs, first, second, *(accs or []))


def add_kernel(a_ref, b_ref, out_ref):
    total = a_ref[...].astype(jnp.float32) + b_ref[...].astype(jnp.float32)
    out_ref[...] = total.astype(out_ref.dtype)


def scale_kernel(*refs, total_land):
    ritz_ref, out_ref = refs[-2:]
    factor = 1.0 / (ritz_ref[...] * math.sqrt(total_land))
    start = 0
    for a_ref, b_ref in zip(refs[0:-2:2], refs[1:-2:2]):
        stop = start + a_ref.shape[1]
        total = a_ref[...].astype(jnp.float32) + b_ref[...].astype(jnp.float32)
        out_ref[:, start:stop] = total * factor
        start = stop


def small_call(kernel, out, *args):
    return pl.pallas_call(
        kernel,
        out_shape=jax.ShapeDtypeStruct(out.shape, out.dtype),
        compiler_params=pltpu.CompilerParams(vmem_limit_bytes=8 * MIB),
    )(*args)


def local(slab, landmarks, codes, exponents, eigvec, ritz):
    n_lm, n_sl = lax.axis_size("lm"), lax.axis_size("sl")
    total_land = codes.shape[0] * n_lm * n_sl
    coeff = 1.0 / math.sqrt(slab.shape[1])
    cols = ritz.shape[0]
    rows = slab.shape[0]
    ways = n_sl.bit_length() - 2

    second = second_half(landmarks)
    first = prepare(landmarks, codes.T, exponents, eigvec.T)
    blocks = {0: [first, second]}
    for k in range(ways):
        blocks[1 << k] = [None, None]
    for turn in (0, 1):
        for k in range(ways):
            piece = (k + turn) % 2
            blocks[1 << k][piece] = chip_send(blocks[0][piece], k, n_sl)
    late_slab, _ = lax.optimization_barrier((slab, second))
    turned = jax.ShapeDtypeStruct(slab.shape[::-1], slab.dtype)
    other = small_call(transpose_kernel, turned, core_send(late_slab, n_sl))
    slab = small_call(transpose_kernel, turned, slab)
    (acc,) = stage([slab], first, second, None, coeff, cols)
    held = [blocks[1 << k][k % 2] for k in range(ways)]
    held, acc = lax.optimization_barrier((held, acc))
    for k in range(ways):
        blocks[1 << k][k % 2] = held[k]
    (other_acc,) = stage([other], first, second, None, coeff, cols)
    accs = [acc, other_acc]
    for t in range(1, 1 << ways):
        if t in blocks:
            continue
        low, high = (t & -t).bit_length() - 1, t.bit_length() - 1
        blocks[t] = [
            chip_send(blocks[t ^ (1 << high)][0], high, n_sl),
            chip_send(blocks[t ^ (1 << low)][1], low, n_sl),
        ]

    for t in range(1, (1 << ways) - 1):
        accs = stage([slab, other], *blocks[t], accs, coeff, cols)
    end = blocks[(1 << ways) - 1]
    width = rows // 2
    spans = [(0, width), (width, rows)]
    half = jax.ShapeDtypeStruct((cols, width), jnp.bfloat16)
    (early,) = stage([other], *end, accs[1:], coeff, cols, spans[:1])
    received = [core_send(early, n_sl)]
    late, mine = stage([other, slab], *end, accs[::-1], coeff, cols, spans[::-1])
    received.append(core_send(late, n_sl))
    total = small_call(add_kernel, half, mine, received[0])
    acc, total = lax.optimization_barrier((accs[0], total))
    (mine,) = stage([slab], *end, [acc], coeff, cols, spans[1:])
    totals = [total, small_call(add_kernel, half, mine, received[1])]
    turns = n_lm.bit_length() - 1
    for k in range(turns - 1):
        arrived = [lm_send(total, k, n_lm, n_sl) for total in totals]
        totals = [small_call(add_kernel, half, a, b) for a, b in zip(totals, arrived)]
    pairs = [(total, lm_send(total, turns - 1, n_lm, n_sl)) for total in totals]
    scale = functools.partial(scale_kernel, total_land=total_land)
    out = jax.ShapeDtypeStruct((cols, rows), jnp.float32)
    return small_call(scale, out, *(x for pair in pairs for x in pair), ritz[:, None]).T


def solution(mesh):
    return jax.shard_map(
        local,
        mesh=mesh,
        in_specs=(
            P("sl", None),
            P(("lm", "sl"), None),
            P(("lm", "sl"), None),
            P(("lm", "sl")),
            P(),
            P(),
        ),
        out_specs=P("sl", None),
        check_vma=False,
    )
```

```python
import functools
import math

import jax
import jax.numpy as jnp
from jax import lax
from jax.experimental import pallas as pl
from jax.experimental.pallas import tpu as pltpu
from jax.sharding import PartitionSpec as P

BLOCK = 128
SHIFT = 16
CHUNK = 512
MIB = 2**20


def core_send(value, n):
    return lax.ppermute(value, "sl", [(i, i ^ 1) for i in range(n)])


def chip_send(value, k, n):
    bits = [1 << b for b in range(1, n.bit_length() - 1)]
    return lax.ppermute(value, "sl", [(i, i ^ bits[(k + i % 2) % len(bits)]) for i in range(n)])


def lm_send(value, k, n_lm, n_sl):
    bits = [1 << b for b in range(n_lm.bit_length() - 1)]
    perm = [
        (i * n_sl + j, (i ^ bits[(k + j % 2) % len(bits)]) * n_sl + j)
        for i in range(n_lm)
        for j in range(n_sl)
    ]
    return lax.ppermute(value, ("lm", "sl"), perm)


def prepare_kernel(
    land_ref, codes_ref, exponents_ref, eig_ref, first_ref, codes, eig, exponents, sems
):
    rows, feat = land_ref.shape
    half = rows // 2 - SHIFT
    ritz = eig_ref.shape[0]
    pairs = [
        (codes_ref, codes),
        (eig_ref, eig),
        (exponents_ref, exponents),
        (land_ref.at[:half], first_ref.at[:half]),
    ]
    copies = [pltpu.make_async_copy(src, dst, sems.at[k]) for k, (src, dst) in enumerate(pairs)]
    for copy in copies:
        copy.start()
    for copy in copies[:3]:
        copy.wait()
    pieces = []
    for b in range(rows // BLOCK):
        scale = lax.shift_left(jnp.int32(1), exponents[b] + 15).astype(jnp.float32) * 2.0**-15
        pieces.append(codes[:, b * BLOCK : (b + 1) * BLOCK].astype(jnp.float32) * scale)
    basis = jnp.concatenate(pieces, axis=1).astype(jnp.bfloat16)
    vectors = jnp.dot(eig[...], basis, preferred_element_type=jnp.float32).astype(jnp.bfloat16)
    chunks = feat // rows
    depth = ritz // chunks
    for c in range(chunks):
        first_ref[half:, c * rows : (c + 1) * rows] = vectors[c * depth : (c + 1) * depth, :]
    for copy in copies[3:]:
        copy.wait()


def tail_kernel(land_ref, out_ref, sem):
    copy = pltpu.make_async_copy(land_ref.at[land_ref.shape[0] - out_ref.shape[0] :], out_ref, sem)
    copy.start()
    copy.wait()


def second_half(landmarks):
    rows, feat = landmarks.shape
    return pl.pallas_call(
        tail_kernel,
        out_shape=jax.ShapeDtypeStruct((rows // 2 + SHIFT, feat), jnp.bfloat16),
        in_specs=[pl.BlockSpec(memory_space=pltpu.HBM)],
        scratch_shapes=[pltpu.SemaphoreType.DMA],
        compiler_params=pltpu.CompilerParams(vmem_limit_bytes=8 * MIB),
    )(pltpu.with_memory_space_constraint(landmarks, pltpu.HBM))


def prepare(landmarks, codes_t, exponents, eig_t):
    rows, feat = landmarks.shape
    extra = eig_t.shape[0] * rows // feat
    return pl.pallas_call(
        prepare_kernel,
        out_shape=jax.ShapeDtypeStruct((rows // 2 - SHIFT + extra, feat), jnp.bfloat16),
        in_specs=[pl.BlockSpec(memory_space=pltpu.HBM)] * 4,
        scratch_shapes=[
            pltpu.VMEM(codes_t.shape, codes_t.dtype),
            pltpu.VMEM(eig_t.shape, eig_t.dtype),
            pltpu.SMEM(exponents.shape, exponents.dtype),
            pltpu.SemaphoreType.DMA((4,)),
        ],
        compiler_params=pltpu.CompilerParams(vmem_limit_bytes=8 * MIB),
    )(*(pltpu.with_memory_space_constraint(x, pltpu.HBM) for x in (landmarks, codes_t, exponents, eig_t)))


def transpose_kernel(in_ref, out_ref):
    for k in range(in_ref.shape[0] // CHUNK):
        rows = slice(k * CHUNK, (k + 1) * CHUNK)
        out_ref[:, rows] = in_ref[rows, :].T


def stage_kernel(count, coeff, ritz, has_acc, spans, *refs):
    slabs = refs[:count]
    first_ref, second_ref = refs[count : count + 2]
    accs = refs[count + 2 : 2 * count + 2] if has_acc else [None] * count
    outs = refs[-count:]
    tail, feat = second_ref.shape
    rows = (first_ref.shape[0] + tail) * feat // (feat + ritz)
    head = rows - tail
    land = jnp.concatenate([first_ref[:head, :], second_ref[...]], axis=0)
    vec = jnp.concatenate(
        [first_ref[head:, c * rows : (c + 1) * rows] for c in range(feat // rows)], axis=0
    )
    work = [
        (k, slice(c, min(c + CHUNK, stop)))
        for k, (start, stop) in enumerate(spans)
        for c in range(start, stop, CHUNK)
    ]

    def scores(k, cols):
        return jnp.dot(land, slabs[k][:, cols], preferred_element_type=jnp.float32)

    ahead = scores(*work[0])
    for n, (k, cols) in enumerate(work):
        now, ahead = ahead, scores(*work[n + 1]) if n + 1 < len(work) else None
        affinity = jnp.exp(now * coeff).astype(jnp.bfloat16)
        term = jnp.dot(vec, affinity, preferred_element_type=jnp.float32)
        place = slice(cols.start - spans[k][0], cols.stop - spans[k][0])
        term = term if accs[k] is None else accs[k][:, cols] + term
        outs[k][:, place] = term.astype(outs[k].dtype)


def stage(slabs, first, second, accs, coeff, ritz, spans=None, dtype=jnp.float32):
    feat, rows = slabs[0].shape
    land = (first.shape[0] + second.shape[0]) * feat // (feat + ritz)
    count = len(slabs)
    spans = spans or [(0, rows)] * count
    rows = spans[0][1] - spans[0][0]
    return pl.pallas_call(
        functools.partial(stage_kernel, count, coeff, ritz, accs is not None, spans),
        out_shape=[jax.ShapeDtypeStruct((ritz, rows), dtype)] * count,
        compiler_params=pltpu.CompilerParams(vmem_limit_bytes=32 * MIB),
        cost_estimate=pl.CostEstimate(
            flops=2 * count * rows * land * (feat + 4 * ritz),
            bytes_accessed=2 * (count * rows + land) * feat,
            transcendentals=count * rows * land,
        ),
    )(*slabs, first, second, *(accs or []))


def add_kernel(a_ref, b_ref, out_ref):
    total = a_ref[...].astype(jnp.float32) + b_ref[...].astype(jnp.float32)
    out_ref[...] = total.astype(out_ref.dtype)


def split_kernel(mine_ref, early_ref, last_ref, *outs):
    start = 0
    for out_ref in outs:
        cols = slice(start, start + out_ref.shape[1])
        total = mine_ref[:, cols] + early_ref[:, cols] + last_ref[:, cols].astype(jnp.float32)
        out_ref[...] = total.astype(out_ref.dtype)
        start = cols.stop


def scale_kernel(*refs, total_land):
    ritz_ref, out_ref = refs[-2:]
    factor = 1.0 / (ritz_ref[...] * math.sqrt(total_land))
    start = 0
    for a_ref, b_ref in zip(refs[0:-2:2], refs[1:-2:2]):
        stop = start + a_ref.shape[1]
        total = a_ref[...].astype(jnp.float32) + b_ref[...].astype(jnp.float32)
        out_ref[:, start:stop] = total * factor
        start = stop


def small_call(kernel, out, *args):
    return pl.pallas_call(
        kernel,
        out_shape=out,
        compiler_params=pltpu.CompilerParams(vmem_limit_bytes=8 * MIB),
    )(*args)


def local(slab, landmarks, codes, exponents, eigvec, ritz):
    n_lm, n_sl = lax.axis_size("lm"), lax.axis_size("sl")
    total_land = codes.shape[0] * n_lm * n_sl
    coeff = 1.0 / math.sqrt(slab.shape[1])
    cols = ritz.shape[0]
    rows = slab.shape[0]
    ways = n_sl.bit_length() - 2

    second = second_half(landmarks)
    first = prepare(landmarks, codes.T, exponents, eigvec.T)
    blocks = {0: [first, second]}
    for k in range(ways):
        blocks[1 << k] = [None, None]
    for turn in (0, 1):
        for k in range(ways):
            piece = (k + turn) % 2
            blocks[1 << k][piece] = chip_send(blocks[0][piece], k, n_sl)
    late_slab, _ = lax.optimization_barrier((slab, second))
    turned = jax.ShapeDtypeStruct(slab.shape[::-1], slab.dtype)
    far = core_send(late_slab, n_sl)
    slab = small_call(transpose_kernel, turned, slab)
    (acc,) = stage([slab], first, second, None, coeff, cols)
    held = [blocks[1 << k][k % 2] for k in range(ways)]
    held, acc = lax.optimization_barrier((held, acc))
    for k in range(ways):
        blocks[1 << k][k % 2] = held[k]
    (blocks[2][1], far) = lax.optimization_barrier((blocks[2][1], far))
    other = small_call(transpose_kernel, turned, far)
    (other_acc,) = stage([other], first, second, None, coeff, cols)
    accs = [acc, other_acc]
    for t in range(1, 1 << ways):
        if t in blocks:
            continue
        low, high = (t & -t).bit_length() - 1, t.bit_length() - 1
        blocks[t] = [
            chip_send(blocks[t ^ (1 << high)][0], high, n_sl),
            chip_send(blocks[t ^ (1 << low)][1], low, n_sl),
        ]

    for t in range(1, (1 << ways) - 1):
        accs = stage([slab, other], *blocks[t], accs, coeff, cols)
    end = blocks[(1 << ways) - 1]
    early = core_send(accs[1], n_sl)
    (theirs,) = stage([other], *end, None, coeff, cols, dtype=jnp.bfloat16)
    last = core_send(theirs, n_sl)
    (mine,) = stage([slab], *end, accs[:1], coeff, cols)
    half = jax.ShapeDtypeStruct((cols, rows // 2), jnp.bfloat16)
    totals = small_call(split_kernel, [half] * 2, mine, early, last)
    turns = n_lm.bit_length() - 1
    for k in range(turns - 1):
        arrived = [lm_send(total, k, n_lm, n_sl) for total in totals]
        totals = [small_call(add_kernel, half, a, b) for a, b in zip(totals, arrived)]
    pairs = [(total, lm_send(total, turns - 1, n_lm, n_sl)) for total in totals]
    scale = functools.partial(scale_kernel, total_land=total_land)
    out = jax.ShapeDtypeStruct((cols, rows), jnp.float32)
    return small_call(scale, out, *(x for pair in pairs for x in pair), ritz[:, None]).T


def solution(mesh):
    return jax.shard_map(
        local,
        mesh=mesh,
        in_specs=(
            P("sl", None),
            P(("lm", "sl"), None),
            P(("lm", "sl"), None),
            P(("lm", "sl")),
            P(),
            P(),
        ),
        out_specs=P("sl", None),
        check_vma=False,
    )
```

```python
import functools
import math

import jax
import jax.numpy as jnp
from jax import lax
from jax.experimental import pallas as pl
from jax.experimental.pallas import tpu as pltpu
from jax.sharding import PartitionSpec as P

BLOCK = 128
SHIFT = 16
CHUNK = 512
MIB = 2**20


def core_send(value, n):
    return lax.ppermute(value, "sl", [(i, i ^ 1) for i in range(n)])


def chip_send(value, k, n):
    bits = [1 << b for b in range(1, n.bit_length() - 1)]
    return lax.ppermute(value, "sl", [(i, i ^ bits[(k + i % 2) % len(bits)]) for i in range(n)])


def lm_send(value, k, n_lm, n_sl):
    bits = [1 << b for b in range(n_lm.bit_length() - 1)]
    perm = [
        (i * n_sl + j, (i ^ bits[(k + j % 2) % len(bits)]) * n_sl + j)
        for i in range(n_lm)
        for j in range(n_sl)
    ]
    return lax.ppermute(value, ("lm", "sl"), perm)


def prepare_kernel(
    land_ref, codes_ref, exponents_ref, eig_ref, first_ref, codes, eig, exponents, sems
):
    rows, feat = land_ref.shape
    half = rows // 2 - SHIFT
    ritz = eig_ref.shape[0]
    pairs = [
        (codes_ref, codes),
        (eig_ref, eig),
        (exponents_ref, exponents),
        (land_ref.at[:half], first_ref.at[:half]),
    ]
    copies = [pltpu.make_async_copy(src, dst, sems.at[k]) for k, (src, dst) in enumerate(pairs)]
    for copy in copies:
        copy.start()
    for copy in copies[:3]:
        copy.wait()
    pieces = []
    for b in range(rows // BLOCK):
        scale = lax.shift_left(jnp.int32(1), exponents[b] + 15).astype(jnp.float32) * 2.0**-15
        pieces.append(codes[:, b * BLOCK : (b + 1) * BLOCK].astype(jnp.float32) * scale)
    basis = jnp.concatenate(pieces, axis=1).astype(jnp.bfloat16)
    vectors = jnp.dot(eig[...], basis, preferred_element_type=jnp.float32).astype(jnp.bfloat16)
    chunks = feat // rows
    depth = ritz // chunks
    for c in range(chunks):
        first_ref[half:, c * rows : (c + 1) * rows] = vectors[c * depth : (c + 1) * depth, :]
    for copy in copies[3:]:
        copy.wait()


def tail_kernel(land_ref, out_ref, sem):
    copy = pltpu.make_async_copy(land_ref.at[land_ref.shape[0] - out_ref.shape[0] :], out_ref, sem)
    copy.start()
    copy.wait()


def second_half(landmarks):
    rows, feat = landmarks.shape
    return pl.pallas_call(
        tail_kernel,
        out_shape=jax.ShapeDtypeStruct((rows // 2 + SHIFT, feat), jnp.bfloat16),
        in_specs=[pl.BlockSpec(memory_space=pltpu.HBM)],
        scratch_shapes=[pltpu.SemaphoreType.DMA],
        compiler_params=pltpu.CompilerParams(vmem_limit_bytes=8 * MIB),
    )(pltpu.with_memory_space_constraint(landmarks, pltpu.HBM))


def prepare(landmarks, codes_t, exponents, eig_t):
    rows, feat = landmarks.shape
    extra = eig_t.shape[0] * rows // feat
    return pl.pallas_call(
        prepare_kernel,
        out_shape=jax.ShapeDtypeStruct((rows // 2 - SHIFT + extra, feat), jnp.bfloat16),
        in_specs=[pl.BlockSpec(memory_space=pltpu.HBM)] * 4,
        scratch_shapes=[
            pltpu.VMEM(codes_t.shape, codes_t.dtype),
            pltpu.VMEM(eig_t.shape, eig_t.dtype),
            pltpu.SMEM(exponents.shape, exponents.dtype),
            pltpu.SemaphoreType.DMA((4,)),
        ],
        compiler_params=pltpu.CompilerParams(vmem_limit_bytes=8 * MIB),
    )(*(pltpu.with_memory_space_constraint(x, pltpu.HBM) for x in (landmarks, codes_t, exponents, eig_t)))


def transpose_kernel(in_ref, out_ref):
    for k in range(in_ref.shape[0] // CHUNK):
        rows = slice(k * CHUNK, (k + 1) * CHUNK)
        out_ref[:, rows] = in_ref[rows, :].T


def stage_kernel(count, coeff, ritz, has_acc, spans, *refs):
    slabs = refs[:count]
    first_ref, second_ref = refs[count : count + 2]
    accs = refs[count + 2 : 2 * count + 2] if has_acc else [None] * count
    outs = refs[-count:]
    tail, feat = second_ref.shape
    rows = (first_ref.shape[0] + tail) * feat // (feat + ritz)
    head = rows - tail
    land = jnp.concatenate([first_ref[:head, :], second_ref[...]], axis=0)
    vec = jnp.concatenate(
        [first_ref[head:, c * rows : (c + 1) * rows] for c in range(feat // rows)], axis=0
    )
    work = [
        (k, slice(c, min(c + CHUNK, stop)))
        for k, (start, stop) in enumerate(spans)
        for c in range(start, stop, CHUNK)
    ]

    def scores(k, cols):
        return jnp.dot(land, slabs[k][:, cols], preferred_element_type=jnp.float32)

    ahead = scores(*work[0])
    for n, (k, cols) in enumerate(work):
        now, ahead = ahead, scores(*work[n + 1]) if n + 1 < len(work) else None
        affinity = jnp.exp(now * coeff).astype(jnp.bfloat16)
        term = jnp.dot(vec, affinity, preferred_element_type=jnp.float32)
        place = slice(cols.start - spans[k][0], cols.stop - spans[k][0])
        outs[k][:, place] = term if accs[k] is None else accs[k][:, cols] + term


def stage(slabs, first, second, accs, coeff, ritz, spans=None):
    feat, rows = slabs[0].shape
    land = (first.shape[0] + second.shape[0]) * feat // (feat + ritz)
    count = len(slabs)
    spans = spans or [(0, rows)] * count
    rows = spans[0][1] - spans[0][0]
    return pl.pallas_call(
        functools.partial(stage_kernel, count, coeff, ritz, accs is not None, spans),
        out_shape=[jax.ShapeDtypeStruct((ritz, rows), jnp.float32)] * count,
        compiler_params=pltpu.CompilerParams(vmem_limit_bytes=32 * MIB),
        cost_estimate=pl.CostEstimate(
            flops=2 * count * rows * land * (feat + 4 * ritz),
            bytes_accessed=2 * (count * rows + land) * feat,
            transcendentals=count * rows * land,
        ),
    )(*slabs, first, second, *(accs or []))


def add_kernel(a_ref, b_ref, out_ref):
    total = a_ref[...].astype(jnp.float32) + b_ref[...].astype(jnp.float32)
    out_ref[...] = total.astype(out_ref.dtype)


def scale_kernel(*refs, total_land):
    ritz_ref, out_ref = refs[-2:]
    factor = 1.0 / (ritz_ref[...] * math.sqrt(total_land))
    start = 0
    for a_ref, b_ref in zip(refs[0:-2:2], refs[1:-2:2]):
        stop = start + a_ref.shape[1]
        total = a_ref[...].astype(jnp.float32) + b_ref[...].astype(jnp.float32)
        out_ref[:, start:stop] = total * factor
        start = stop


def small_call(kernel, out, *args):
    return pl.pallas_call(
        kernel,
        out_shape=jax.ShapeDtypeStruct(out.shape, out.dtype),
        compiler_params=pltpu.CompilerParams(vmem_limit_bytes=8 * MIB),
    )(*args)


def local(slab, landmarks, codes, exponents, eigvec, ritz):
    n_lm, n_sl = lax.axis_size("lm"), lax.axis_size("sl")
    total_land = codes.shape[0] * n_lm * n_sl
    coeff = 1.0 / math.sqrt(slab.shape[1])
    cols = ritz.shape[0]
    rows = slab.shape[0]
    ways = n_sl.bit_length() - 2

    second = second_half(landmarks)
    first = prepare(landmarks, codes.T, exponents, eigvec.T)
    blocks = {0: [first, second]}
    for k in range(ways):
        blocks[1 << k] = [None, None]
    for turn in (0, 1):
        for k in range(ways):
            piece = (k + turn) % 2
            blocks[1 << k][piece] = chip_send(blocks[0][piece], k, n_sl)
    turned = jax.ShapeDtypeStruct(slab.shape[::-1], slab.dtype)
    other = small_call(transpose_kernel, turned, core_send(slab, n_sl))
    slab = small_call(transpose_kernel, turned, slab)
    (acc,) = stage([slab], first, second, None, coeff, cols)
    held = [blocks[1 << k][k % 2] for k in range(ways)]
    held, acc = lax.optimization_barrier((held, acc))
    for k in range(ways):
        blocks[1 << k][k % 2] = held[k]
    (other_acc,) = stage([other], first, second, None, coeff, cols)
    accs = [acc, other_acc]
    for t in range(1, 1 << ways):
        if t in blocks:
            continue
        low, high = (t & -t).bit_length() - 1, t.bit_length() - 1
        blocks[t] = [
            chip_send(blocks[t ^ (1 << high)][0], high, n_sl),
            chip_send(blocks[t ^ (1 << low)][1], low, n_sl),
        ]

    for t in range(1, (1 << ways) - 1):
        accs = stage([slab, other], *blocks[t], accs, coeff, cols)
    end = blocks[(1 << ways) - 1]
    width = rows // 2
    spans = [(0, width), (width, rows)]
    half = jax.ShapeDtypeStruct((cols, width), jnp.bfloat16)
    (early,) = stage([other], *end, accs[1:], coeff, cols, spans[:1])
    received = [core_send(early, n_sl)]
    late, mine = stage([other, slab], *end, accs[::-1], coeff, cols, spans[::-1])
    received.append(core_send(late, n_sl))
    total = small_call(add_kernel, half, mine, received[0])
    acc, total = lax.optimization_barrier((accs[0], total))
    (mine,) = stage([slab], *end, [acc], coeff, cols, spans[1:])
    totals = [total, small_call(add_kernel, half, mine, received[1])]
    turns = n_lm.bit_length() - 1
    for k in range(turns - 1):
        arrived = [lm_send(total, k, n_lm, n_sl) for total in totals]
        totals = [small_call(add_kernel, half, a, b) for a, b in zip(totals, arrived)]
    pairs = [(total, lm_send(total, turns - 1, n_lm, n_sl)) for total in totals]
    scale = functools.partial(scale_kernel, total_land=total_land)
    out = jax.ShapeDtypeStruct((cols, rows), jnp.float32)
    return small_call(scale, out, *(x for pair in pairs for x in pair), ritz[:, None]).T


def solution(mesh):
    return jax.shard_map(
        local,
        mesh=mesh,
        in_specs=(
            P("sl", None),
            P(("lm", "sl"), None),
            P(("lm", "sl"), None),
            P(("lm", "sl")),
            P(),
            P(),
        ),
        out_specs=P("sl", None),
        check_vma=False,
    )
```

```python
import functools
import math

import jax
import jax.numpy as jnp
from jax import lax
from jax.experimental import pallas as pl
from jax.experimental.pallas import tpu as pltpu
from jax.sharding import PartitionSpec as P

BLOCK = 128
SHIFT = 16
CHUNK = 512
MIB = 2**20


def core_send(value, n):
    return lax.ppermute(value, "sl", [(i, i ^ 1) for i in range(n)])


def chip_send(value, k, n):
    bits = [1 << b for b in range(1, n.bit_length() - 1)]
    return lax.ppermute(value, "sl", [(i, i ^ bits[(k + i % 2) % len(bits)]) for i in range(n)])


def lm_send(value, k, n_lm, n_sl):
    bits = [1 << b for b in range(n_lm.bit_length() - 1)]
    perm = [
        (i * n_sl + j, (i ^ bits[(k + j % 2) % len(bits)]) * n_sl + j)
        for i in range(n_lm)
        for j in range(n_sl)
    ]
    return lax.ppermute(value, ("lm", "sl"), perm)


def prepare_kernel(
    land_ref, codes_ref, exponents_ref, eig_ref, first_ref, second_ref, codes, eig, exponents, sems
):
    rows, feat = land_ref.shape
    half = rows // 2 - SHIFT
    ritz = eig_ref.shape[0]
    pairs = [
        (codes_ref, codes),
        (eig_ref, eig),
        (exponents_ref, exponents),
        (land_ref.at[:half], first_ref.at[:half]),
        (land_ref.at[half:], second_ref),
    ]
    copies = [pltpu.make_async_copy(src, dst, sems.at[k]) for k, (src, dst) in enumerate(pairs)]
    for copy in copies:
        copy.start()
    for copy in copies[:3]:
        copy.wait()
    pieces = []
    for b in range(rows // BLOCK):
        scale = lax.shift_left(jnp.int32(1), exponents[b] + 15).astype(jnp.float32) * 2.0**-15
        pieces.append(codes[:, b * BLOCK : (b + 1) * BLOCK].astype(jnp.float32) * scale)
    basis = jnp.concatenate(pieces, axis=1).astype(jnp.bfloat16)
    vectors = jnp.dot(eig[...], basis, preferred_element_type=jnp.float32).astype(jnp.bfloat16)
    chunks = feat // rows
    depth = ritz // chunks
    for c in range(chunks):
        first_ref[half:, c * rows : (c + 1) * rows] = vectors[c * depth : (c + 1) * depth, :]
    for copy in copies[3:]:
        copy.wait()


def prepare(landmarks, codes_t, exponents, eig_t):
    rows, feat = landmarks.shape
    extra = eig_t.shape[0] * rows // feat
    return pl.pallas_call(
        prepare_kernel,
        out_shape=[
            jax.ShapeDtypeStruct((rows // 2 - SHIFT + extra, feat), jnp.bfloat16),
            jax.ShapeDtypeStruct((rows // 2 + SHIFT, feat), jnp.bfloat16),
        ],
        in_specs=[pl.BlockSpec(memory_space=pltpu.HBM)] * 4,
        scratch_shapes=[
            pltpu.VMEM(codes_t.shape, codes_t.dtype),
            pltpu.VMEM(eig_t.shape, eig_t.dtype),
            pltpu.SMEM(exponents.shape, exponents.dtype),
            pltpu.SemaphoreType.DMA((5,)),
        ],
        compiler_params=pltpu.CompilerParams(vmem_limit_bytes=8 * MIB),
    )(*(pltpu.with_memory_space_constraint(x, pltpu.HBM) for x in (landmarks, codes_t, exponents, eig_t)))


def transpose_kernel(in_ref, out_ref):
    for k in range(in_ref.shape[0] // CHUNK):
        rows = slice(k * CHUNK, (k + 1) * CHUNK)
        out_ref[:, rows] = in_ref[rows, :].T


def stage_kernel(count, coeff, ritz, has_acc, spans, *refs):
    slabs = refs[:count]
    first_ref, second_ref = refs[count : count + 2]
    accs = refs[count + 2 : 2 * count + 2] if has_acc else [None] * count
    outs = refs[-count:]
    tail, feat = second_ref.shape
    rows = (first_ref.shape[0] + tail) * feat // (feat + ritz)
    head = rows - tail
    land = jnp.concatenate([first_ref[:head, :], second_ref[...]], axis=0)
    vec = jnp.concatenate(
        [first_ref[head:, c * rows : (c + 1) * rows] for c in range(feat // rows)], axis=0
    )
    work = [
        (k, slice(c, min(c + CHUNK, stop)))
        for k, (start, stop) in enumerate(spans)
        for c in range(start, stop, CHUNK)
    ]

    def scores(k, cols):
        return jnp.dot(land, slabs[k][:, cols], preferred_element_type=jnp.float32)

    ahead = scores(*work[0])
    for n, (k, cols) in enumerate(work):
        now, ahead = ahead, scores(*work[n + 1]) if n + 1 < len(work) else None
        affinity = jnp.exp(now * coeff).astype(jnp.bfloat16)
        term = jnp.dot(vec, affinity, preferred_element_type=jnp.float32)
        place = slice(cols.start - spans[k][0], cols.stop - spans[k][0])
        outs[k][:, place] = term if accs[k] is None else accs[k][:, cols] + term


def stage(slabs, first, second, accs, coeff, ritz, spans=None):
    feat, rows = slabs[0].shape
    land = (first.shape[0] + second.shape[0]) * feat // (feat + ritz)
    count = len(slabs)
    spans = spans or [(0, rows)] * count
    rows = spans[0][1] - spans[0][0]
    return pl.pallas_call(
        functools.partial(stage_kernel, count, coeff, ritz, accs is not None, spans),
        out_shape=[jax.ShapeDtypeStruct((ritz, rows), jnp.float32)] * count,
        compiler_params=pltpu.CompilerParams(vmem_limit_bytes=32 * MIB),
        cost_estimate=pl.CostEstimate(
            flops=2 * count * rows * land * (feat + 4 * ritz),
            bytes_accessed=2 * (count * rows + land) * feat,
            transcendentals=count * rows * land,
        ),
    )(*slabs, first, second, *(accs or []))


def add_kernel(a_ref, b_ref, out_ref):
    total = a_ref[...].astype(jnp.float32) + b_ref[...].astype(jnp.float32)
    out_ref[...] = total.astype(out_ref.dtype)


def scale_kernel(*refs, total_land):
    ritz_ref, out_ref = refs[-2:]
    factor = 1.0 / (ritz_ref[...] * math.sqrt(total_land))
    start = 0
    for a_ref, b_ref in zip(refs[0:-2:2], refs[1:-2:2]):
        stop = start + a_ref.shape[1]
        total = a_ref[...].astype(jnp.float32) + b_ref[...].astype(jnp.float32)
        out_ref[:, start:stop] = total * factor
        start = stop


def small_call(kernel, out, *args):
    return pl.pallas_call(
        kernel,
        out_shape=jax.ShapeDtypeStruct(out.shape, out.dtype),
        compiler_params=pltpu.CompilerParams(vmem_limit_bytes=8 * MIB),
    )(*args)


def local(slab, landmarks, codes, exponents, eigvec, ritz):
    n_lm, n_sl = lax.axis_size("lm"), lax.axis_size("sl")
    total_land = codes.shape[0] * n_lm * n_sl
    coeff = 1.0 / math.sqrt(slab.shape[1])
    cols = ritz.shape[0]
    rows = slab.shape[0]
    ways = n_sl.bit_length() - 2

    first, second = prepare(landmarks, codes.T, exponents, eigvec.T)
    blocks = {0: [first, second]}
    for k in range(ways):
        blocks[1 << k] = [None, None]
    for turn in (0, 1):
        for k in range(ways):
            piece = (k + turn) % 2
            blocks[1 << k][piece] = chip_send(blocks[0][piece], k, n_sl)
    turned = jax.ShapeDtypeStruct(slab.shape[::-1], slab.dtype)
    other = small_call(transpose_kernel, turned, core_send(slab, n_sl))
    slab = small_call(transpose_kernel, turned, slab)
    (acc,) = stage([slab], first, second, None, coeff, cols)
    held = [blocks[1 << k][k % 2] for k in range(ways)]
    held, acc = lax.optimization_barrier((held, acc))
    for k in range(ways):
        blocks[1 << k][k % 2] = held[k]
    (other_acc,) = stage([other], first, second, None, coeff, cols)
    accs = [acc, other_acc]
    for t in range(1, 1 << ways):
        if t in blocks:
            continue
        low, high = (t & -t).bit_length() - 1, t.bit_length() - 1
        blocks[t] = [
            chip_send(blocks[t ^ (1 << high)][0], high, n_sl),
            chip_send(blocks[t ^ (1 << low)][1], low, n_sl),
        ]

    for t in range(1, (1 << ways) - 1):
        accs = stage([slab, other], *blocks[t], accs, coeff, cols)
    end = blocks[(1 << ways) - 1]
    width = rows // 2
    spans = [(0, width), (width, rows)]
    half = jax.ShapeDtypeStruct((cols, width), jnp.bfloat16)
    (early,) = stage([other], *end, accs[1:], coeff, cols, spans[:1])
    received = [core_send(early, n_sl)]
    late, mine = stage([other, slab], *end, accs[::-1], coeff, cols, spans[::-1])
    received.append(core_send(late, n_sl))
    total = small_call(add_kernel, half, mine, received[0])
    acc, total = lax.optimization_barrier((accs[0], total))
    (mine,) = stage([slab], *end, [acc], coeff, cols, spans[1:])
    totals = [total, small_call(add_kernel, half, mine, received[1])]
    turns = n_lm.bit_length() - 1
    for k in range(turns - 1):
        arrived = [lm_send(total, k, n_lm, n_sl) for total in totals]
        totals = [small_call(add_kernel, half, a, b) for a, b in zip(totals, arrived)]
    pairs = [(total, lm_send(total, turns - 1, n_lm, n_sl)) for total in totals]
    scale = functools.partial(scale_kernel, total_land=total_land)
    out = jax.ShapeDtypeStruct((cols, rows), jnp.float32)
    return small_call(scale, out, *(x for pair in pairs for x in pair), ritz[:, None]).T


def solution(mesh):
    return jax.shard_map(
        local,
        mesh=mesh,
        in_specs=(
            P("sl", None),
            P(("lm", "sl"), None),
            P(("lm", "sl"), None),
            P(("lm", "sl")),
            P(),
            P(),
        ),
        out_specs=P("sl", None),
        check_vma=False,
    )
```

```python
import functools
import math

import jax
import jax.numpy as jnp
from jax import lax
from jax.experimental import pallas as pl
from jax.experimental.pallas import tpu as pltpu
from jax.sharding import PartitionSpec as P

BLOCK = 128
SHIFT = 16
CHUNK = 512
MIB = 2**20


def core_send(value, n):
    return lax.ppermute(value, "sl", [(i, i ^ 1) for i in range(n)])


def chip_send(value, k, n):
    bits = [1 << b for b in range(1, n.bit_length() - 1)]
    return lax.ppermute(value, "sl", [(i, i ^ bits[(k + i % 2) % len(bits)]) for i in range(n)])


def lm_send(value, k, n_lm, n_sl):
    bits = [1 << b for b in range(n_lm.bit_length() - 1)]
    perm = [
        (i * n_sl + j, (i ^ bits[(k + j % 2) % len(bits)]) * n_sl + j)
        for i in range(n_lm)
        for j in range(n_sl)
    ]
    return lax.ppermute(value, ("lm", "sl"), perm)


def prepare_kernel(
    land_ref, codes_ref, exponents_ref, eig_ref, first_ref, codes, eig, exponents, sems
):
    rows, feat = land_ref.shape
    half = rows // 2 - SHIFT
    ritz = eig_ref.shape[0]
    pairs = [
        (codes_ref, codes),
        (eig_ref, eig),
        (exponents_ref, exponents),
        (land_ref.at[:half], first_ref.at[:half]),
    ]
    copies = [pltpu.make_async_copy(src, dst, sems.at[k]) for k, (src, dst) in enumerate(pairs)]
    for copy in copies:
        copy.start()
    for copy in copies[:3]:
        copy.wait()
    pieces = []
    for b in range(rows // BLOCK):
        scale = lax.shift_left(jnp.int32(1), exponents[b] + 15).astype(jnp.float32) * 2.0**-15
        pieces.append(codes[:, b * BLOCK : (b + 1) * BLOCK].astype(jnp.float32) * scale)
    basis = jnp.concatenate(pieces, axis=1).astype(jnp.bfloat16)
    vectors = jnp.dot(eig[...], basis, preferred_element_type=jnp.float32).astype(jnp.bfloat16)
    chunks = feat // rows
    depth = ritz // chunks
    for c in range(chunks):
        first_ref[half:, c * rows : (c + 1) * rows] = vectors[c * depth : (c + 1) * depth, :]
    for copy in copies[3:]:
        copy.wait()


def tail_kernel(land_ref, out_ref, sem):
    copy = pltpu.make_async_copy(land_ref.at[land_ref.shape[0] - out_ref.shape[0] :], out_ref, sem)
    copy.start()
    copy.wait()


def second_half(landmarks):
    rows, feat = landmarks.shape
    return pl.pallas_call(
        tail_kernel,
        out_shape=jax.ShapeDtypeStruct((rows // 2 + SHIFT, feat), jnp.bfloat16),
        in_specs=[pl.BlockSpec(memory_space=pltpu.HBM)],
        scratch_shapes=[pltpu.SemaphoreType.DMA],
        compiler_params=pltpu.CompilerParams(vmem_limit_bytes=8 * MIB),
    )(pltpu.with_memory_space_constraint(landmarks, pltpu.HBM))


def prepare(landmarks, codes_t, exponents, eig_t):
    rows, feat = landmarks.shape
    extra = eig_t.shape[0] * rows // feat
    return pl.pallas_call(
        prepare_kernel,
        out_shape=jax.ShapeDtypeStruct((rows // 2 - SHIFT + extra, feat), jnp.bfloat16),
        in_specs=[pl.BlockSpec(memory_space=pltpu.HBM)] * 4,
        scratch_shapes=[
            pltpu.VMEM(codes_t.shape, codes_t.dtype),
            pltpu.VMEM(eig_t.shape, eig_t.dtype),
            pltpu.SMEM(exponents.shape, exponents.dtype),
            pltpu.SemaphoreType.DMA((4,)),
        ],
        compiler_params=pltpu.CompilerParams(vmem_limit_bytes=8 * MIB),
    )(*(pltpu.with_memory_space_constraint(x, pltpu.HBM) for x in (landmarks, codes_t, exponents, eig_t)))


def transpose_kernel(in_ref, out_ref):
    for k in range(in_ref.shape[0] // CHUNK):
        rows = slice(k * CHUNK, (k + 1) * CHUNK)
        out_ref[:, rows] = in_ref[rows, :].T


def stage_kernel(count, coeff, ritz, has_acc, spans, *refs):
    slabs = refs[:count]
    first_ref, second_ref = refs[count : count + 2]
    accs = refs[count + 2 : 2 * count + 2] if has_acc else [None] * count
    outs = refs[-count:]
    tail, feat = second_ref.shape
    rows = (first_ref.shape[0] + tail) * feat // (feat + ritz)
    head = rows - tail
    land = jnp.concatenate([first_ref[:head, :], second_ref[...]], axis=0)
    vec = jnp.concatenate(
        [first_ref[head:, c * rows : (c + 1) * rows] for c in range(feat // rows)], axis=0
    )
    work = [
        (k, slice(c, min(c + CHUNK, stop)))
        for k, (start, stop) in enumerate(spans)
        for c in range(start, stop, CHUNK)
    ]

    def scores(k, cols):
        return jnp.dot(land, slabs[k][:, cols], preferred_element_type=jnp.float32)

    ahead = scores(*work[0])
    for n, (k, cols) in enumerate(work):
        now, ahead = ahead, scores(*work[n + 1]) if n + 1 < len(work) else None
        affinity = jnp.exp(now * coeff).astype(jnp.bfloat16)
        term = jnp.dot(vec, affinity, preferred_element_type=jnp.float32)
        place = slice(cols.start - spans[k][0], cols.stop - spans[k][0])
        outs[k][:, place] = term if accs[k] is None else accs[k][:, cols] + term


def stage(slabs, first, second, accs, coeff, ritz, spans=None):
    feat, rows = slabs[0].shape
    land = (first.shape[0] + second.shape[0]) * feat // (feat + ritz)
    count = len(slabs)
    spans = spans or [(0, rows)] * count
    rows = spans[0][1] - spans[0][0]
    return pl.pallas_call(
        functools.partial(stage_kernel, count, coeff, ritz, accs is not None, spans),
        out_shape=[jax.ShapeDtypeStruct((ritz, rows), jnp.float32)] * count,
        compiler_params=pltpu.CompilerParams(vmem_limit_bytes=32 * MIB),
        cost_estimate=pl.CostEstimate(
            flops=2 * count * rows * land * (feat + 4 * ritz),
            bytes_accessed=2 * (count * rows + land) * feat,
            transcendentals=count * rows * land,
        ),
    )(*slabs, first, second, *(accs or []))


def add_kernel(a_ref, b_ref, out_ref):
    total = a_ref[...].astype(jnp.float32) + b_ref[...].astype(jnp.float32)
    out_ref[...] = total.astype(out_ref.dtype)


def scale_kernel(*refs, total_land):
    ritz_ref, out_ref = refs[-2:]
    factor = 1.0 / (ritz_ref[...] * math.sqrt(total_land))
    start = 0
    for a_ref, b_ref in zip(refs[0:-2:2], refs[1:-2:2]):
        stop = start + a_ref.shape[1]
        total = a_ref[...].astype(jnp.float32) + b_ref[...].astype(jnp.float32)
        out_ref[:, start:stop] = total * factor
        start = stop


def small_call(kernel, out, *args):
    return pl.pallas_call(
        kernel,
        out_shape=jax.ShapeDtypeStruct(out.shape, out.dtype),
        compiler_params=pltpu.CompilerParams(vmem_limit_bytes=8 * MIB),
    )(*args)


def local(slab, landmarks, codes, exponents, eigvec, ritz):
    n_lm, n_sl = lax.axis_size("lm"), lax.axis_size("sl")
    total_land = codes.shape[0] * n_lm * n_sl
    coeff = 1.0 / math.sqrt(slab.shape[1])
    cols = ritz.shape[0]
    rows = slab.shape[0]
    ways = n_sl.bit_length() - 2

    second = second_half(landmarks)
    first = prepare(landmarks, codes.T, exponents, eigvec.T)
    blocks = {0: [first, second]}
    for k in range(ways):
        blocks[1 << k] = [None, None]
    for k in range(ways):
        blocks[1 << k][k % 2] = chip_send(blocks[0][k % 2], k, n_sl)
    turned = jax.ShapeDtypeStruct(slab.shape[::-1], slab.dtype)
    other = small_call(transpose_kernel, turned, core_send(slab, n_sl))
    slab = small_call(transpose_kernel, turned, slab)
    later, slab = lax.optimization_barrier((blocks[0], slab))
    for k in range(ways):
        blocks[1 << k][1 - k % 2] = chip_send(later[1 - k % 2], k, n_sl)
    (acc,) = stage([slab], first, second, None, coeff, cols)
    held = [blocks[1 << k][k % 2] for k in range(ways)]
    held, acc = lax.optimization_barrier((held, acc))
    for k in range(ways):
        blocks[1 << k][k % 2] = held[k]
    (other_acc,) = stage([other], first, second, None, coeff, cols)
    accs = [acc, other_acc]
    for t in range(1, 1 << ways):
        if t in blocks:
            continue
        low, high = (t & -t).bit_length() - 1, t.bit_length() - 1
        blocks[t] = [
            chip_send(blocks[t ^ (1 << high)][0], high, n_sl),
            chip_send(blocks[t ^ (1 << low)][1], low, n_sl),
        ]

    for t in range(1, (1 << ways) - 1):
        accs = stage([slab, other], *blocks[t], accs, coeff, cols)
    end = blocks[(1 << ways) - 1]
    width = rows // 2
    spans = [(0, width), (width, rows)]
    half = jax.ShapeDtypeStruct((cols, width), jnp.bfloat16)
    (early,) = stage([other], *end, accs[1:], coeff, cols, spans[:1])
    received = [core_send(early, n_sl)]
    late, mine = stage([other, slab], *end, accs[::-1], coeff, cols, spans[::-1])
    received.append(core_send(late, n_sl))
    total = small_call(add_kernel, half, mine, received[0])
    acc, total = lax.optimization_barrier((accs[0], total))
    (mine,) = stage([slab], *end, [acc], coeff, cols, spans[1:])
    totals = [total, small_call(add_kernel, half, mine, received[1])]
    turns = n_lm.bit_length() - 1
    for k in range(turns - 1):
        arrived = [lm_send(total, k, n_lm, n_sl) for total in totals]
        totals = [small_call(add_kernel, half, a, b) for a, b in zip(totals, arrived)]
    pairs = [(total, lm_send(total, turns - 1, n_lm, n_sl)) for total in totals]
    scale = functools.partial(scale_kernel, total_land=total_land)
    out = jax.ShapeDtypeStruct((cols, rows), jnp.float32)
    return small_call(scale, out, *(x for pair in pairs for x in pair), ritz[:, None]).T


def solution(mesh):
    return jax.shard_map(
        local,
        mesh=mesh,
        in_specs=(
            P("sl", None),
            P(("lm", "sl"), None),
            P(("lm", "sl"), None),
            P(("lm", "sl")),
            P(),
            P(),
        ),
        out_specs=P("sl", None),
        check_vma=False,
    )
```

```python
import functools
import math

import jax
import jax.numpy as jnp
from jax import lax
from jax.experimental import pallas as pl
from jax.experimental.pallas import tpu as pltpu
from jax.sharding import PartitionSpec as P

BLOCK = 128
SHIFT = 16
CHUNK = 512
MIB = 2**20


def core_send(value, n):
    return lax.ppermute(value, "sl", [(i, i ^ 1) for i in range(n)])


def chip_send(value, k, n):
    bits = [1 << b for b in range(1, n.bit_length() - 1)]
    return lax.ppermute(value, "sl", [(i, i ^ bits[(k + i % 2) % len(bits)]) for i in range(n)])


def lm_send(value, k, n_lm, n_sl):
    bits = [1 << b for b in range(n_lm.bit_length() - 1)]
    perm = [
        (i * n_sl + j, (i ^ bits[(k + j % 2) % len(bits)]) * n_sl + j)
        for i in range(n_lm)
        for j in range(n_sl)
    ]
    return lax.ppermute(value, ("lm", "sl"), perm)


def prepare_kernel(
    land_ref, codes_ref, exponents_ref, eig_ref, first_ref, codes, eig, exponents, sems
):
    rows, feat = land_ref.shape
    half = rows // 2 - SHIFT
    ritz = eig_ref.shape[0]
    pairs = [
        (codes_ref, codes),
        (eig_ref, eig),
        (exponents_ref, exponents),
        (land_ref.at[:half], first_ref.at[:half]),
    ]
    copies = [pltpu.make_async_copy(src, dst, sems.at[k]) for k, (src, dst) in enumerate(pairs)]
    for copy in copies:
        copy.start()
    for copy in copies[:3]:
        copy.wait()
    pieces = []
    for b in range(rows // BLOCK):
        scale = lax.shift_left(jnp.int32(1), exponents[b] + 15).astype(jnp.float32) * 2.0**-15
        pieces.append(codes[:, b * BLOCK : (b + 1) * BLOCK].astype(jnp.float32) * scale)
    basis = jnp.concatenate(pieces, axis=1).astype(jnp.bfloat16)
    vectors = jnp.dot(eig[...], basis, preferred_element_type=jnp.float32).astype(jnp.bfloat16)
    chunks = feat // rows
    depth = ritz // chunks
    for c in range(chunks):
        first_ref[half:, c * rows : (c + 1) * rows] = vectors[c * depth : (c + 1) * depth, :]
    for copy in copies[3:]:
        copy.wait()


def tail_kernel(land_ref, out_ref, sem):
    copy = pltpu.make_async_copy(land_ref.at[land_ref.shape[0] - out_ref.shape[0] :], out_ref, sem)
    copy.start()
    copy.wait()


def second_half(landmarks):
    rows, feat = landmarks.shape
    return pl.pallas_call(
        tail_kernel,
        out_shape=jax.ShapeDtypeStruct((rows // 2 + SHIFT, feat), jnp.bfloat16),
        in_specs=[pl.BlockSpec(memory_space=pltpu.HBM)],
        scratch_shapes=[pltpu.SemaphoreType.DMA],
        compiler_params=pltpu.CompilerParams(vmem_limit_bytes=8 * MIB),
    )(pltpu.with_memory_space_constraint(landmarks, pltpu.HBM))


def prepare(landmarks, codes_t, exponents, eig_t):
    rows, feat = landmarks.shape
    extra = eig_t.shape[0] * rows // feat
    return pl.pallas_call(
        prepare_kernel,
        out_shape=jax.ShapeDtypeStruct((rows // 2 - SHIFT + extra, feat), jnp.bfloat16),
        in_specs=[pl.BlockSpec(memory_space=pltpu.HBM)] * 4,
        scratch_shapes=[
            pltpu.VMEM(codes_t.shape, codes_t.dtype),
            pltpu.VMEM(eig_t.shape, eig_t.dtype),
            pltpu.SMEM(exponents.shape, exponents.dtype),
            pltpu.SemaphoreType.DMA((4,)),
        ],
        compiler_params=pltpu.CompilerParams(vmem_limit_bytes=8 * MIB),
    )(*(pltpu.with_memory_space_constraint(x, pltpu.HBM) for x in (landmarks, codes_t, exponents, eig_t)))


def transpose_kernel(in_ref, out_ref):
    for k in range(in_ref.shape[0] // CHUNK):
        rows = slice(k * CHUNK, (k + 1) * CHUNK)
        out_ref[:, rows] = in_ref[rows, :].T


def stage_kernel(count, coeff, ritz, has_acc, spans, *refs):
    slabs = refs[:count]
    first_ref, second_ref = refs[count : count + 2]
    accs = refs[count + 2 : 2 * count + 2] if has_acc else [None] * count
    outs = refs[-count:]
    tail, feat = second_ref.shape
    rows = (first_ref.shape[0] + tail) * feat // (feat + ritz)
    head = rows - tail
    land = jnp.concatenate([first_ref[:head, :], second_ref[...]], axis=0)
    vec = jnp.concatenate(
        [first_ref[head:, c * rows : (c + 1) * rows] for c in range(feat // rows)], axis=0
    )
    work = [
        (k, slice(c, min(c + CHUNK, stop)))
        for k, (start, stop) in enumerate(spans)
        for c in range(start, stop, CHUNK)
    ]

    def scores(k, cols):
        return jnp.dot(land, slabs[k][:, cols], preferred_element_type=jnp.float32)

    ahead = scores(*work[0])
    for n, (k, cols) in enumerate(work):
        now, ahead = ahead, scores(*work[n + 1]) if n + 1 < len(work) else None
        affinity = jnp.exp(now * coeff).astype(jnp.bfloat16)
        term = jnp.dot(vec, affinity, preferred_element_type=jnp.float32)
        place = slice(cols.start - spans[k][0], cols.stop - spans[k][0])
        term = term if accs[k] is None else accs[k][:, cols] + term
        outs[k][:, place] = term.astype(outs[k].dtype)


def stage(slabs, first, second, accs, coeff, ritz, spans=None, dtype=jnp.float32):
    feat, rows = slabs[0].shape
    land = (first.shape[0] + second.shape[0]) * feat // (feat + ritz)
    count = len(slabs)
    spans = spans or [(0, rows)] * count
    rows = spans[0][1] - spans[0][0]
    return pl.pallas_call(
        functools.partial(stage_kernel, count, coeff, ritz, accs is not None, spans),
        out_shape=[jax.ShapeDtypeStruct((ritz, rows), dtype)] * count,
        compiler_params=pltpu.CompilerParams(vmem_limit_bytes=32 * MIB),
        cost_estimate=pl.CostEstimate(
            flops=2 * count * rows * land * (feat + 4 * ritz),
            bytes_accessed=2 * (count * rows + land) * feat,
            transcendentals=count * rows * land,
        ),
    )(*slabs, first, second, *(accs or []))


def add_kernel(a_ref, b_ref, out_ref):
    total = a_ref[...].astype(jnp.float32) + b_ref[...].astype(jnp.float32)
    out_ref[...] = total.astype(out_ref.dtype)


def split_kernel(mine_ref, early_ref, last_ref, *outs):
    start = 0
    for out_ref in outs:
        cols = slice(start, start + out_ref.shape[1])
        total = mine_ref[:, cols] + early_ref[:, cols] + last_ref[:, cols].astype(jnp.float32)
        out_ref[...] = total.astype(out_ref.dtype)
        start = cols.stop


def scale_kernel(*refs, total_land):
    ritz_ref, out_ref = refs[-2:]
    factor = 1.0 / (ritz_ref[...] * math.sqrt(total_land))
    start = 0
    for a_ref, b_ref in zip(refs[0:-2:2], refs[1:-2:2]):
        stop = start + a_ref.shape[1]
        total = a_ref[...].astype(jnp.float32) + b_ref[...].astype(jnp.float32)
        out_ref[:, start:stop] = total * factor
        start = stop


def small_call(kernel, out, *args):
    return pl.pallas_call(
        kernel,
        out_shape=out,
        compiler_params=pltpu.CompilerParams(vmem_limit_bytes=8 * MIB),
    )(*args)


def local(slab, landmarks, codes, exponents, eigvec, ritz):
    n_lm, n_sl = lax.axis_size("lm"), lax.axis_size("sl")
    total_land = codes.shape[0] * n_lm * n_sl
    coeff = 1.0 / math.sqrt(slab.shape[1])
    cols = ritz.shape[0]
    rows = slab.shape[0]
    ways = n_sl.bit_length() - 2

    second = second_half(landmarks)
    first = prepare(landmarks, codes.T, exponents, eigvec.T)
    blocks = {0: [first, second]}
    for k in range(ways):
        blocks[1 << k] = [None, None]
    for turn in (0, 1):
        for k in range(ways):
            piece = (k + turn) % 2
            blocks[1 << k][piece] = chip_send(blocks[0][piece], k, n_sl)
    late_slab, _ = lax.optimization_barrier((slab, second))
    turned = jax.ShapeDtypeStruct(slab.shape[::-1], slab.dtype)
    far = core_send(late_slab, n_sl)
    slab = small_call(transpose_kernel, turned, slab)
    (acc,) = stage([slab], first, second, None, coeff, cols)
    held = [blocks[1 << k][k % 2] for k in range(ways)]
    held, acc = lax.optimization_barrier((held, acc))
    for k in range(ways):
        blocks[1 << k][k % 2] = held[k]
    (blocks[2][1], far) = lax.optimization_barrier((blocks[2][1], far))
    other = small_call(transpose_kernel, turned, far)
    (other_acc,) = stage([other], first, second, None, coeff, cols)
    accs = [acc, other_acc]
    for t in range(1, 1 << ways):
        if t in blocks:
            continue
        low, high = (t & -t).bit_length() - 1, t.bit_length() - 1
        blocks[t] = [
            chip_send(blocks[t ^ (1 << high)][0], high, n_sl),
            chip_send(blocks[t ^ (1 << low)][1], low, n_sl),
        ]

    for t in range(1, (1 << ways) - 1):
        accs = stage([slab, other], *blocks[t], accs, coeff, cols)
    end = blocks[(1 << ways) - 1]
    early = core_send(accs[1], n_sl)
    (theirs,) = stage([other], *end, None, coeff, cols, dtype=jnp.bfloat16)
    last = core_send(theirs, n_sl)
    (mine,) = stage([slab], *end, accs[:1], coeff, cols)
    half = jax.ShapeDtypeStruct((cols, rows), jnp.bfloat16)
    totals = small_call(split_kernel, [half], mine, early, last)
    turns = n_lm.bit_length() - 1
    for k in range(turns - 1):
        arrived = [lm_send(total, k, n_lm, n_sl) for total in totals]
        totals = [small_call(add_kernel, half, a, b) for a, b in zip(totals, arrived)]
    pairs = [(total, lm_send(total, turns - 1, n_lm, n_sl)) for total in totals]
    scale = functools.partial(scale_kernel, total_land=total_land)
    out = jax.ShapeDtypeStruct((cols, rows), jnp.float32)
    return small_call(scale, out, *(x for pair in pairs for x in pair), ritz[:, None]).T


def solution(mesh):
    return jax.shard_map(
        local,
        mesh=mesh,
        in_specs=(
            P("sl", None),
            P(("lm", "sl"), None),
            P(("lm", "sl"), None),
            P(("lm", "sl")),
            P(),
            P(),
        ),
        out_specs=P("sl", None),
        check_vma=False,
    )
```

```python
import functools
import math

import jax
import jax.numpy as jnp
from jax import lax
from jax.experimental import pallas as pl
from jax.experimental.pallas import tpu as pltpu
from jax.sharding import PartitionSpec as P

BLOCK = 128
SHIFT = 16
CHUNK = 512
MIB = 2**20


def core_send(value, n):
    return lax.ppermute(value, "sl", [(i, i ^ 1) for i in range(n)])


def chip_send(value, k, n):
    bits = [1 << b for b in range(1, n.bit_length() - 1)]
    return lax.ppermute(value, "sl", [(i, i ^ bits[(k + 1 - i % 2) % len(bits)]) for i in range(n)])


def lm_send(value, k, n_lm, n_sl):
    bits = [1 << b for b in range(n_lm.bit_length() - 1)]
    perm = [
        (i * n_sl + j, (i ^ bits[(k + j % 2) % len(bits)]) * n_sl + j)
        for i in range(n_lm)
        for j in range(n_sl)
    ]
    return lax.ppermute(value, ("lm", "sl"), perm)


def prepare_kernel(
    land_ref, codes_ref, exponents_ref, eig_ref, first_ref, codes, eig, exponents, sems
):
    rows, feat = land_ref.shape
    half = rows // 2 - SHIFT
    ritz = eig_ref.shape[0]
    pairs = [
        (codes_ref, codes),
        (eig_ref, eig),
        (exponents_ref, exponents),
        (land_ref.at[:half], first_ref.at[:half]),
    ]
    copies = [pltpu.make_async_copy(src, dst, sems.at[k]) for k, (src, dst) in enumerate(pairs)]
    for copy in copies:
        copy.start()
    for copy in copies[:3]:
        copy.wait()
    pieces = []
    for b in range(rows // BLOCK):
        scale = lax.shift_left(jnp.int32(1), exponents[b] + 15).astype(jnp.float32) * 2.0**-15
        pieces.append(codes[:, b * BLOCK : (b + 1) * BLOCK].astype(jnp.float32) * scale)
    basis = jnp.concatenate(pieces, axis=1).astype(jnp.bfloat16)
    vectors = jnp.dot(eig[...], basis, preferred_element_type=jnp.float32).astype(jnp.bfloat16)
    chunks = feat // rows
    depth = ritz // chunks
    for c in range(chunks):
        first_ref[half:, c * rows : (c + 1) * rows] = vectors[c * depth : (c + 1) * depth, :]
    for copy in copies[3:]:
        copy.wait()


def tail_kernel(land_ref, out_ref, sem):
    copy = pltpu.make_async_copy(land_ref.at[land_ref.shape[0] - out_ref.shape[0] :], out_ref, sem)
    copy.start()
    copy.wait()


def second_half(landmarks):
    rows, feat = landmarks.shape
    return pl.pallas_call(
        tail_kernel,
        out_shape=jax.ShapeDtypeStruct((rows // 2 + SHIFT, feat), jnp.bfloat16),
        in_specs=[pl.BlockSpec(memory_space=pltpu.HBM)],
        scratch_shapes=[pltpu.SemaphoreType.DMA],
        compiler_params=pltpu.CompilerParams(vmem_limit_bytes=8 * MIB),
    )(pltpu.with_memory_space_constraint(landmarks, pltpu.HBM))


def prepare(landmarks, codes_t, exponents, eig_t):
    rows, feat = landmarks.shape
    extra = eig_t.shape[0] * rows // feat
    return pl.pallas_call(
        prepare_kernel,
        out_shape=jax.ShapeDtypeStruct((rows // 2 - SHIFT + extra, feat), jnp.bfloat16),
        in_specs=[pl.BlockSpec(memory_space=pltpu.HBM)] * 4,
        scratch_shapes=[
            pltpu.VMEM(codes_t.shape, codes_t.dtype),
            pltpu.VMEM(eig_t.shape, eig_t.dtype),
            pltpu.SMEM(exponents.shape, exponents.dtype),
            pltpu.SemaphoreType.DMA((4,)),
        ],
        compiler_params=pltpu.CompilerParams(vmem_limit_bytes=8 * MIB),
    )(*(pltpu.with_memory_space_constraint(x, pltpu.HBM) for x in (landmarks, codes_t, exponents, eig_t)))


def transpose_kernel(in_ref, out_ref):
    for k in range(in_ref.shape[0] // CHUNK):
        rows = slice(k * CHUNK, (k + 1) * CHUNK)
        out_ref[:, rows] = in_ref[rows, :].T


def stage_kernel(count, coeff, ritz, has_acc, spans, *refs):
    slabs = refs[:count]
    first_ref, second_ref = refs[count : count + 2]
    accs = refs[count + 2 : 2 * count + 2] if has_acc else [None] * count
    outs = refs[-count:]
    tail, feat = second_ref.shape
    rows = (first_ref.shape[0] + tail) * feat // (feat + ritz)
    head = rows - tail
    land = jnp.concatenate([first_ref[:head, :], second_ref[...]], axis=0)
    vec = jnp.concatenate(
        [first_ref[head:, c * rows : (c + 1) * rows] for c in range(feat // rows)], axis=0
    )
    work = [
        (k, slice(c, min(c + CHUNK, stop)))
        for k, (start, stop) in enumerate(spans)
        for c in range(start, stop, CHUNK)
    ]

    def scores(k, cols):
        return jnp.dot(land, slabs[k][:, cols], preferred_element_type=jnp.float32)

    ahead = scores(*work[0])
    for n, (k, cols) in enumerate(work):
        now, ahead = ahead, scores(*work[n + 1]) if n + 1 < len(work) else None
        affinity = jnp.exp(now * coeff).astype(jnp.bfloat16)
        term = jnp.dot(vec, affinity, preferred_element_type=jnp.float32)
        place = slice(cols.start - spans[k][0], cols.stop - spans[k][0])
        outs[k][:, place] = term if accs[k] is None else accs[k][:, cols] + term


def stage(slabs, first, second, accs, coeff, ritz, spans=None):
    feat, rows = slabs[0].shape
    land = (first.shape[0] + second.shape[0]) * feat // (feat + ritz)
    count = len(slabs)
    spans = spans or [(0, rows)] * count
    rows = spans[0][1] - spans[0][0]
    return pl.pallas_call(
        functools.partial(stage_kernel, count, coeff, ritz, accs is not None, spans),
        out_shape=[jax.ShapeDtypeStruct((ritz, rows), jnp.float32)] * count,
        compiler_params=pltpu.CompilerParams(vmem_limit_bytes=32 * MIB),
        cost_estimate=pl.CostEstimate(
            flops=2 * count * rows * land * (feat + 4 * ritz),
            bytes_accessed=2 * (count * rows + land) * feat,
            transcendentals=count * rows * land,
        ),
    )(*slabs, first, second, *(accs or []))


def add_kernel(a_ref, b_ref, out_ref):
    total = a_ref[...].astype(jnp.float32) + b_ref[...].astype(jnp.float32)
    out_ref[...] = total.astype(out_ref.dtype)


def scale_kernel(*refs, total_land):
    ritz_ref, out_ref = refs[-2:]
    factor = 1.0 / (ritz_ref[...] * math.sqrt(total_land))
    start = 0
    for a_ref, b_ref in zip(refs[0:-2:2], refs[1:-2:2]):
        stop = start + a_ref.shape[1]
        total = a_ref[...].astype(jnp.float32) + b_ref[...].astype(jnp.float32)
        out_ref[:, start:stop] = total * factor
        start = stop


def small_call(kernel, out, *args):
    return pl.pallas_call(
        kernel,
        out_shape=jax.ShapeDtypeStruct(out.shape, out.dtype),
        compiler_params=pltpu.CompilerParams(vmem_limit_bytes=8 * MIB),
    )(*args)


def local(slab, landmarks, codes, exponents, eigvec, ritz):
    n_lm, n_sl = lax.axis_size("lm"), lax.axis_size("sl")
    total_land = codes.shape[0] * n_lm * n_sl
    coeff = 1.0 / math.sqrt(slab.shape[1])
    cols = ritz.shape[0]
    rows = slab.shape[0]
    ways = n_sl.bit_length() - 2

    second = second_half(landmarks)
    first = prepare(landmarks, codes.T, exponents, eigvec.T)
    blocks = {0: [first, second]}
    for k in range(ways):
        blocks[1 << k] = [None, None]
    for turn in (0, 1):
        for k in range(ways):
            piece = (k + turn) % 2
            blocks[1 << k][piece] = chip_send(blocks[0][piece], k, n_sl)
    late_slab, _ = lax.optimization_barrier((slab, second))
    turned = jax.ShapeDtypeStruct(slab.shape[::-1], slab.dtype)
    other = small_call(transpose_kernel, turned, core_send(late_slab, n_sl))
    slab = small_call(transpose_kernel, turned, slab)
    (acc,) = stage([slab], first, second, None, coeff, cols)
    held = [blocks[1 << k][k % 2] for k in range(ways)]
    held, acc = lax.optimization_barrier((held, acc))
    for k in range(ways):
        blocks[1 << k][k % 2] = held[k]
    (other_acc,) = stage([other], first, second, None, coeff, cols)
    accs = [acc, other_acc]
    for t in range(1, 1 << ways):
        if t in blocks:
            continue
        low, high = (t & -t).bit_length() - 1, t.bit_length() - 1
        blocks[t] = [
            chip_send(blocks[t ^ (1 << high)][0], high, n_sl),
            chip_send(blocks[t ^ (1 << low)][1], low, n_sl),
        ]

    for t in range(1, (1 << ways) - 1):
        accs = stage([slab, other], *blocks[t], accs, coeff, cols)
    end = blocks[(1 << ways) - 1]
    width = rows // 2
    spans = [(0, width), (width, rows)]
    half = jax.ShapeDtypeStruct((cols, width), jnp.bfloat16)
    (early,) = stage([other], *end, accs[1:], coeff, cols, spans[:1])
    received = [core_send(early, n_sl)]
    late, mine = stage([other, slab], *end, accs[::-1], coeff, cols, spans[::-1])
    received.append(core_send(late, n_sl))
    total = small_call(add_kernel, half, mine, received[0])
    acc, total = lax.optimization_barrier((accs[0], total))
    (mine,) = stage([slab], *end, [acc], coeff, cols, spans[1:])
    totals = [total, small_call(add_kernel, half, mine, received[1])]
    turns = n_lm.bit_length() - 1
    for k in range(turns - 1):
        arrived = [lm_send(total, k, n_lm, n_sl) for total in totals]
        totals = [small_call(add_kernel, half, a, b) for a, b in zip(totals, arrived)]
    pairs = [(total, lm_send(total, turns - 1, n_lm, n_sl)) for total in totals]
    scale = functools.partial(scale_kernel, total_land=total_land)
    out = jax.ShapeDtypeStruct((cols, rows), jnp.float32)
    return small_call(scale, out, *(x for pair in pairs for x in pair), ritz[:, None]).T


def solution(mesh):
    return jax.shard_map(
        local,
        mesh=mesh,
        in_specs=(
            P("sl", None),
            P(("lm", "sl"), None),
            P(("lm", "sl"), None),
            P(("lm", "sl")),
            P(),
            P(),
        ),
        out_specs=P("sl", None),
        check_vma=False,
    )
```

```python
import functools
import math

import jax
import jax.numpy as jnp
from jax import lax
from jax.experimental import pallas as pl
from jax.experimental.pallas import tpu as pltpu
from jax.sharding import PartitionSpec as P

BLOCK = 128
SHIFT = 16
CHUNK = 512
MIB = 2**20


def core_send(value, n):
    return lax.ppermute(value, "sl", [(i, i ^ 1) for i in range(n)])


def chip_send(value, k, n):
    bits = [1 << b for b in range(1, n.bit_length() - 1)]
    return lax.ppermute(value, "sl", [(i, i ^ bits[(k + 1 - i % 2) % len(bits)]) for i in range(n)])


def lm_send(value, k, n_lm, n_sl):
    bits = [1 << b for b in range(n_lm.bit_length() - 1)]
    perm = [
        (i * n_sl + j, (i ^ bits[(k + j % 2) % len(bits)]) * n_sl + j)
        for i in range(n_lm)
        for j in range(n_sl)
    ]
    return lax.ppermute(value, ("lm", "sl"), perm)


def prepare_kernel(
    land_ref, codes_ref, exponents_ref, eig_ref, first_ref, codes, eig, exponents, sems
):
    rows, feat = land_ref.shape
    half = rows // 2 - SHIFT
    ritz = eig_ref.shape[0]
    pairs = [
        (codes_ref, codes),
        (eig_ref, eig),
        (exponents_ref, exponents),
        (land_ref.at[:half], first_ref.at[:half]),
    ]
    copies = [pltpu.make_async_copy(src, dst, sems.at[k]) for k, (src, dst) in enumerate(pairs)]
    for copy in copies:
        copy.start()
    for copy in copies[:3]:
        copy.wait()
    pieces = []
    for b in range(rows // BLOCK):
        scale = lax.shift_left(jnp.int32(1), exponents[b] + 15).astype(jnp.float32) * 2.0**-15
        pieces.append(codes[:, b * BLOCK : (b + 1) * BLOCK].astype(jnp.float32) * scale)
    basis = jnp.concatenate(pieces, axis=1).astype(jnp.bfloat16)
    vectors = jnp.dot(eig[...], basis, preferred_element_type=jnp.float32).astype(jnp.bfloat16)
    chunks = feat // rows
    depth = ritz // chunks
    for c in range(chunks):
        first_ref[half:, c * rows : (c + 1) * rows] = vectors[c * depth : (c + 1) * depth, :]
    for copy in copies[3:]:
        copy.wait()


def tail_kernel(land_ref, out_ref, sem):
    copy = pltpu.make_async_copy(land_ref.at[land_ref.shape[0] - out_ref.shape[0] :], out_ref, sem)
    copy.start()
    copy.wait()


def second_half(landmarks):
    rows, feat = landmarks.shape
    return pl.pallas_call(
        tail_kernel,
        out_shape=jax.ShapeDtypeStruct((rows // 2 + SHIFT, feat), jnp.bfloat16),
        in_specs=[pl.BlockSpec(memory_space=pltpu.HBM)],
        scratch_shapes=[pltpu.SemaphoreType.DMA],
        compiler_params=pltpu.CompilerParams(vmem_limit_bytes=8 * MIB),
    )(pltpu.with_memory_space_constraint(landmarks, pltpu.HBM))


def prepare(landmarks, codes_t, exponents, eig_t):
    rows, feat = landmarks.shape
    extra = eig_t.shape[0] * rows // feat
    return pl.pallas_call(
        prepare_kernel,
        out_shape=jax.ShapeDtypeStruct((rows // 2 - SHIFT + extra, feat), jnp.bfloat16),
        in_specs=[pl.BlockSpec(memory_space=pltpu.HBM)] * 4,
        scratch_shapes=[
            pltpu.VMEM(codes_t.shape, codes_t.dtype),
            pltpu.VMEM(eig_t.shape, eig_t.dtype),
            pltpu.SMEM(exponents.shape, exponents.dtype),
            pltpu.SemaphoreType.DMA((4,)),
        ],
        compiler_params=pltpu.CompilerParams(vmem_limit_bytes=8 * MIB),
    )(*(pltpu.with_memory_space_constraint(x, pltpu.HBM) for x in (landmarks, codes_t, exponents, eig_t)))


def transpose_kernel(in_ref, out_ref):
    for k in range(in_ref.shape[0] // CHUNK):
        rows = slice(k * CHUNK, (k + 1) * CHUNK)
        out_ref[:, rows] = in_ref[rows, :].T


def stage_kernel(count, coeff, ritz, has_acc, spans, *refs):
    slabs = refs[:count]
    first_ref, second_ref = refs[count : count + 2]
    accs = refs[count + 2 : 2 * count + 2] if has_acc else [None] * count
    outs = refs[-count:]
    tail, feat = second_ref.shape
    rows = (first_ref.shape[0] + tail) * feat // (feat + ritz)
    head = rows - tail
    land = jnp.concatenate([first_ref[:head, :], second_ref[...]], axis=0)
    vec = jnp.concatenate(
        [first_ref[head:, c * rows : (c + 1) * rows] for c in range(feat // rows)], axis=0
    )
    work = [
        (k, slice(c, min(c + CHUNK, stop)))
        for k, (start, stop) in enumerate(spans)
        for c in range(start, stop, CHUNK)
    ]

    def scores(k, cols):
        return jnp.dot(land, slabs[k][:, cols], preferred_element_type=jnp.float32)

    ahead = scores(*work[0])
    for n, (k, cols) in enumerate(work):
        now, ahead = ahead, scores(*work[n + 1]) if n + 1 < len(work) else None
        affinity = jnp.exp(now * coeff).astype(jnp.bfloat16)
        term = jnp.dot(vec, affinity, preferred_element_type=jnp.float32)
        place = slice(cols.start - spans[k][0], cols.stop - spans[k][0])
        outs[k][:, place] = term if accs[k] is None else accs[k][:, cols] + term


def stage(slabs, first, second, accs, coeff, ritz, spans=None):
    feat, rows = slabs[0].shape
    land = (first.shape[0] + second.shape[0]) * feat // (feat + ritz)
    count = len(slabs)
    spans = spans or [(0, rows)] * count
    rows = spans[0][1] - spans[0][0]
    return pl.pallas_call(
        functools.partial(stage_kernel, count, coeff, ritz, accs is not None, spans),
        out_shape=[jax.ShapeDtypeStruct((ritz, rows), jnp.float32)] * count,
        compiler_params=pltpu.CompilerParams(vmem_limit_bytes=32 * MIB),
        cost_estimate=pl.CostEstimate(
            flops=2 * count * rows * land * (feat + 4 * ritz),
            bytes_accessed=2 * (count * rows + land) * feat,
            transcendentals=count * rows * land,
        ),
    )(*slabs, first, second, *(accs or []))


def add_kernel(a_ref, b_ref, out_ref):
    total = a_ref[...].astype(jnp.float32) + b_ref[...].astype(jnp.float32)
    out_ref[...] = total.astype(out_ref.dtype)


def scale_kernel(*refs, total_land):
    ritz_ref, out_ref = refs[-2:]
    factor = 1.0 / (ritz_ref[...] * math.sqrt(total_land))
    start = 0
    for a_ref, b_ref in zip(refs[0:-2:2], refs[1:-2:2]):
        stop = start + a_ref.shape[1]
        total = a_ref[...].astype(jnp.float32) + b_ref[...].astype(jnp.float32)
        out_ref[:, start:stop] = total * factor
        start = stop


def small_call(kernel, out, *args):
    return pl.pallas_call(
        kernel,
        out_shape=jax.ShapeDtypeStruct(out.shape, out.dtype),
        compiler_params=pltpu.CompilerParams(vmem_limit_bytes=8 * MIB),
    )(*args)


def local(slab, landmarks, codes, exponents, eigvec, ritz):
    n_lm, n_sl = lax.axis_size("lm"), lax.axis_size("sl")
    total_land = codes.shape[0] * n_lm * n_sl
    coeff = 1.0 / math.sqrt(slab.shape[1])
    cols = ritz.shape[0]
    rows = slab.shape[0]
    ways = n_sl.bit_length() - 2

    second = second_half(landmarks)
    first = prepare(landmarks, codes.T, exponents, eigvec.T)
    blocks = {0: [first, second]}
    for k in range(ways):
        blocks[1 << k] = [None, None]
    for turn in (0, 1):
        for k in range(ways):
            piece = (k + turn) % 2
            blocks[1 << k][piece] = chip_send(blocks[0][piece], k, n_sl)
    turned = jax.ShapeDtypeStruct(slab.shape[::-1], slab.dtype)
    other = small_call(transpose_kernel, turned, core_send(slab, n_sl))
    slab = small_call(transpose_kernel, turned, slab)
    (acc,) = stage([slab], first, second, None, coeff, cols)
    held = [blocks[1 << k][k % 2] for k in range(ways)]
    held, acc = lax.optimization_barrier((held, acc))
    for k in range(ways):
        blocks[1 << k][k % 2] = held[k]
    (other_acc,) = stage([other], first, second, None, coeff, cols)
    accs = [acc, other_acc]
    for t in range(1, 1 << ways):
        if t in blocks:
            continue
        low, high = (t & -t).bit_length() - 1, t.bit_length() - 1
        blocks[t] = [
            chip_send(blocks[t ^ (1 << high)][0], high, n_sl),
            chip_send(blocks[t ^ (1 << low)][1], low, n_sl),
        ]

    for t in range(1, (1 << ways) - 1):
        accs = stage([slab, other], *blocks[t], accs, coeff, cols)
    end = blocks[(1 << ways) - 1]
    width = rows // 2
    spans = [(0, width), (width, rows)]
    half = jax.ShapeDtypeStruct((cols, width), jnp.bfloat16)
    (early,) = stage([other], *end, accs[1:], coeff, cols, spans[:1])
    received = [core_send(early, n_sl)]
    late, mine = stage([other, slab], *end, accs[::-1], coeff, cols, spans[::-1])
    received.append(core_send(late, n_sl))
    total = small_call(add_kernel, half, mine, received[0])
    acc, total = lax.optimization_barrier((accs[0], total))
    (mine,) = stage([slab], *end, [acc], coeff, cols, spans[1:])
    totals = [total, small_call(add_kernel, half, mine, received[1])]
    turns = n_lm.bit_length() - 1
    for k in range(turns - 1):
        arrived = [lm_send(total, k, n_lm, n_sl) for total in totals]
        totals = [small_call(add_kernel, half, a, b) for a, b in zip(totals, arrived)]
    pairs = [(total, lm_send(total, turns - 1, n_lm, n_sl)) for total in totals]
    scale = functools.partial(scale_kernel, total_land=total_land)
    out = jax.ShapeDtypeStruct((cols, rows), jnp.float32)
    return small_call(scale, out, *(x for pair in pairs for x in pair), ritz[:, None]).T


def solution(mesh):
    return jax.shard_map(
        local,
        mesh=mesh,
        in_specs=(
            P("sl", None),
            P(("lm", "sl"), None),
            P(("lm", "sl"), None),
            P(("lm", "sl")),
            P(),
            P(),
        ),
        out_specs=P("sl", None),
        check_vma=False,
    )
```

```python
import functools
import math

import jax
import jax.numpy as jnp
from jax import lax
from jax.experimental import pallas as pl
from jax.experimental.pallas import tpu as pltpu
from jax.sharding import PartitionSpec as P

BLOCK = 128
SHIFT = 16
CHUNK = 512
MIB = 2**20


def core_send(value, n):
    return lax.ppermute(value, "sl", [(i, i ^ 1) for i in range(n)])


def chip_send(value, k, n):
    bits = [1 << b for b in range(1, n.bit_length() - 1)]
    return lax.ppermute(value, "sl", [(i, i ^ bits[(k + 1 - i % 2) % len(bits)]) for i in range(n)])


def lm_send(value, k, n_lm, n_sl):
    bits = [1 << b for b in range(n_lm.bit_length() - 1)]
    perm = [
        (i * n_sl + j, (i ^ bits[(k + j % 2) % len(bits)]) * n_sl + j)
        for i in range(n_lm)
        for j in range(n_sl)
    ]
    return lax.ppermute(value, ("lm", "sl"), perm)


def prepare_kernel(
    land_ref, codes_ref, exponents_ref, eig_ref, first_ref, codes, eig, exponents, sems
):
    rows, feat = land_ref.shape
    half = rows // 2 - SHIFT
    ritz = eig_ref.shape[0]
    pairs = [
        (codes_ref, codes),
        (eig_ref, eig),
        (exponents_ref, exponents),
        (land_ref.at[:half], first_ref.at[:half]),
    ]
    copies = [pltpu.make_async_copy(src, dst, sems.at[k]) for k, (src, dst) in enumerate(pairs)]
    for copy in copies:
        copy.start()
    for copy in copies[:3]:
        copy.wait()
    pieces = []
    for b in range(rows // BLOCK):
        scale = lax.shift_left(jnp.int32(1), exponents[b] + 15).astype(jnp.float32) * 2.0**-15
        pieces.append(codes[:, b * BLOCK : (b + 1) * BLOCK].astype(jnp.float32) * scale)
    basis = jnp.concatenate(pieces, axis=1).astype(jnp.bfloat16)
    vectors = jnp.dot(eig[...], basis, preferred_element_type=jnp.float32).astype(jnp.bfloat16)
    chunks = feat // rows
    depth = ritz // chunks
    for c in range(chunks):
        first_ref[half:, c * rows : (c + 1) * rows] = vectors[c * depth : (c + 1) * depth, :]
    for copy in copies[3:]:
        copy.wait()


def tail_kernel(land_ref, out_ref, sem):
    copy = pltpu.make_async_copy(land_ref.at[land_ref.shape[0] - out_ref.shape[0] :], out_ref, sem)
    copy.start()
    copy.wait()


def second_half(landmarks):
    rows, feat = landmarks.shape
    return pl.pallas_call(
        tail_kernel,
        out_shape=jax.ShapeDtypeStruct((rows // 2 + SHIFT, feat), jnp.bfloat16),
        in_specs=[pl.BlockSpec(memory_space=pltpu.HBM)],
        scratch_shapes=[pltpu.SemaphoreType.DMA],
        compiler_params=pltpu.CompilerParams(vmem_limit_bytes=8 * MIB),
    )(pltpu.with_memory_space_constraint(landmarks, pltpu.HBM))


def prepare(landmarks, codes_t, exponents, eig_t):
    rows, feat = landmarks.shape
    extra = eig_t.shape[0] * rows // feat
    return pl.pallas_call(
        prepare_kernel,
        out_shape=jax.ShapeDtypeStruct((rows // 2 - SHIFT + extra, feat), jnp.bfloat16),
        in_specs=[pl.BlockSpec(memory_space=pltpu.HBM)] * 4,
        scratch_shapes=[
            pltpu.VMEM(codes_t.shape, codes_t.dtype),
            pltpu.VMEM(eig_t.shape, eig_t.dtype),
            pltpu.SMEM(exponents.shape, exponents.dtype),
            pltpu.SemaphoreType.DMA((4,)),
        ],
        compiler_params=pltpu.CompilerParams(vmem_limit_bytes=8 * MIB),
    )(*(pltpu.with_memory_space_constraint(x, pltpu.HBM) for x in (landmarks, codes_t, exponents, eig_t)))


def transpose_kernel(in_ref, out_ref):
    for k in range(in_ref.shape[0] // CHUNK):
        rows = slice(k * CHUNK, (k + 1) * CHUNK)
        out_ref[:, rows] = in_ref[rows, :].T


def stage_kernel(count, coeff, ritz, has_acc, spans, *refs):
    slabs = refs[:count]
    first_ref, second_ref = refs[count : count + 2]
    accs = refs[count + 2 : 2 * count + 2] if has_acc else [None] * count
    outs = refs[-count:]
    tail, feat = second_ref.shape
    rows = (first_ref.shape[0] + tail) * feat // (feat + ritz)
    head = rows - tail
    land = jnp.concatenate([first_ref[:head, :], second_ref[...]], axis=0)
    vec = jnp.concatenate(
        [first_ref[head:, c * rows : (c + 1) * rows] for c in range(feat // rows)], axis=0
    )
    work = [
        (k, slice(c, min(c + CHUNK, stop)))
        for k, (start, stop) in enumerate(spans)
        for c in range(start, stop, CHUNK)
    ]

    def scores(k, cols):
        return jnp.dot(land, slabs[k][:, cols], preferred_element_type=jnp.float32)

    ahead = scores(*work[0])
    for n, (k, cols) in enumerate(work):
        now, ahead = ahead, scores(*work[n + 1]) if n + 1 < len(work) else None
        affinity = jnp.exp2(now * coeff).astype(jnp.bfloat16)
        term = jnp.dot(vec, affinity, preferred_element_type=jnp.float32)
        place = slice(cols.start - spans[k][0], cols.stop - spans[k][0])
        outs[k][:, place] = term if accs[k] is None else accs[k][:, cols] + term


def stage(slabs, first, second, accs, coeff, ritz, spans=None):
    feat, rows = slabs[0].shape
    land = (first.shape[0] + second.shape[0]) * feat // (feat + ritz)
    count = len(slabs)
    spans = spans or [(0, rows)] * count
    rows = spans[0][1] - spans[0][0]
    return pl.pallas_call(
        functools.partial(stage_kernel, count, coeff, ritz, accs is not None, spans),
        out_shape=[jax.ShapeDtypeStruct((ritz, rows), jnp.float32)] * count,
        compiler_params=pltpu.CompilerParams(vmem_limit_bytes=32 * MIB),
        cost_estimate=pl.CostEstimate(
            flops=2 * count * rows * land * (feat + 4 * ritz),
            bytes_accessed=2 * (count * rows + land) * feat,
            transcendentals=count * rows * land,
        ),
    )(*slabs, first, second, *(accs or []))


def add_kernel(a_ref, b_ref, out_ref):
    total = a_ref[...].astype(jnp.float32) + b_ref[...].astype(jnp.float32)
    out_ref[...] = total.astype(out_ref.dtype)


def scale_kernel(*refs, total_land):
    ritz_ref, out_ref = refs[-2:]
    factor = 1.0 / (ritz_ref[...] * math.sqrt(total_land))
    start = 0
    for a_ref, b_ref in zip(refs[0:-2:2], refs[1:-2:2]):
        stop = start + a_ref.shape[1]
        total = a_ref[...].astype(jnp.float32) + b_ref[...].astype(jnp.float32)
        out_ref[:, start:stop] = total * factor
        start = stop


def small_call(kernel, out, *args):
    return pl.pallas_call(
        kernel,
        out_shape=jax.ShapeDtypeStruct(out.shape, out.dtype),
        compiler_params=pltpu.CompilerParams(vmem_limit_bytes=8 * MIB),
    )(*args)


def local(slab, landmarks, codes, exponents, eigvec, ritz):
    n_lm, n_sl = lax.axis_size("lm"), lax.axis_size("sl")
    total_land = codes.shape[0] * n_lm * n_sl
    coeff = math.log2(math.e) / math.sqrt(slab.shape[1])
    cols = ritz.shape[0]
    rows = slab.shape[0]
    ways = n_sl.bit_length() - 2

    second = second_half(landmarks)
    first = prepare(landmarks, codes.T, exponents, eigvec.T)
    blocks = {0: [first, second]}
    for k in range(ways):
        blocks[1 << k] = [None, None]
    for turn in (0, 1):
        for k in range(ways):
            piece = (k + turn) % 2
            blocks[1 << k][piece] = chip_send(blocks[0][piece], k, n_sl)
    late_slab, _ = lax.optimization_barrier((slab, second))
    turned = jax.ShapeDtypeStruct(slab.shape[::-1], slab.dtype)
    other = small_call(transpose_kernel, turned, core_send(late_slab, n_sl))
    slab = small_call(transpose_kernel, turned, slab)
    (acc,) = stage([slab], first, second, None, coeff, cols)
    held = [blocks[1 << k][k % 2] for k in range(ways)]
    held, acc = lax.optimization_barrier((held, acc))
    for k in range(ways):
        blocks[1 << k][k % 2] = held[k]
    (other_acc,) = stage([other], first, second, None, coeff, cols)
    accs = [acc, other_acc]
    for t in range(1, 1 << ways):
        if t in blocks:
            continue
        low, high = (t & -t).bit_length() - 1, t.bit_length() - 1
        blocks[t] = [
            chip_send(blocks[t ^ (1 << high)][0], high, n_sl),
            chip_send(blocks[t ^ (1 << low)][1], low, n_sl),
        ]

    for t in range(1, (1 << ways) - 1):
        accs = stage([slab, other], *blocks[t], accs, coeff, cols)
    end = blocks[(1 << ways) - 1]
    width = rows // 2
    spans = [(0, width), (width, rows)]
    half = jax.ShapeDtypeStruct((cols, width), jnp.bfloat16)
    (early,) = stage([other], *end, accs[1:], coeff, cols, spans[:1])
    received = [core_send(early, n_sl)]
    late, mine = stage([other, slab], *end, accs[::-1], coeff, cols, spans[::-1])
    received.append(core_send(late, n_sl))
    total = small_call(add_kernel, half, mine, received[0])
    acc, total = lax.optimization_barrier((accs[0], total))
    (mine,) = stage([slab], *end, [acc], coeff, cols, spans[1:])
    totals = [total, small_call(add_kernel, half, mine, received[1])]
    turns = n_lm.bit_length() - 1
    for k in range(turns - 1):
        arrived = [lm_send(total, k, n_lm, n_sl) for total in totals]
        totals = [small_call(add_kernel, half, a, b) for a, b in zip(totals, arrived)]
    pairs = [(total, lm_send(total, turns - 1, n_lm, n_sl)) for total in totals]
    scale = functools.partial(scale_kernel, total_land=total_land)
    out = jax.ShapeDtypeStruct((cols, rows), jnp.float32)
    return small_call(scale, out, *(x for pair in pairs for x in pair), ritz[:, None]).T


def solution(mesh):
    return jax.shard_map(
        local,
        mesh=mesh,
        in_specs=(
            P("sl", None),
            P(("lm", "sl"), None),
            P(("lm", "sl"), None),
            P(("lm", "sl")),
            P(),
            P(),
        ),
        out_specs=P("sl", None),
        check_vma=False,
    )
```

```python
import functools
import math

import jax
import jax.numpy as jnp
from jax import lax
from jax.experimental import pallas as pl
from jax.experimental.pallas import tpu as pltpu
from jax.sharding import PartitionSpec as P

BLOCK = 128
SHIFT = 16
CHUNK = 512
MIB = 2**20


def core_send(value, n):
    return lax.ppermute(value, "sl", [(i, i ^ 1) for i in range(n)])


def chip_send(value, k, n):
    bits = [1 << b for b in range(1, n.bit_length() - 1)]
    return lax.ppermute(value, "sl", [(i, i ^ bits[(k + 1 - i % 2) % len(bits)]) for i in range(n)])


def lm_send(value, k, n_lm, n_sl):
    bits = [1 << b for b in range(n_lm.bit_length() - 1)]
    perm = [
        (i * n_sl + j, (i ^ bits[(k + j % 2) % len(bits)]) * n_sl + j)
        for i in range(n_lm)
        for j in range(n_sl)
    ]
    return lax.ppermute(value, ("lm", "sl"), perm)


def prepare_kernel(
    land_ref, codes_ref, exponents_ref, eig_ref, first_ref, codes, eig, exponents, sems
):
    rows, feat = land_ref.shape
    half = rows // 2 - SHIFT
    ritz = eig_ref.shape[0]
    pairs = [
        (codes_ref, codes),
        (eig_ref, eig),
        (exponents_ref, exponents),
        (land_ref.at[:half], first_ref.at[:half]),
    ]
    copies = [pltpu.make_async_copy(src, dst, sems.at[k]) for k, (src, dst) in enumerate(pairs)]
    for copy in copies:
        copy.start()
    for copy in copies[:3]:
        copy.wait()
    pieces = []
    for b in range(rows // BLOCK):
        scale = lax.shift_left(jnp.int32(1), exponents[b] + 15).astype(jnp.float32) * 2.0**-15
        pieces.append(codes[:, b * BLOCK : (b + 1) * BLOCK].astype(jnp.float32) * scale)
    basis = jnp.concatenate(pieces, axis=1).astype(jnp.bfloat16)
    vectors = jnp.dot(eig[...], basis, preferred_element_type=jnp.float32).astype(jnp.bfloat16)
    chunks = feat // rows
    depth = ritz // chunks
    for c in range(chunks):
        first_ref[half:, c * rows : (c + 1) * rows] = vectors[c * depth : (c + 1) * depth, :]
    for copy in copies[3:]:
        copy.wait()


def tail_kernel(land_ref, out_ref, sem):
    copy = pltpu.make_async_copy(land_ref.at[land_ref.shape[0] - out_ref.shape[0] :], out_ref, sem)
    copy.start()
    copy.wait()


def second_half(landmarks):
    rows, feat = landmarks.shape
    return pl.pallas_call(
        tail_kernel,
        out_shape=jax.ShapeDtypeStruct((rows // 2 + SHIFT, feat), jnp.bfloat16),
        in_specs=[pl.BlockSpec(memory_space=pltpu.HBM)],
        scratch_shapes=[pltpu.SemaphoreType.DMA],
        compiler_params=pltpu.CompilerParams(vmem_limit_bytes=8 * MIB),
    )(pltpu.with_memory_space_constraint(landmarks, pltpu.HBM))


def prepare(landmarks, codes_t, exponents, eig_t):
    rows, feat = landmarks.shape
    extra = eig_t.shape[0] * rows // feat
    return pl.pallas_call(
        prepare_kernel,
        out_shape=jax.ShapeDtypeStruct((rows // 2 - SHIFT + extra, feat), jnp.bfloat16),
        in_specs=[pl.BlockSpec(memory_space=pltpu.HBM)] * 4,
        scratch_shapes=[
            pltpu.VMEM(codes_t.shape, codes_t.dtype),
            pltpu.VMEM(eig_t.shape, eig_t.dtype),
            pltpu.SMEM(exponents.shape, exponents.dtype),
            pltpu.SemaphoreType.DMA((4,)),
        ],
        compiler_params=pltpu.CompilerParams(vmem_limit_bytes=8 * MIB),
    )(*(pltpu.with_memory_space_constraint(x, pltpu.HBM) for x in (landmarks, codes_t, exponents, eig_t)))


def transpose_kernel(in_ref, out_ref):
    for k in range(in_ref.shape[0] // CHUNK):
        rows = slice(k * CHUNK, (k + 1) * CHUNK)
        out_ref[:, rows] = in_ref[rows, :].T


def stage_kernel(count, coeff, ritz, has_acc, spans, *refs):
    slabs = refs[:count]
    first_ref, second_ref = refs[count : count + 2]
    accs = refs[count + 2 : 2 * count + 2] if has_acc else [None] * count
    outs = refs[-count:]
    tail, feat = second_ref.shape
    rows = (first_ref.shape[0] + tail) * feat // (feat + ritz)
    head = rows - tail
    land = jnp.concatenate([first_ref[:head, :], second_ref[...]], axis=0)
    vec = jnp.concatenate(
        [first_ref[head:, c * rows : (c + 1) * rows] for c in range(feat // rows)], axis=0
    )
    work = [
        (k, slice(c, min(c + CHUNK, stop)))
        for k, (start, stop) in enumerate(spans)
        for c in range(start, stop, CHUNK)
    ]

    def scores(k, cols):
        return jnp.dot(land, slabs[k][:, cols], preferred_element_type=jnp.float32)

    ahead = scores(*work[0])
    for n, (k, cols) in enumerate(work):
        now, ahead = ahead, scores(*work[n + 1]) if n + 1 < len(work) else None
        affinity = jnp.exp(now * coeff).astype(jnp.bfloat16)
        term = jnp.dot(vec, affinity, preferred_element_type=jnp.float32)
        place = slice(cols.start - spans[k][0], cols.stop - spans[k][0])
        outs[k][:, place] = term if accs[k] is None else accs[k][:, cols] + term


def stage(slabs, first, second, accs, coeff, ritz, spans=None):
    feat, rows = slabs[0].shape
    land = (first.shape[0] + second.shape[0]) * feat // (feat + ritz)
    count = len(slabs)
    spans = spans or [(0, rows)] * count
    rows = spans[0][1] - spans[0][0]
    return pl.pallas_call(
        functools.partial(stage_kernel, count, coeff, ritz, accs is not None, spans),
        out_shape=[jax.ShapeDtypeStruct((ritz, rows), jnp.float32)] * count,
        compiler_params=pltpu.CompilerParams(vmem_limit_bytes=32 * MIB),
        cost_estimate=pl.CostEstimate(
            flops=2 * count * rows * land * (feat + 4 * ritz),
            bytes_accessed=2 * (count * rows + land) * feat,
            transcendentals=count * rows * land,
        ),
    )(*slabs, first, second, *(accs or []))


def add_kernel(a_ref, b_ref, out_ref):
    total = a_ref[...].astype(jnp.float32) + b_ref[...].astype(jnp.float32)
    out_ref[...] = total.astype(out_ref.dtype)


def scale_kernel(*refs, total_land):
    ritz_ref, out_ref = refs[-2:]
    factor = 1.0 / (ritz_ref[...] * math.sqrt(total_land))
    start = 0
    for a_ref, b_ref in zip(refs[0:-2:2], refs[1:-2:2]):
        stop = start + a_ref.shape[1]
        total = a_ref[...].astype(jnp.float32) + b_ref[...].astype(jnp.float32)
        out_ref[:, start:stop] = total * factor
        start = stop


def small_call(kernel, out, *args):
    return pl.pallas_call(
        kernel,
        out_shape=jax.ShapeDtypeStruct(out.shape, out.dtype),
        compiler_params=pltpu.CompilerParams(vmem_limit_bytes=8 * MIB),
    )(*args)


def local(slab, landmarks, codes, exponents, eigvec, ritz):
    n_lm, n_sl = lax.axis_size("lm"), lax.axis_size("sl")
    total_land = codes.shape[0] * n_lm * n_sl
    coeff = 1.0 / math.sqrt(slab.shape[1])
    cols = ritz.shape[0]
    rows = slab.shape[0]
    ways = n_sl.bit_length() - 2

    second = second_half(landmarks)
    first = prepare(landmarks, codes.T, exponents, eigvec.T)
    blocks = {0: [first, second]}
    for k in range(ways):
        blocks[1 << k] = [None, None]
    for turn in (0, 1):
        for k in range(ways):
            piece = (k + turn) % 2
            blocks[1 << k][piece] = chip_send(blocks[0][piece], k, n_sl)
    late_slab, _ = lax.optimization_barrier((slab, second))
    turned = jax.ShapeDtypeStruct(slab.shape[::-1], slab.dtype)
    far = core_send(late_slab, n_sl)
    slab = small_call(transpose_kernel, turned, slab)
    (acc,) = stage([slab], first, second, None, coeff, cols)
    held = [blocks[1 << k][k % 2] for k in range(ways)]
    held, acc = lax.optimization_barrier((held, acc))
    for k in range(ways):
        blocks[1 << k][k % 2] = held[k]
    blocks[2][1], far = lax.optimization_barrier((blocks[2][1], far))
    other = small_call(transpose_kernel, turned, far)
    (other_acc,) = stage([other], first, second, None, coeff, cols)
    accs = [acc, other_acc]
    for t in range(1, 1 << ways):
        if t in blocks:
            continue
        low, high = (t & -t).bit_length() - 1, t.bit_length() - 1
        blocks[t] = [
            chip_send(blocks[t ^ (1 << high)][0], high, n_sl),
            chip_send(blocks[t ^ (1 << low)][1], low, n_sl),
        ]

    for t in range(1, (1 << ways) - 1):
        accs = stage([slab, other], *blocks[t], accs, coeff, cols)
    end = blocks[(1 << ways) - 1]
    width = rows // 2
    spans = [(0, width), (width, rows)]
    half = jax.ShapeDtypeStruct((cols, width), jnp.bfloat16)
    (early,) = stage([other], *end, accs[1:], coeff, cols, spans[:1])
    received = [core_send(early, n_sl)]
    late, mine = stage([other, slab], *end, accs[::-1], coeff, cols, spans[::-1])
    received.append(core_send(late, n_sl))
    total = small_call(add_kernel, half, mine, received[0])
    acc, total = lax.optimization_barrier((accs[0], total))
    (mine,) = stage([slab], *end, [acc], coeff, cols, spans[1:])
    totals = [total, small_call(add_kernel, half, mine, received[1])]
    turns = n_lm.bit_length() - 1
    for k in range(turns - 1):
        arrived = [lm_send(total, k, n_lm, n_sl) for total in totals]
        totals = [small_call(add_kernel, half, a, b) for a, b in zip(totals, arrived)]
    pairs = [(total, lm_send(total, turns - 1, n_lm, n_sl)) for total in totals]
    scale = functools.partial(scale_kernel, total_land=total_land)
    out = jax.ShapeDtypeStruct((cols, rows), jnp.float32)
    return small_call(scale, out, *(x for pair in pairs for x in pair), ritz[:, None]).T


def solution(mesh):
    return jax.shard_map(
        local,
        mesh=mesh,
        in_specs=(
            P("sl", None),
            P(("lm", "sl"), None),
            P(("lm", "sl"), None),
            P(("lm", "sl")),
            P(),
            P(),
        ),
        out_specs=P("sl", None),
        check_vma=False,
    )
```

```python
import functools
import math

import jax
import jax.numpy as jnp
from jax import lax
from jax.experimental import pallas as pl
from jax.experimental.pallas import tpu as pltpu
from jax.sharding import PartitionSpec as P

BLOCK = 128
SHIFT = 16
CHUNK = 512
MIB = 2**20


def core_send(value, n):
    return lax.ppermute(value, "sl", [(i, i ^ 1) for i in range(n)])


def chip_send(value, k, n):
    bits = [1 << b for b in range(1, n.bit_length() - 1)]
    return lax.ppermute(value, "sl", [(i, i ^ bits[(k + 1 - i % 2) % len(bits)]) for i in range(n)])


def lm_send(value, k, n_lm, n_sl):
    bits = [1 << b for b in range(n_lm.bit_length() - 1)]
    perm = [
        (i * n_sl + j, (i ^ bits[(k + j % 2) % len(bits)]) * n_sl + j)
        for i in range(n_lm)
        for j in range(n_sl)
    ]
    return lax.ppermute(value, ("lm", "sl"), perm)


def prepare_kernel(
    land_ref, codes_ref, exponents_ref, eig_ref, first_ref, codes, eig, exponents, sems
):
    rows, feat = land_ref.shape
    half = rows // 2 - SHIFT
    ritz = eig_ref.shape[0]
    pairs = [
        (codes_ref, codes),
        (eig_ref, eig),
        (exponents_ref, exponents),
        (land_ref.at[:half], first_ref.at[:half]),
    ]
    copies = [pltpu.make_async_copy(src, dst, sems.at[k]) for k, (src, dst) in enumerate(pairs)]
    for copy in copies:
        copy.start()
    for copy in copies[:3]:
        copy.wait()
    pieces = []
    for b in range(rows // BLOCK):
        scale = lax.shift_left(jnp.int32(1), exponents[b] + 15).astype(jnp.float32) * 2.0**-15
        pieces.append(codes[:, b * BLOCK : (b + 1) * BLOCK].astype(jnp.float32) * scale)
    basis = jnp.concatenate(pieces, axis=1).astype(jnp.bfloat16)
    vectors = jnp.dot(eig[...], basis, preferred_element_type=jnp.float32).astype(jnp.bfloat16)
    chunks = feat // rows
    depth = ritz // chunks
    for c in range(chunks):
        first_ref[half:, c * rows : (c + 1) * rows] = vectors[c * depth : (c + 1) * depth, :]
    for copy in copies[3:]:
        copy.wait()


def tail_kernel(land_ref, out_ref, sem):
    copy = pltpu.make_async_copy(land_ref.at[land_ref.shape[0] - out_ref.shape[0] :], out_ref, sem)
    copy.start()
    copy.wait()


def second_half(landmarks):
    rows, feat = landmarks.shape
    return pl.pallas_call(
        tail_kernel,
        out_shape=jax.ShapeDtypeStruct((rows // 2 + SHIFT, feat), jnp.bfloat16),
        in_specs=[pl.BlockSpec(memory_space=pltpu.HBM)],
        scratch_shapes=[pltpu.SemaphoreType.DMA],
        compiler_params=pltpu.CompilerParams(vmem_limit_bytes=8 * MIB),
    )(pltpu.with_memory_space_constraint(landmarks, pltpu.HBM))


def prepare(landmarks, codes_t, exponents, eig_t):
    rows, feat = landmarks.shape
    extra = eig_t.shape[0] * rows // feat
    return pl.pallas_call(
        prepare_kernel,
        out_shape=jax.ShapeDtypeStruct((rows // 2 - SHIFT + extra, feat), jnp.bfloat16),
        in_specs=[pl.BlockSpec(memory_space=pltpu.HBM)] * 4,
        scratch_shapes=[
            pltpu.VMEM(codes_t.shape, codes_t.dtype),
            pltpu.VMEM(eig_t.shape, eig_t.dtype),
            pltpu.SMEM(exponents.shape, exponents.dtype),
            pltpu.SemaphoreType.DMA((4,)),
        ],
        compiler_params=pltpu.CompilerParams(vmem_limit_bytes=8 * MIB),
    )(*(pltpu.with_memory_space_constraint(x, pltpu.HBM) for x in (landmarks, codes_t, exponents, eig_t)))


def transpose_kernel(in_ref, out_ref):
    for k in range(in_ref.shape[0] // CHUNK):
        rows = slice(k * CHUNK, (k + 1) * CHUNK)
        out_ref[:, rows] = in_ref[rows, :].T


def stage_kernel(count, coeff, ritz, has_acc, spans, *refs):
    slabs = refs[:count]
    first_ref, second_ref = refs[count : count + 2]
    accs = refs[count + 2 : 2 * count + 2] if has_acc else [None] * count
    outs = refs[-count:]
    tail, feat = second_ref.shape
    rows = (first_ref.shape[0] + tail) * feat // (feat + ritz)
    head = rows - tail
    land = jnp.concatenate([first_ref[:head, :], second_ref[...]], axis=0)
    vec = jnp.concatenate(
        [first_ref[head:, c * rows : (c + 1) * rows] for c in range(feat // rows)], axis=0
    )
    work = [
        (k, slice(c, min(c + CHUNK, stop)))
        for k, (start, stop) in enumerate(spans)
        for c in range(start, stop, CHUNK)
    ]

    def scores(k, cols):
        return jnp.dot(land, slabs[k][:, cols], preferred_element_type=jnp.float32)

    ahead = scores(*work[0])
    for n, (k, cols) in enumerate(work):
        now, ahead = ahead, scores(*work[n + 1]) if n + 1 < len(work) else None
        affinity = jnp.exp(now * coeff).astype(jnp.bfloat16)
        term = jnp.dot(vec, affinity, preferred_element_type=jnp.float32)
        place = slice(cols.start - spans[k][0], cols.stop - spans[k][0])
        outs[k][:, place] = term if accs[k] is None else accs[k][:, cols] + term


def stage(slabs, first, second, accs, coeff, ritz, spans=None):
    feat, rows = slabs[0].shape
    land = (first.shape[0] + second.shape[0]) * feat // (feat + ritz)
    count = len(slabs)
    spans = spans or [(0, rows)] * count
    rows = spans[0][1] - spans[0][0]
    return pl.pallas_call(
        functools.partial(stage_kernel, count, coeff, ritz, accs is not None, spans),
        out_shape=[jax.ShapeDtypeStruct((ritz, rows), jnp.float32)] * count,
        compiler_params=pltpu.CompilerParams(vmem_limit_bytes=32 * MIB),
        cost_estimate=pl.CostEstimate(
            flops=2 * count * rows * land * (feat + 4 * ritz),
            bytes_accessed=2 * (count * rows + land) * feat,
            transcendentals=count * rows * land,
        ),
    )(*slabs, first, second, *(accs or []))


def add_kernel(a_ref, b_ref, out_ref):
    total = a_ref[...].astype(jnp.float32) + b_ref[...].astype(jnp.float32)
    out_ref[...] = total.astype(out_ref.dtype)


def scale_kernel(*refs, total_land):
    ritz_ref, out_ref = refs[-2:]
    factor = 1.0 / (ritz_ref[...] * math.sqrt(total_land))
    start = 0
    for a_ref, b_ref in zip(refs[0:-2:2], refs[1:-2:2]):
        stop = start + a_ref.shape[1]
        total = a_ref[...].astype(jnp.float32) + b_ref[...].astype(jnp.float32)
        out_ref[:, start:stop] = total * factor
        start = stop


def small_call(kernel, out, *args):
    return pl.pallas_call(
        kernel,
        out_shape=jax.ShapeDtypeStruct(out.shape, out.dtype),
        compiler_params=pltpu.CompilerParams(vmem_limit_bytes=8 * MIB),
    )(*args)


def local(slab, landmarks, codes, exponents, eigvec, ritz):
    n_lm, n_sl = lax.axis_size("lm"), lax.axis_size("sl")
    total_land = codes.shape[0] * n_lm * n_sl
    coeff = 1.0 / math.sqrt(slab.shape[1])
    cols = ritz.shape[0]
    rows = slab.shape[0]
    ways = n_sl.bit_length() - 2

    second = second_half(landmarks)
    first = prepare(landmarks, codes.T, exponents, eigvec.T)
    blocks = {0: [first, second]}
    for k in range(ways):
        blocks[1 << k] = [None, None]
    for turn in (0, 1):
        for k in range(ways):
            piece = (k + turn) % 2
            blocks[1 << k][piece] = chip_send(blocks[0][piece], k, n_sl)
    late_slab, _ = lax.optimization_barrier((slab, second))
    turned = jax.ShapeDtypeStruct(slab.shape[::-1], slab.dtype)
    other = small_call(transpose_kernel, turned, core_send(late_slab, n_sl))
    slab = small_call(transpose_kernel, turned, slab)
    (acc,) = stage([slab], first, second, None, coeff, cols)
    for k in reversed(range(ways)):
        blocks[1 << k][k % 2], acc = lax.optimization_barrier((blocks[1 << k][k % 2], acc))
    (other_acc,) = stage([other], first, second, None, coeff, cols)
    accs = [acc, other_acc]
    for t in range(1, 1 << ways):
        if t in blocks:
            continue
        low, high = (t & -t).bit_length() - 1, t.bit_length() - 1
        blocks[t] = [
            chip_send(blocks[t ^ (1 << high)][0], high, n_sl),
            chip_send(blocks[t ^ (1 << low)][1], low, n_sl),
        ]

    for t in range(1, (1 << ways) - 1):
        accs = stage([slab, other], *blocks[t], accs, coeff, cols)
    end = blocks[(1 << ways) - 1]
    width = rows // 2
    spans = [(0, width), (width, rows)]
    half = jax.ShapeDtypeStruct((cols, width), jnp.bfloat16)
    (early,) = stage([other], *end, accs[1:], coeff, cols, spans[:1])
    received = [core_send(early, n_sl)]
    late, mine = stage([other, slab], *end, accs[::-1], coeff, cols, spans[::-1])
    received.append(core_send(late, n_sl))
    total = small_call(add_kernel, half, mine, received[0])
    acc, total = lax.optimization_barrier((accs[0], total))
    (mine,) = stage([slab], *end, [acc], coeff, cols, spans[1:])
    totals = [total, small_call(add_kernel, half, mine, received[1])]
    turns = n_lm.bit_length() - 1
    for k in range(turns - 1):
        arrived = [lm_send(total, k, n_lm, n_sl) for total in totals]
        totals = [small_call(add_kernel, half, a, b) for a, b in zip(totals, arrived)]
    pairs = [(total, lm_send(total, turns - 1, n_lm, n_sl)) for total in totals]
    scale = functools.partial(scale_kernel, total_land=total_land)
    out = jax.ShapeDtypeStruct((cols, rows), jnp.float32)
    return small_call(scale, out, *(x for pair in pairs for x in pair), ritz[:, None]).T


def solution(mesh):
    return jax.shard_map(
        local,
        mesh=mesh,
        in_specs=(
            P("sl", None),
            P(("lm", "sl"), None),
            P(("lm", "sl"), None),
            P(("lm", "sl")),
            P(),
            P(),
        ),
        out_specs=P("sl", None),
        check_vma=False,
    )
```
